32 devices in a mesh: items: 16 (over z, x, core), frames: 2 (over y).
Axes of the slice: x: 2, y: 2, z: 4, core: 2. Of those that a mesh axis runs over, the one named last changes fastest.
Arguments:
- tokens: bfloat16 [64, 1024, 768], P('items', 'frames'), may hold values from -6 to 6
- skip: int32 [64], P('items'), may hold values from 0 to 1
- latent_init: bfloat16 [128, 768], replicated, may hold values from -6 to 6
- tok_gain: float32 [768], replicated, may hold values from 0.25 to 1.75
- query_gain: float32 [768], replicated, may hold values from 0.25 to 1.75
- mlp_gain: float32 [768], replicated, may hold values from 0.25 to 1.75
- self_gain: float32 [768], replicated, may hold values from 0.25 to 1.75
- w_query: bfloat16 [768, 768], replicated, may hold values from -0.4375 to 0.4375
- w_keyval: bfloat16 [768, 1536], replicated, may hold values from -0.21875 to 0.21875
- w_out: bfloat16 [768, 768], replicated, may hold values from -1.75 to 1.75
- w_up: bfloat16 [768, 3072], replicated, may hold values from -0.21875 to 0.21875
- w_down: bfloat16 [3072, 768], replicated, may hold values from -0.15625 to 0.15625
- w_self_qkv: bfloat16 [768, 2304], replicated, may hold values from -0.3125 to 0.3125
- w_self_out: bfloat16 [768, 768], replicated, may hold values from -0.3125 to 0.3125
- grad_out: bfloat16 [64, 128, 768], P('items'), may hold values from -6 to 6
Outputs:
- latents: bfloat16 [64, 128, 768], P('items', 'frames')
- token_grad: bfloat16 [64, 1024, 768], P('items', 'frames')
- latent_grad: float32 [128, 768], P(None, 'frames')
- tok_gain_grad: float32 [768], P('frames')
- query_gain_grad: float32 [768], P('frames')
- mlp_gain_grad: float32 [768], P('frames')
- self_gain_grad: float32 [768], P('frames')
- w_query_grad: float32 [768, 768], P(None, 'frames')
- w_keyval_grad: float32 [768, 1536], P(None, 'frames')
- w_out_grad: float32 [768, 768], P(None, 'frames')
- w_up_grad: float32 [768, 3072], P(None, 'frames')
- w_down_grad: float32 [3072, 768], P(None, 'frames')
- w_self_qkv_grad: float32 [768, 2304], P(None, 'frames')
- w_self_out_grad: float32 [768, 768], P(None, 'frames')
The draws below stay inside these ranges and needn't reach their ends.
Inputs may be any that keep to these rules, and one draw needn't show every extreme that they name: `skip`: 1 skips the item's cross-attention, 0 keeps it.
All inputs are finite; a program needn't handle non-finite values.
Results may differ from the reference program's by a relative error of at most 0.023.
The reference program's roundings to bfloat16 on the way count: a program that leaves them out, or rounds other values in their place, can miss the bound.
Values sent between devices are 32-bit elements; how exact they have to be, the bound alone decides.
A program may use at most 192 MiB of HBM per device.

```python
import jax
import jax.numpy as jnp
from jax import lax

D = 768
HEADS = 12
FF = 3072
LATENTS = 128
HEAD_DIM = 64
SEQ = 1024
ITEMS = 64


def set_ends(drawn, stream_key, least, high):
    index_at = [jax.random.randint(jax.random.fold_in(stream_key, axis), (), 0, length) for axis, length in enumerate(drawn.shape)]
    widest = drawn.shape.index(max(drawn.shape))
    beside = index_at[:widest] + [(index_at[widest] + 1) % drawn.shape[widest]] + index_at[widest + 1:]
    return drawn.at[tuple(index_at)].set(least).at[tuple(beside)].set(high)


def block_scale(own_key, extent, shards, low, top_value):
    def one(position, shards_of):
        steps = jax.random.uniform(jax.random.fold_in(jax.random.fold_in(own_key, 6), position), (shards_of,), jnp.float32, low / len(shards), top_value / len(shards))
        return jnp.repeat(jnp.exp(steps), extent[position] // shards_of).reshape((-1,) + (1,) * (len(extent) - position - 1))

    level = one(*shards[0])
    for cut in shards[1:]:
        level = level * one(*cut)
    return level


def scatter_about(own_key, dims, spread, most, shards=(), kind=jnp.bfloat16):
    drawn = jax.random.normal(own_key, dims, jnp.float32) * spread
    if len(shards) > 0:
        drawn = block_scale(own_key, dims, shards, -0.22, 0.18) * drawn
    return jnp.clip(drawn, min=-most, max=most).astype(kind)


def setup_inputs(seed: int = 0) -> dict:
    seeds = jax.random.split(jax.random.key(seed), 16)
    return {
        "tokens": scatter_about(seeds[0], (ITEMS, SEQ, D), 1.0, 6.0, ((0, 16), (1, 2))),
        "skip": set_ends(jax.random.randint(seeds[1], (ITEMS,), 0, 2), jax.random.fold_in(seeds[1], 1), 0, 1).astype(jnp.int32),
        "latent_init": scatter_about(seeds[2], (LATENTS, D), 1.0, 6.0),
        "tok_gain": jnp.clip(1.0 + 0.15 * jax.random.normal(seeds[3], (D,), jnp.float32), 0.25, 1.75),
        "query_gain": jnp.clip(1.0 + 0.15 * jax.random.normal(seeds[4], (D,), jnp.float32), 0.25, 1.75),
        "mlp_gain": jnp.clip(1.0 + 0.15 * jax.random.normal(seeds[5], (D,), jnp.float32), 0.25, 1.75),
        "self_gain": jnp.clip(1.0 + 0.15 * jax.random.normal(seeds[6], (D,), jnp.float32), 0.25, 1.75),
        "w_query": scatter_about(seeds[7], (D, D), (D // 4) ** -0.5, 0.4375),
        "w_keyval": scatter_about(seeds[8], (D, 2 * D), D ** -0.5, 0.21875),
        "w_out": scatter_about(seeds[9], (D, D), (D // 64) ** -0.5, 1.75),
        "w_up": scatter_about(seeds[10], (D, FF), D ** -0.5, 0.21875),
        "w_down": scatter_about(seeds[11], (FF, D), (FF // 2) ** -0.5, 0.15625),
        "w_self_qkv": scatter_about(seeds[12], (D, 3 * D), (D // 2) ** -0.5, 0.3125),
        "w_self_out": scatter_about(seeds[13], (D, D), (D // 2) ** -0.5, 0.3125),
        "grad_out": scatter_about(seeds[14], (ITEMS, LATENTS, D), 1.0, 6.0, ((0, 16),)),
    }


@jax.custom_vjp
def low(v):
    return lax.optimization_barrier(v.astype(jnp.bfloat16)).astype(jnp.float32)

@jax.custom_vjp
def low_back(v):
    return v

def low_keep(v):
    return (low(v), None)

def low_pass(kept, grad):
    return (grad,)

def back_keep(v):
    return (v, None)

def back_low(kept, grad):
    return (low(grad),)
low.defvjp(low_keep, low_pass)
low_back.defvjp(back_keep, back_low)
EPSILON = 1e-05

def layer_norm(values, gain):
    center = lax.optimization_barrier(jnp.mean(values, axis=-1, keepdims=True))
    centered = values - center
    variance = lax.optimization_barrier(jnp.mean(centered * centered, axis=-1, keepdims=True))
    return centered * lax.rsqrt(variance + EPSILON) * gain

def product(left, right):
    return jnp.dot(left, right, precision=lax.Precision.HIGHEST)

def softmax_rows(scores):
    shifted = jnp.exp(scores - lax.optimization_barrier(jnp.max(scores, axis=-1, keepdims=True)))
    return shifted / lax.optimization_barrier(jnp.sum(shifted, axis=-1, keepdims=True))

def attend(queries, keys_in, values_in):
    query_count = queries.shape[0]
    key_count = keys_in.shape[0]
    query_heads = queries.reshape(query_count, HEADS, HEAD_DIM)
    key_heads = keys_in.reshape(key_count, HEADS, HEAD_DIM)
    value_heads = values_in.reshape(key_count, HEADS, HEAD_DIM)
    scores = low_back(jnp.einsum('qhe,khe->hqk', query_heads, key_heads, precision=lax.Precision.HIGHEST) * HEAD_DIM ** (-0.5))
    weights = low(softmax_rows(scores))
    mixed = jnp.einsum('hqk,khe->qhe', weights, value_heads, precision=lax.Precision.HIGHEST)
    return mixed.reshape(query_count, D)

def forward(token_rows, keep_flag, params):
    latent, tok_gain, query_gain, mlp_gain, self_gain, w_query, w_keyval, w_out, w_up, w_down, w_self_qkv, w_self_out = params
    tok_in = low(layer_norm(token_rows, tok_gain))
    keyval = low(low_back(product(tok_in, w_keyval)))
    query_in = low(layer_norm(latent, query_gain))
    queries = low(product(query_in, w_query))
    heard = low(low_back(attend(queries, keyval[:, :D], keyval[:, D:])))
    after_cross = latent + keep_flag * low_back(product(heard, w_out))
    mlp_in = low(layer_norm(after_cross, mlp_gain))
    hidden = low_back(product(mlp_in, w_up))
    after_mlp = after_cross + low_back(product(low(jax.nn.gelu(hidden)), w_down))
    self_in = low(layer_norm(after_mlp, self_gain))
    triple = low(low_back(product(self_in, w_self_qkv)))
    mixed = low(low_back(attend(triple[:, :D], triple[:, D:2 * D], triple[:, 2 * D:])))
    return after_mlp + low_back(product(mixed, w_self_out))

def reference(tokens, skip, latent_init, tok_gain, query_gain, mlp_gain, self_gain, w_query, w_keyval, w_out, w_up, w_down, w_self_qkv, w_self_out, grad_out):
    params = (latent_init.astype(jnp.float32), tok_gain.astype(jnp.float32), query_gain.astype(jnp.float32), mlp_gain.astype(jnp.float32), self_gain.astype(jnp.float32), w_query.astype(jnp.float32), w_keyval.astype(jnp.float32), w_out.astype(jnp.float32), w_up.astype(jnp.float32), w_down.astype(jnp.float32), w_self_qkv.astype(jnp.float32), w_self_out.astype(jnp.float32))
    zeros = jax.tree.map(jnp.zeros_like, params)

    def one_item(totals, inputs):
        token_rows, flag, cotangent = inputs
        keep_flag = 1.0 - flag.astype(jnp.float32)

        def run(rows, weights):
            return forward(rows, keep_flag, weights)
        result, pull = jax.vjp(run, token_rows.astype(jnp.float32), params)
        rows_grad, weight_grads = pull(cotangent.astype(jnp.float32))
        totals = jax.tree.map(jnp.add, totals, weight_grads)
        return (totals, (result.astype(jnp.bfloat16), rows_grad.astype(jnp.bfloat16)))
    totals, outputs = lax.scan(one_item, zeros, (tokens, skip, grad_out))
    return (outputs[0], outputs[1], totals[0], totals[1], totals[2], totals[3], totals[4], totals[5], totals[6], totals[7], totals[8], totals[9], totals[10], totals[11])
```

```python
import functools

import jax
import jax.numpy as jnp
from jax import lax
from jax.experimental import pallas as pl
from jax.experimental.pallas import tpu as pltpu
from jax.sharding import PartitionSpec as P

HEADS = 12


EPSILON = 1e-05


def norm_parts(values):
    center = jnp.mean(values, axis=-1, keepdims=True)
    centered = values - center
    inverse = lax.rsqrt(jnp.mean(centered * centered, axis=-1, keepdims=True) + EPSILON)
    return (centered * inverse, inverse)


def norm_back(incoming, normed, inverse, gain):
    scaled = incoming * gain
    gain_grad = jnp.sum((incoming * normed).reshape(-1, normed.shape[-1]), axis=0)
    average = jnp.mean(scaled, axis=-1, keepdims=True)
    along = jnp.mean(scaled * normed, axis=-1, keepdims=True)
    return (inverse * (scaled - average - normed * along), gain_grad)


def forward_mul(left, weight):
    return jnp.einsum("irk,kn->irn", left, weight, preferred_element_type=jnp.float32)


def input_mul(grad_rows, weight):
    return jnp.einsum("irn,kn->irk", grad_rows, weight, preferred_element_type=jnp.float32)


def weight_mul(left, grad_rows):
    return jnp.einsum("irk,irn->kn", left, grad_rows, preferred_element_type=jnp.float32)


def split_heads(values):
    return values.reshape(values.shape[0], values.shape[1], HEADS, values.shape[2] // HEADS)


def join_heads(values):
    return values.reshape(values.shape[0], values.shape[1], values.shape[2] * values.shape[3])


def own_columns(gradient, column_index, parts):
    span = gradient.shape[-1] // parts
    return lax.dynamic_slice_in_dim(gradient, column_index * span, span, gradient.ndim - 1)


def pack(array, pieces, width):
    rows, columns = array.shape[-2] // pieces, array.shape[-1] // width
    split = array.reshape(array.shape[:-2] + (pieces, rows, columns, width))
    split = jnp.swapaxes(split, -3, -2)
    return split.reshape(array.shape[:-2] + (pieces, columns * rows, width))


def unpack(packed, rows, columns):
    pieces, _, width = packed.shape
    split = packed.reshape(pieces, columns // width, rows // pieces, width)
    return jnp.swapaxes(split, 1, 2).reshape(rows, columns)


def cut(packed, shapes):
    width, start, out = packed.shape[-1], 0, []
    for rows, columns in shapes:
        count = rows * columns // width // packed.shape[0]
        out.append(unpack(packed[:, start : start + count], rows, columns))
        start += count
    return out


MESH = pl.DeviceIdType.MESH


def add_into(target, parts, rows):
    step = next(size for size in (104, 80, 64, 48, 40, 24, 16, 8) if rows % size == 0)

    def body(index, carry):
        window = pl.ds(pl.multiple_of(index * step, 8), step)
        total = parts[0][window]
        for part in parts[1:]:
            total = total + part[window]
        target[window] = total
        return carry

    lax.fori_loop(0, rows // step, body, 0)


def reduce_kernel(
    chips, frames, spans,
    mid_ref, kv_ref, mid_out, kv_out,
    mine, sib, rx, kmine, ksib, ky, krx,
    ld_sem, sib_send, sib_recv, rs_send, rs_recv, ag_send, ag_recv, share_send, share_recv, own_sem,
    kld_sem, ksib_send, ksib_recv, y_send, y_recv, krs_send, krs_recv, kag_send, kag_recv, kshare_send, kshare_recv,
):
    items = lax.axis_index("items")
    frame = lax.axis_index("frames")
    core = lax.rem(items, 2)
    chip = items // 2
    column = lax.rem(chip, 2)
    line = chip // 2
    place = line + column * (chips - 1 - 2 * line)
    way = 1 - 2 * core

    def device_at(position):
        position = lax.rem(position + 2 * chips, chips)
        far = position // (chips // 2)
        return (2 * (position + far * (chips - 1 - 2 * position)) + far) * 2 + core

    right, left = device_at(place + way), device_at(place - way)
    sibling = items + way
    kv_rows = kv_ref.shape[3]

    def chunk(offset):
        return lax.rem(place + way * offset + 2 * chips, chips)

    def sib_chunk(offset):
        return lax.rem(place - way * offset + 2 * chips, chips)

    barrier = pltpu.get_barrier_semaphore()
    for peer in (left, right, sibling):
        pl.semaphore_signal(barrier, inc=1, device_id=(peer, frame), device_id_type=MESH)
    for hop in range(1, frames):
        pl.semaphore_signal(barrier, inc=1, device_id=(items, lax.rem(frame + hop, frames)), device_id_type=MESH)
    pl.semaphore_wait(barrier, 3 + frames - 1)

    def remote(src, dst, send, recv, peer):
        return pltpu.make_async_remote_copy(
            src_ref=src, dst_ref=dst, send_sem=send, recv_sem=recv, device_id=peer, device_id_type=MESH
        )

    def load(k):
        return pltpu.make_async_copy(mid_ref.at[core, k], mine.at[k], ld_sem.at[k])

    def pair(k):
        return remote(mid_ref.at[1 - core, k], sib.at[k], sib_send.at[k], sib_recv.at[k], (sibling, frame))

    def ring(j, k):
        rows = pl.ds(*spans[j])
        return remote(mine.at[k, rows], rx.at[k, rows], rs_send.at[j, k], rs_recv.at[j, k], (right, frame))

    def gather(j, k, source):
        rows = pl.ds(*spans[j])
        return remote(source.at[k, rows], mid_out.at[core, k, rows], ag_send.at[j, k], ag_recv.at[j, k], (right, frame))

    def share(j, k, source):
        rows = pl.ds(*spans[j])
        return remote(source.at[k, rows], mid_out.at[core, k, rows], share_send.at[j, k], share_recv.at[j, k], (sibling, frame))

    def share_from(j, k):
        rows = pl.ds(*spans[j])
        return remote(mine.at[k, rows], mid_out.at[1 - core, k, rows], share_send.at[j, k], share_recv.at[j, k], (sibling, frame))

    def kload(k):
        return pltpu.make_async_copy(kv_ref.at[:, core, k], kmine.at[:, k], kld_sem.at[k])

    def kpair(k):
        return remote(kv_ref.at[:, 1 - core, k], ksib.at[:, k], ksib_send.at[k], ksib_recv.at[k], (sibling, frame))

    def across(hop):
        other = lax.rem(frame + hop, frames)
        return remote(kmine.at[other], ky.at[hop - 1], y_send.at[hop - 1], y_recv.at[hop - 1], (items, other))

    def kring(k):
        return remote(kmine.at[frame, k], krx.at[k], krs_send.at[k], krs_recv.at[k], (right, frame))

    def kgather(k, source):
        return remote(source, kv_out.at[core, k], kag_send.at[k], kag_recv.at[k], (right, frame))

    def kshare(k, source):
        return remote(source, kv_out.at[core, k], kshare_send.at[k], kshare_recv.at[k], (sibling, frame))

    def kshare_from(k):
        return remote(kmine.at[frame, k], kv_out.at[1 - core, k], kshare_send.at[k], kshare_recv.at[k], (sibling, frame))

    def start_stage(index, carry):
        load(chunk(-index)).start()
        pair(sib_chunk(-index)).start()
        return carry

    lax.fori_loop(0, chips, start_stage, 0)

    def start_kstage(index, carry):
        kload(index).start()
        kpair(index).start()
        return carry

    lax.fori_loop(0, chips, start_kstage, 0)

    def ring_step(step, first):
        k = chunk(-step)
        load(k).wait()
        pair(k).wait_recv()
        for j, (start, count) in enumerate(spans):
            rows = pl.ds(start, count)
            parts = [mine.at[k, rows], sib.at[k, rows]]
            if not first:
                ring(j, k).wait_recv()
                parts.append(rx.at[k, rows])
            add_into(mine.at[k, rows], parts, count)
            ring(j, k).start()

    ring_step(0, True)

    def kstage(k, carry):
        kload(k).wait()
        kpair(k).wait_recv()
        for f in range(frames):
            add_into(kmine.at[f, k], [kmine.at[f, k], ksib.at[f, k]], kv_rows)
        return carry

    lax.fori_loop(0, chips, kstage, 0)
    for hop in range(1, frames):
        across(hop).start()

    def ring_loop(step, carry):
        ring_step(step, False)
        return carry

    lax.fori_loop(1, chips - 1, ring_loop, 0)

    k = chunk(1)
    load(k).wait()
    pair(k).wait_recv()
    for j, (start, count) in enumerate(spans):
        rows = pl.ds(start, count)
        ring(j, k).wait_recv()
        add_into(mine.at[k, rows], [mine.at[k, rows], sib.at[k, rows], rx.at[k, rows]], count)
        gather(j, k, mine).start()
        share(j, k, mine).start()
        pltpu.make_async_copy(mine.at[k, rows], mid_out.at[core, k, rows], own_sem.at[j]).start()

    for hop in range(1, frames):
        across(hop).wait_recv()

    def kstep(step):
        k = chunk(-step)
        if step < chips:
            parts = [kmine.at[frame, k]] + [ky.at[hop, k] for hop in range(frames - 1)]
            if step > 0:
                kring(k).wait_recv()
                parts.append(krx.at[k])
            add_into(kmine.at[frame, k], parts, kv_rows)
            if step < chips - 1:
                kring(k).start()
            else:
                kgather(k, kmine.at[frame, k]).start()
                kshare(k, kmine.at[frame, k]).start()
                pltpu.make_async_copy(kmine.at[frame, k], kv_out.at[core, k], own_sem.at[len(spans)]).start()
        else:
            kgather(k, kmine.at[frame, k]).wait_recv()
            if step < 2 * chips - 2:
                kgather(k, kv_out.at[core, k]).start()
            kshare(k, kv_out.at[core, k]).start()

    kdone = 0
    for step in range(1, chips):
        k = chunk(1 - step)
        for j in range(len(spans)):
            gather(j, k, mine).wait_recv()
            if step < chips - 1:
                gather(j, k, mid_out.at[core]).start()
            share(j, k, mid_out.at[core]).start()
            if kdone < 2 * chips - 1:
                kstep(kdone)
                kdone += 1
    for step in range(kdone, 2 * chips - 1):
        kstep(step)

    def drain(k, carry):
        pair(k).wait_send()
        kpair(k).wait_send()
        for j in range(len(spans)):
            share(j, k, mine).wait_send()
            share_from(j, k).wait_recv()
        kshare(k, kmine.at[frame, k]).wait_send()
        kshare_from(k).wait_recv()
        return carry

    lax.fori_loop(0, chips, drain, 0)

    def drain_ring(step, carry):
        for j in range(len(spans)):
            ring(j, chunk(-step)).wait_send()
            gather(j, chunk(1 - step), mine).wait_send()
        kring(chunk(-step)).wait_send()
        kgather(chunk(1 - step), kmine.at[frame, 0]).wait_send()
        return carry

    lax.fori_loop(0, chips - 1, drain_ring, 0)
    for hop in range(1, frames):
        across(hop).wait_send()
    k = chunk(1)
    for j, (start, count) in enumerate(spans):
        rows = pl.ds(start, count)
        pltpu.make_async_copy(mine.at[k, rows], mid_out.at[core, k, rows], own_sem.at[j]).wait()
    pltpu.make_async_copy(kmine.at[frame, k], kv_out.at[core, k], own_sem.at[len(spans)]).wait()


def reduce_all(mid, kv):
    chips, rows, width = mid.shape[1:]
    frames, kv_rows = kv.shape[0], kv.shape[3]
    half = (rows // 16 + 1) // 2 * 8
    spans = ((0, rows - half), (rows - half, half))
    dma = pltpu.SemaphoreType.DMA
    n = len(spans)
    f32 = jnp.float32
    scratch = [
        pltpu.VMEM((chips, rows, width), f32), pltpu.VMEM((chips, rows, width), f32), pltpu.VMEM((chips, rows, width), f32),
        pltpu.VMEM((frames, chips, kv_rows, width), f32), pltpu.VMEM((frames, chips, kv_rows, width), f32),
        pltpu.VMEM((max(frames - 1, 1), chips, kv_rows, width), f32), pltpu.VMEM((chips, kv_rows, width), f32),
        dma((chips,)), dma((chips,)), dma((chips,)),
        dma((n, chips)), dma((n, chips)), dma((n, chips)), dma((n, chips)), dma((n, chips)), dma((n, chips)), dma((n + 1,)),
        dma((chips,)), dma((chips,)), dma((chips,)),
        dma((max(frames - 1, 1),)), dma((max(frames - 1, 1),)),
        dma((chips,)), dma((chips,)), dma((chips,)), dma((chips,)), dma((chips,)), dma((chips,)),
    ]
    return pl.pallas_call(
        functools.partial(reduce_kernel, chips, frames, spans),
        out_shape=(jax.ShapeDtypeStruct(mid.shape, f32), jax.ShapeDtypeStruct(kv.shape[1:], f32)),
        in_specs=[pl.BlockSpec(memory_space=pl.ANY)] * 2,
        out_specs=(pl.BlockSpec(memory_space=pl.ANY),) * 2,
        scratch_shapes=scratch,
        compiler_params=pltpu.CompilerParams(collective_id=0, has_side_effects=True, vmem_limit_bytes=56 * 2**20),
        name="reduce_all",
    )(mid, kv)


def shards(
    tokens,
    skip,
    latent_init,
    tok_gain,
    query_gain,
    mlp_gain,
    self_gain,
    w_query,
    w_keyval,
    w_out,
    w_up,
    w_down,
    w_self_qkv,
    w_self_out,
    grad_out,
):
    item_count, row_count, width = tokens.shape
    latent_count = latent_init.shape[0]
    factor = (width // HEADS) ** (-0.5)
    keep_flag = (1 - skip).astype(jnp.float32)[:, None, None]
    tok_normed, tok_inverse = norm_parts(tokens.astype(jnp.float32))
    tok_in = (tok_normed * tok_gain).astype(jnp.bfloat16)
    keyval = forward_mul(tok_in, w_keyval).astype(jnp.bfloat16)
    key_heads = split_heads(keyval[..., :width])
    value_heads = split_heads(keyval[..., width:])
    latent_rows = latent_init.astype(jnp.float32)
    query_normed, query_inverse = norm_parts(latent_rows)
    query_in = (query_normed * query_gain).astype(jnp.bfloat16)
    query_one = jnp.dot(query_in, w_query, preferred_element_type=jnp.float32).astype(jnp.bfloat16)
    queries = jnp.broadcast_to(query_one, (item_count, latent_count, width))
    query_heads = split_heads(queries)
    scores = (
        jnp.einsum("iqhe,ikhe->ihqk", query_heads, key_heads, preferred_element_type=jnp.float32)
        * factor
    )
    local_max = jnp.max(scores, axis=-1)
    row_max = lax.pmax(local_max, "frames")
    row_total = lax.psum(jnp.sum(jnp.exp(scores - row_max[..., None]), axis=-1), "frames")
    log_total = row_max + jnp.log(row_total)
    probs_low = jnp.exp(scores - log_total[..., None]).astype(jnp.bfloat16)
    heard_part = join_heads(
        jnp.einsum("ihqk,ikhe->iqhe", probs_low, value_heads, preferred_element_type=jnp.float32)
    )
    heard = lax.psum(heard_part, "frames")
    heard_low = heard.astype(jnp.bfloat16)
    after_cross = latent_rows[None] + keep_flag * forward_mul(heard_low, w_out)
    mlp_normed, mlp_inverse = norm_parts(after_cross)
    mlp_in = (mlp_normed * mlp_gain).astype(jnp.bfloat16)
    hidden = forward_mul(mlp_in, w_up)
    activation, gelu_pull = jax.vjp(jax.nn.gelu, hidden)
    activation_low = activation.astype(jnp.bfloat16)
    after_mlp = after_cross + forward_mul(activation_low, w_down)
    self_normed, self_inverse = norm_parts(after_mlp)
    self_in = (self_normed * self_gain).astype(jnp.bfloat16)
    triple = forward_mul(self_in, w_self_qkv).astype(jnp.bfloat16)
    self_query = split_heads(triple[..., :width])
    self_key = split_heads(triple[..., width : 2 * width])
    self_value = split_heads(triple[..., 2 * width :])
    self_scores = (
        jnp.einsum("iqhe,ikhe->ihqk", self_query, self_key, preferred_element_type=jnp.float32)
        * factor
    )
    self_shifted = jnp.exp(self_scores - jnp.max(self_scores, axis=-1, keepdims=True))
    self_probs = self_shifted / jnp.sum(self_shifted, axis=-1, keepdims=True)
    self_low = self_probs.astype(jnp.bfloat16)
    mixed = join_heads(
        jnp.einsum("ihqk,ikhe->iqhe", self_low, self_value, preferred_element_type=jnp.float32)
    )
    mixed_low = mixed.astype(jnp.bfloat16)
    after_self = after_mlp + forward_mul(mixed_low, w_self_out)
    frame_count = lax.axis_size("frames")
    frame_index = lax.axis_index("frames")
    latent_share = latent_count // frame_count
    out_latents = lax.dynamic_slice_in_dim(
        after_self, frame_index * latent_share, latent_share, 1
    ).astype(jnp.bfloat16)
    cotangent = grad_out.astype(jnp.float32)
    grad_self_out = weight_mul(mixed_low, own_columns(grad_out, frame_index, frame_count))
    d_mixed = input_mul(grad_out, w_self_out).astype(jnp.bfloat16)
    d_mixed_heads = split_heads(d_mixed)
    d_self_probs = jnp.einsum(
        "iqhe,ikhe->ihqk", d_mixed_heads, self_value, preferred_element_type=jnp.float32
    )
    self_delta = jnp.einsum("iqhe,iqhe->ihq", d_mixed_heads.astype(jnp.float32), split_heads(mixed))
    d_self_scores = (self_probs * (d_self_probs - self_delta[..., None])).astype(jnp.bfloat16)
    d_self_query = (
        jnp.einsum("ihqk,ikhe->iqhe", d_self_scores, self_key, preferred_element_type=jnp.float32)
        * factor
    )
    d_self_key = (
        jnp.einsum("ihqk,iqhe->ikhe", d_self_scores, self_query, preferred_element_type=jnp.float32)
        * factor
    )
    d_self_value = jnp.einsum(
        "ihqk,iqhe->ikhe", self_low, d_mixed_heads, preferred_element_type=jnp.float32
    )
    d_triple = jnp.concatenate(
        [join_heads(d_self_query), join_heads(d_self_key), join_heads(d_self_value)], axis=-1
    ).astype(jnp.bfloat16)
    grad_self_qkv = weight_mul(self_in, own_columns(d_triple, frame_index, frame_count))
    self_back, grad_self_gain = norm_back(
        input_mul(d_triple, w_self_qkv), self_normed, self_inverse, self_gain
    )
    d_after_mlp = cotangent + self_back
    mlp_branch = d_after_mlp.astype(jnp.bfloat16)
    grad_down = weight_mul(activation_low, own_columns(mlp_branch, frame_index, frame_count))
    d_activation = input_mul(mlp_branch, w_down)
    d_hidden = gelu_pull(d_activation)[0].astype(jnp.bfloat16)
    grad_up = weight_mul(mlp_in, own_columns(d_hidden, frame_index, frame_count))
    mlp_back, grad_mlp_gain = norm_back(
        input_mul(d_hidden, w_up), mlp_normed, mlp_inverse, mlp_gain
    )
    d_after_cross = d_after_mlp + mlp_back
    d_attn = (keep_flag * d_after_cross).astype(jnp.bfloat16)
    grad_out_w = weight_mul(heard_low, own_columns(d_attn, frame_index, frame_count))
    d_heard = input_mul(d_attn, w_out).astype(jnp.bfloat16)
    d_heard_heads = split_heads(d_heard)
    again_scores = (
        jnp.einsum("iqhe,ikhe->ihqk", query_heads, key_heads, preferred_element_type=jnp.float32)
        * factor
    )
    probs_full = jnp.exp(again_scores - log_total[..., None])
    probs_again = probs_full.astype(jnp.bfloat16)
    d_probs = jnp.einsum(
        "iqhe,ikhe->ihqk", d_heard_heads, value_heads, preferred_element_type=jnp.float32
    )
    cross_delta = jnp.einsum(
        "iqhe,iqhe->ihq", d_heard_heads.astype(jnp.float32), split_heads(heard)
    )
    d_scores = (probs_full * (d_probs - cross_delta[..., None])).astype(jnp.bfloat16)
    query_part = join_heads(
        jnp.einsum("ihqk,ikhe->iqhe", d_scores, key_heads, preferred_element_type=jnp.float32)
        * factor
    )
    query_total = jnp.sum(query_part, axis=0)
    d_keys = (
        jnp.einsum("ihqk,iqhe->ikhe", d_scores, query_heads, preferred_element_type=jnp.float32)
        * factor
    )
    d_values = jnp.einsum(
        "ihqk,iqhe->ikhe", probs_again, d_heard_heads, preferred_element_type=jnp.float32
    )
    d_keyval = jnp.concatenate([join_heads(d_keys), join_heads(d_values)], axis=-1).astype(
        jnp.bfloat16
    )
    keyval_part = weight_mul(tok_in, d_keyval)
    token_back, tok_gain_part = norm_back(
        input_mul(d_keyval, w_keyval), tok_normed, tok_inverse, tok_gain
    )
    token_grad = token_back.astype(jnp.bfloat16)
    query_incoming = jnp.dot(
        query_total, w_query.astype(jnp.float32).T, precision=lax.Precision.HIGHEST
    )
    query_back, query_gain_part = norm_back(query_incoming, query_normed, query_inverse, query_gain)
    own = width // frame_count
    item_devices = lax.axis_size("items")
    mid = jnp.concatenate(
        [pack(part, item_devices, own) for part in (grad_out_w, grad_up, grad_down, grad_self_qkv, grad_self_out)],
        axis=1,
    )

    def blocks(array):
        return jnp.swapaxes(array.reshape(array.shape[0], frame_count, array.shape[1] // frame_count), 0, 1)

    mine_only = (jnp.arange(frame_count) == frame_index).astype(jnp.float32)[:, None, None]
    latent_part = blocks(query_back) + mine_only * blocks(jnp.sum(d_after_cross, axis=0))
    gains = jnp.stack([grad_mlp_gain, grad_self_gain, tok_gain_part, query_gain_part])
    gain_part = blocks(gains) * jnp.where(jnp.arange(4)[None, :, None] < 2, mine_only, 1.0)
    gain_part = jnp.pad(gain_part, ((0, 0), (0, 8 * item_devices - 4), (0, 0)))
    small = jnp.concatenate([blocks(query_total), latent_part], axis=1)
    kv = jnp.concatenate(
        [pack(blocks(keyval_part), item_devices, own), pack(small, item_devices, own), pack(gain_part, item_devices, own)],
        axis=2,
    )
    chips = item_devices // 2
    mid_sum, kv_sum = reduce_all(
        mid.reshape(2, chips, mid.shape[1], own), kv.reshape(frame_count, 2, chips, kv.shape[2], own)
    )
    mid_sum = mid_sum.reshape(mid.shape)
    kv_sum = kv_sum.reshape(kv.shape[1:])
    hidden_width = w_up.shape[1]
    sum_out, sum_up, sum_down, sum_qkv, sum_self_out = cut(
        mid_sum,
        (
            (width, own),
            (width, hidden_width // frame_count),
            (hidden_width, own),
            (width, 3 * own),
            (width, own),
        ),
    )
    sum_keyval, sum_small, sum_gains = cut(
        kv_sum, ((width, 2 * own), (2 * latent_count, own), (8 * item_devices, own))
    )
    grad_query_w = jnp.dot(
        query_in.astype(jnp.float32).T, sum_small[:latent_count], precision=lax.Precision.HIGHEST
    )
    return (
        out_latents,
        token_grad,
        sum_small[latent_count:],
        sum_gains[2],
        sum_gains[3],
        sum_gains[0],
        sum_gains[1],
        grad_query_w,
        sum_keyval,
        sum_out,
        sum_up,
        sum_down,
        sum_qkv,
        sum_self_out,
    )


def solution(mesh):
    in_specs = (
        P("items", "frames", None),
        P("items"),
        P(),
        P(),
        P(),
        P(),
        P(),
        P(),
        P(),
        P(),
        P(),
        P(),
        P(),
        P(),
        P("items", None, None),
    )
    out_specs = (
        P("items", "frames", None),
        P("items", "frames", None),
        P(None, "frames"),
        P("frames"),
        P("frames"),
        P("frames"),
        P("frames"),
        P(None, "frames"),
        P(None, "frames"),
        P(None, "frames"),
        P(None, "frames"),
        P(None, "frames"),
        P(None, "frames"),
        P(None, "frames"),
    )
    return jax.shard_map(shards, mesh=mesh, in_specs=in_specs, out_specs=out_specs, check_vma=False)
```

```python
import functools

import jax
import jax.numpy as jnp
from jax import lax
from jax.experimental import pallas as pl
from jax.experimental.pallas import tpu as pltpu
from jax.sharding import PartitionSpec as P

MESH = pl.DeviceIdType.MESH
HEADS = 12
EPSILON = 1e-05
LANES = 128
BLOCK = 256
STREAMS = 2


def nn(left, right):
    return lax.dot_general(left, right, (((1,), (0,)), ((), ())), preferred_element_type=jnp.float32)


def nt(left, right):
    return lax.dot_general(left, right, (((1,), (1,)), ((), ())), preferred_element_type=jnp.float32)


def norm_down(columns):
    centered = columns - jnp.mean(columns, axis=0, keepdims=True)
    inverse = lax.rsqrt(jnp.mean(centered * centered, axis=0, keepdims=True) + EPSILON)
    return centered * inverse, inverse


def cross_forward_kernel(
    frames,
    tokens_ref, w_ref, gain_ref, latent_ref, qgain_ref, wq_ref,
    kv_out, heard_out, log_out, query_out,
    tokens, w_t, tok_in, kv, queries, sent, got,
    load_sem, kv_sem, y_send, y_recv,
):
    items, rows, width = tokens_ref.shape
    latents = latent_ref.shape[0]
    head = width // HEADS
    item = lax.axis_index("items")
    frame = lax.axis_index("frames")
    stat = sent.shape[1] - width

    barrier = pltpu.get_barrier_semaphore()
    for hop in range(1, frames):
        pl.semaphore_signal(barrier, inc=1, device_id=(item, lax.rem(frame + hop, frames)), device_id_type=MESH)

    def load(i):
        return pltpu.make_async_copy(tokens_ref.at[i], tokens.at[i], load_sem.at[i])

    def save(i):
        return pltpu.make_async_copy(kv.at[i], kv_out.at[i], kv_sem.at[i])

    def across(i, hop):
        return pltpu.make_async_remote_copy(
            src_ref=sent.at[i], dst_ref=got.at[hop - 1, i], send_sem=y_send.at[hop - 1, i], recv_sem=y_recv.at[hop - 1, i],
            device_id=(item, lax.rem(frame + hop, frames)), device_id_type=MESH,
        )

    for i in range(items):
        load(i).start()
    for block in range(2 * width // 256):
        w_t[pl.ds(block * 256, 256), :] = w_ref[:, pl.ds(block * 256, 256)].T
    rows_in = latent_ref[...].astype(jnp.float32)
    centered = rows_in - jnp.mean(rows_in, axis=-1, keepdims=True)
    inverse = lax.rsqrt(jnp.mean(centered * centered, axis=-1, keepdims=True) + EPSILON)
    query_in = (centered * inverse * qgain_ref[...]).astype(jnp.bfloat16)
    query = nn(query_in, wq_ref[...]).astype(jnp.bfloat16)
    query_out[...] = query
    scaled = query * jnp.bfloat16(head ** -0.5)
    for h in range(HEADS):
        queries[h] = scaled[:, h * head : (h + 1) * head]
    pl.semaphore_wait(barrier, frames - 1)

    def one_item(i, carry):
        load(i).wait()

        def norm_block(b, inner):
            window = pl.ds(pl.multiple_of(b * LANES, LANES), LANES)
            columns = tokens[i, window, :].T.astype(jnp.float32)
            normed, _ = norm_down(columns)
            tok_in[:, window] = (normed * gain_ref[...]).astype(jnp.bfloat16)
            return inner

        lax.fori_loop(0, rows // LANES, norm_block, 0)
        for block in range(2 * width // 256):
            window = pl.ds(block * 256, 256)
            kv[i, window, :] = nn(w_t[window, :], tok_in[...]).astype(jnp.bfloat16)
        save(i).start()
        lane = lax.broadcasted_iota(jnp.int32, (latents, LANES), 1)
        stats = jnp.zeros((latents, LANES), jnp.float32)
        for h in range(HEADS):
            scores = nn(queries[h], kv[i, pl.ds(h * head, head), :])
            most = jnp.max(scores, axis=-1, keepdims=True)
            shifted = jnp.exp(scores - most)
            total = jnp.sum(shifted, axis=-1, keepdims=True)
            stats = jnp.where(lane == h, most, stats)
            stats = jnp.where(lane == h + stat // 2, total, stats)
            sent[i, pl.ds(h * head, head), :] = nt(kv[i, pl.ds(width + h * head, head), :], shifted.astype(jnp.bfloat16))
        sent[i, pl.ds(width, stat), :] = stats.T[:stat]
        for hop in range(1, frames):
            across(i, hop).start()
        return carry

    lax.fori_loop(0, items, one_item, 0)

    def combine(i, carry):
        for hop in range(1, frames):
            across(i, hop).wait_recv()
        parts = [sent.at[i]] + [got.at[hop, i] for hop in range(frames - 1)]
        highs = [part[pl.ds(width, stat // 2), :] for part in parts]
        sums = [part[pl.ds(width + stat // 2, stat // 2), :] for part in parts]
        most = functools.reduce(jnp.maximum, highs)
        total = functools.reduce(jnp.add, [low * jnp.exp(high - most) for high, low in zip(highs, sums)])
        log_total = most + jnp.log(total)
        scales = [jnp.exp(high - log_total) for high in highs]
        for h in range(HEADS):
            window = pl.ds(h * head, head)
            heard_out[i, window, :] = functools.reduce(
                jnp.add, [part[window, :] * scale[h : h + 1] for part, scale in zip(parts, scales)]
            )
        padded = jnp.concatenate([log_total, jnp.zeros((latents - stat // 2, latents), jnp.float32)], axis=0)
        log_out[i] = padded.T
        return carry

    lax.fori_loop(0, items, combine, 0)
    for i in range(items):
        save(i).wait()
        for hop in range(1, frames):
            across(i, hop).wait_send()


def cross_forward(frames, tokens, w_keyval, tok_gain, latent_init, query_gain, w_query):
    items, rows, width = tokens.shape
    latents = latent_init.shape[0]
    dma = pltpu.SemaphoreType.DMA
    vmem = pl.BlockSpec(memory_space=pltpu.VMEM)
    anywhere = pl.BlockSpec(memory_space=pl.ANY)
    peers = max(frames - 1, 1)
    return pl.pallas_call(
        functools.partial(cross_forward_kernel, frames),
        out_shape=(
            jax.ShapeDtypeStruct((items, 2 * width, rows), jnp.bfloat16),
            jax.ShapeDtypeStruct((items, width, latents), jnp.float32),
            jax.ShapeDtypeStruct((items, latents, LANES), jnp.float32),
            jax.ShapeDtypeStruct((latents, width), jnp.bfloat16),
        ),
        in_specs=[anywhere] + [vmem] * 5,
        out_specs=(anywhere, vmem, vmem, vmem),
        scratch_shapes=[
            pltpu.VMEM((items, rows, width), jnp.bfloat16),
            pltpu.VMEM((2 * width, width), jnp.bfloat16),
            pltpu.VMEM((width, rows), jnp.bfloat16),
            pltpu.VMEM((items, 2 * width, rows), jnp.bfloat16),
            pltpu.VMEM((HEADS, latents, width // HEADS), jnp.bfloat16),
            pltpu.VMEM((items, width + 32, latents), jnp.float32),
            pltpu.VMEM((peers, items, width + 32, latents), jnp.float32),
            dma((items,)), dma((items,)), dma((peers, items)), dma((peers, items)),
        ],
        compiler_params=pltpu.CompilerParams(collective_id=1, has_side_effects=True, vmem_limit_bytes=48 * 2**20),
        name="cross_forward",
    )(tokens, w_keyval, tok_gain[:, None], latent_init, query_gain[None, :], w_query)


def gelu_parts(value):
    slope = (2 / jnp.pi) ** 0.5
    square = value * value
    tanh = jnp.tanh(slope * value * (1.0 + 0.044715 * square))
    half = 0.5 + 0.5 * tanh
    bend = (0.5 * slope) * (1.0 + (3 * 0.044715) * square)
    return value * half, half + value * (1.0 - tanh * tanh) * bend


def norm_down_back(incoming, normed, inverse, gain):
    scaled = incoming * gain
    average = jnp.mean(scaled, axis=0, keepdims=True)
    along = jnp.mean(scaled * normed, axis=0, keepdims=True)
    return inverse * (scaled - average - normed * along)


def middle_kernel(
    frames,
    heard_ref, skip_ref, latent_ref, grad_ref, mgain_ref, sgain_ref,
    w_out_ref, w_up_ref, w_down_ref, w_qkv_ref, w_self_ref,
    mid_out, latents_out, d_heard_out, delta_out, d_latent_out, gain_out,
    w_out, w_up, w_down, w_qkv, w_self,
    heard, cross, mlp_in, act, slope, after, self_in, triple, mixed, cotangent, d_mixed, d_triple, d_hidden, branch,
    rows_f32, stage,
    w_sem, stage_sem,
):
    items, width, latents = heard_ref.shape
    hidden = w_up_ref.shape[1]
    head = width // HEADS
    factor = head ** -0.5
    own = width // frames
    frame = lax.axis_index("frames")
    pieces = mid_out.shape[0]
    loads = [
        pltpu.make_async_copy(source, target, w_sem.at[index])
        for index, (source, target) in enumerate(
            ((w_self_ref, w_self), (w_out_ref, w_out), (w_up_ref, w_up), (w_down_ref, w_down), (w_qkv_ref, w_qkv))
        )
    ]
    for copy in loads:
        copy.start()

    def item_window(i):
        return pl.ds(pl.multiple_of(i * latents, latents), latents)

    def each_item(body):
        def step(i, carry):
            body(i, item_window(i))
            return carry

        lax.fori_loop(0, items, step, 0)

    def each_block(count, body):
        def step(b, carry):
            body(pl.ds(pl.multiple_of(b * BLOCK, BLOCK), BLOCK))
            return carry

        lax.fori_loop(0, count // BLOCK, step, 0)

    def down(weight, source, window):
        return nn(weight[:, window].T, source[...])

    sent = [0]

    pending = {}

    def put(first_piece, count, offset, left, right):
        size = width // count
        slot = sent[0] % stage.shape[0]
        sent[0] += 1
        if slot in pending:
            pending[slot].wait()
        view = stage.at[slot]
        for block in range(width // BLOCK):
            window = pl.ds(block * BLOCK, BLOCK)
            view[window, :] = nt(left[window, :], right[...])
        copies = pltpu.make_async_copy(
            view.reshape(count, size, own), mid_out.at[pl.ds(first_piece, count), pl.ds(offset, size)], stage_sem.at[slot]
        )
        copies.start()
        pending[slot] = copies

    def load_heard(i, window):
        heard[:, window] = heard_ref[i].astype(jnp.bfloat16)
        cotangent[:, window] = grad_ref[i].T

    each_item(load_heard)
    loads[0].wait()

    def back_mixed(window):
        d_mixed[window, :] = nn(w_self[window, :], cotangent[...]).astype(jnp.bfloat16)

    each_block(width, back_mixed)
    loads[1].wait()

    def out_block(window):
        cross[window, :] = down(w_out, heard, window)

    each_block(width, out_block)

    def cross_item(i, window):
        keep = (1 - skip_ref[i]).astype(jnp.float32)
        total = latent_ref[...].astype(jnp.float32).T + keep * cross[:, window]
        cross[:, window] = total
        normed, _ = norm_down(total)
        mlp_in[:, window] = (normed * mgain_ref[...]).astype(jnp.bfloat16)

    each_item(cross_item)
    loads[2].wait()

    def up_block(window):
        value, bend = gelu_parts(down(w_up, mlp_in, window))
        act[window, :] = value.astype(jnp.bfloat16)
        slope[window, :] = bend

    each_block(hidden, up_block)
    loads[3].wait()

    def down_block(window):
        after[window, :] = cross[window, :] + down(w_down, act, window)

    each_block(width, down_block)

    def after_item(i, window):
        normed, _ = norm_down(after[:, window])
        self_in[:, window] = (normed * sgain_ref[...]).astype(jnp.bfloat16)

    each_item(after_item)
    loads[4].wait()

    def triple_block(window):
        triple[window, :] = down(w_qkv, self_in, window).astype(jnp.bfloat16)

    each_block(3 * width, triple_block)

    def attend_item(i, window):
        for h in range(HEADS):
            part = [pl.ds(third * width + h * head, head) for third in range(3)]
            query, key, value = [triple[rows, window] for rows in part]
            d_mix = d_mixed[part[0], window]
            scores = nn(query.T, key) * factor
            shifted = jnp.exp(scores - jnp.max(scores, axis=-1, keepdims=True))
            probs = shifted / jnp.sum(shifted, axis=-1, keepdims=True)
            low = probs.astype(jnp.bfloat16)
            mixed[part[0], window] = nt(value, low).astype(jnp.bfloat16)
            d_probs = nn(d_mix.T, value)
            delta = jnp.sum(low.astype(jnp.float32) * d_probs, axis=-1, keepdims=True)
            d_scores = (probs * (d_probs - delta)).astype(jnp.bfloat16)
            d_triple[part[0], window] = (nt(key, d_scores) * factor).astype(jnp.bfloat16)
            d_triple[part[1], window] = (nn(query, d_scores) * factor).astype(jnp.bfloat16)
            d_triple[part[2], window] = nn(d_mix, low).astype(jnp.bfloat16)

    each_item(attend_item)
    up_rows, down_rows = width // pieces, hidden // pieces
    first_up = up_rows
    first_down = first_up + up_rows * (hidden // width)
    first_qkv = first_down + down_rows
    first_self = first_qkv + 3 * up_rows
    my_columns = pl.multiple_of(frame * own, own)
    put(0, pieces, first_self, mixed, cotangent.at[pl.ds(my_columns, own), :])
    for third in range(3):
        put(0, pieces, first_qkv + third * up_rows, self_in, d_triple.at[pl.ds(3 * my_columns + third * own, own), :])

    def self_block(window):
        rows_f32[window, :] = nn(w_qkv[window, :], d_triple[...])

    each_block(width, self_block)
    gain_out[...] = jnp.zeros_like(gain_out)
    lane = lax.broadcasted_iota(jnp.int32, (width, LANES), 1)

    def self_back(i, window):
        normed, inverse = norm_down(after[:, window])
        incoming = rows_f32[:, window]
        gain_out[...] += jnp.where(lane == 1, jnp.sum(incoming * normed, axis=-1, keepdims=True), 0.0)
        d_after = cotangent[:, window].astype(jnp.float32) + norm_down_back(incoming, normed, inverse, sgain_ref[...])
        branch[:, window] = d_after.astype(jnp.bfloat16)
        rows_f32[:, window] = d_after

    each_item(self_back)

    def latents_block(window):
        after[window, :] = after[window, :] + down(w_self, mixed, window)

    each_block(width, latents_block)
    share = latents // frames

    def latents_item(i, window):
        d_latent_out[...] = after[:, window].T
        latents_out[i] = d_latent_out[pl.ds(pl.multiple_of(frame * share, share), share), :].astype(jnp.bfloat16)

    each_item(latents_item)

    for group in range(hidden // width):
        left = act.at[pl.ds(group * width, width), :]
        count = pieces * width // hidden
        put(group * count, count, first_down, left, branch.at[pl.ds(my_columns, own), :])

    def hidden_block(window):
        d_hidden[window, :] = (nn(w_down[window, :], branch[...]) * slope[window, :]).astype(jnp.bfloat16)

    each_block(hidden, hidden_block)
    for part in range(hidden // width):
        put(0, pieces, first_up + part * up_rows, mlp_in, d_hidden.at[pl.ds(frame * (hidden // frames) + part * own, own), :])

    def mlp_block(window):
        after[window, :] = nn(w_up[window, :], d_hidden[...])

    each_block(width, mlp_block)
    d_latent_out[...] = jnp.zeros_like(d_latent_out)

    def mlp_back(i, window):
        normed, inverse = norm_down(cross[:, window])
        incoming = after[:, window]
        gain_out[...] += jnp.where(lane == 0, jnp.sum(incoming * normed, axis=-1, keepdims=True), 0.0)
        d_cross = rows_f32[:, window] + norm_down_back(incoming, normed, inverse, mgain_ref[...])
        d_latent_out[...] += d_cross.T
        keep = (1 - skip_ref[i]).astype(jnp.float32)
        branch[:, window] = (keep * d_cross).astype(jnp.bfloat16)

    each_item(mlp_back)
    put(0, pieces, 0, heard, branch.at[pl.ds(my_columns, own), :])

    def heard_block(window):
        d_heard_out[window, :] = nn(w_out[window, :], branch[...]).astype(jnp.bfloat16)

    each_block(width, heard_block)

    def delta_item(i, window):
        product = d_heard_out[:, window].astype(jnp.float32) * heard_ref[i]
        sums = jnp.sum(product.reshape(HEADS, head, latents), axis=1)
        padded = jnp.concatenate([sums, jnp.zeros((latents - HEADS, latents), jnp.float32)], axis=0)
        delta_out[i] = padded.T

    each_item(delta_item)
    for copy in pending.values():
        copy.wait()


def middle(frames, pieces, heard, skip, latent_init, grad_out, mlp_gain, self_gain, w_out, w_up, w_down, w_self_qkv, w_self_out):
    items, width, latents = heard.shape
    hidden = w_up.shape[1]
    own = width // frames
    columns = items * latents
    rows = (width + hidden + hidden + 3 * width + width) // pieces
    bf16, f32 = jnp.bfloat16, jnp.float32
    vmem = pl.BlockSpec(memory_space=pltpu.VMEM)
    anywhere = pl.BlockSpec(memory_space=pl.ANY)
    dma = pltpu.SemaphoreType.DMA
    return pl.pallas_call(
        functools.partial(middle_kernel, frames),
        out_shape=(
            jax.ShapeDtypeStruct((pieces, rows, own), f32),
            jax.ShapeDtypeStruct((items, latents // frames, width), bf16),
            jax.ShapeDtypeStruct((width, columns), bf16),
            jax.ShapeDtypeStruct((items, latents, LANES), f32),
            jax.ShapeDtypeStruct((latents, width), f32),
            jax.ShapeDtypeStruct((width, LANES), f32),
        ),
        in_specs=[vmem, pl.BlockSpec(memory_space=pltpu.SMEM)] + [vmem] * 4 + [anywhere] * 5,
        out_specs=(anywhere,) + (vmem,) * 5,
        scratch_shapes=[pltpu.VMEM(w.shape, bf16) for w in (w_out, w_up, w_down, w_self_qkv, w_self_out)]
        + [
            pltpu.VMEM((width, columns), bf16),
            pltpu.VMEM((width, columns), f32),
            pltpu.VMEM((width, columns), bf16),
            pltpu.VMEM((hidden, columns), bf16),
            pltpu.VMEM((hidden, columns), f32),
            pltpu.VMEM((width, columns), f32),
            pltpu.VMEM((width, columns), bf16),
            pltpu.VMEM((3 * width, columns), bf16),
            pltpu.VMEM((width, columns), bf16),
            pltpu.VMEM((width, columns), bf16),
            pltpu.VMEM((width, columns), bf16),
            pltpu.VMEM((3 * width, columns), bf16),
            pltpu.VMEM((hidden, columns), bf16),
            pltpu.VMEM((width, columns), bf16),
            pltpu.VMEM((width, columns), f32),
            pltpu.VMEM((3, width, own), f32),
            dma((5,)), dma((3,)),
        ],
        compiler_params=pltpu.CompilerParams(vmem_limit_bytes=58 * 2**20),
        name="middle",
    )(heard, skip, latent_init, grad_out, mlp_gain[:, None], self_gain[:, None], w_out, w_up, w_down, w_self_qkv, w_self_out)


def add_into(target, parts, rows):
    step = next(size for size in (104, 80, 64, 48, 40, 24, 16, 8) if rows % size == 0)

    def body(index, carry):
        window = pl.ds(pl.multiple_of(index * step, 8), step)
        total = parts[0][window]
        for part in parts[1:]:
            total = total + part[window]
        target[window] = total
        return carry

    lax.fori_loop(0, rows // step, body, 0)


def nn_exact(left, right):
    total = jnp.zeros((left.shape[0], right.shape[1]), jnp.float32)
    rest = right
    for _ in range(3):
        part = rest.astype(jnp.bfloat16)
        total = total + nn(left, part)
        rest = rest - part.astype(jnp.float32)
    return total


def backward_kernel(
    chips, frames, spans,
    mid_ref, tokens_ref, kv_ref, d_heard_ref, log_ref, delta_ref, query_ref,
    w_ref, gain_ref, latent_ref, qgain_ref, wq_ref, d_latent_ref, gains_ref,
    mid_out, kv_out, token_out,
    mine, sib, rx, kmine, ksib, ky, krx,
    tokens, kv, tok_in, d_kv, normed, incoming, queries, queries_t, d_query, gain_sum, token_stage,
    ld_sem, sib_send, sib_recv, rs_send, rs_recv, ag_send, ag_recv, share_send, share_recv, own_sem,
    ksib_send, ksib_recv, y_send, y_recv, krs_send, krs_recv, kag_send, kag_recv, kshare_send, kshare_recv,
    tok_sem, kv_sem, out_sem,
):
    items = lax.axis_index("items")
    frame = lax.axis_index("frames")
    core = lax.rem(items, 2)
    chip = items // 2
    column = lax.rem(chip, 2)
    line = chip // 2
    place = line + column * (chips - 1 - 2 * line)
    way = 1 - 2 * core
    count, rows, width = tokens_ref.shape
    latents = latent_ref.shape[0]
    head = width // HEADS
    factor = head ** -0.5
    own = width // frames
    kv_rows = krx.shape[1]

    def device_at(position):
        position = lax.rem(position + 2 * chips, chips)
        far = position // (chips // 2)
        return (2 * (position + far * (chips - 1 - 2 * position)) + far) * 2 + core

    right, left = device_at(place + way), device_at(place - way)
    sibling = items + way

    def chunk(offset):
        return lax.rem(place + way * offset + 2 * chips, chips)

    def sib_chunk(offset):
        return lax.rem(place - way * offset + 2 * chips, chips)

    barrier = pltpu.get_barrier_semaphore()
    for peer in (left, right, sibling):
        pl.semaphore_signal(barrier, inc=1, device_id=(peer, frame), device_id_type=MESH)
    for hop in range(1, frames):
        pl.semaphore_signal(barrier, inc=1, device_id=(items, lax.rem(frame + hop, frames)), device_id_type=MESH)

    def remote(src, dst, send, recv, peer):
        return pltpu.make_async_remote_copy(
            src_ref=src, dst_ref=dst, send_sem=send, recv_sem=recv, device_id=peer, device_id_type=MESH
        )

    def load(k):
        return pltpu.make_async_copy(mid_ref.at[core, k], mine.at[k], ld_sem.at[k])

    def pair(k):
        return remote(mid_ref.at[1 - core, k], sib.at[k], sib_send.at[k], sib_recv.at[k], (sibling, frame))

    def ring(j, k):
        part = pl.ds(*spans[j])
        return remote(mine.at[k, part], rx.at[k, part], rs_send.at[j, k], rs_recv.at[j, k], (right, frame))

    def gather(j, k, source):
        part = pl.ds(*spans[j])
        return remote(source.at[k, part], mid_out.at[core, k, part], ag_send.at[j, k], ag_recv.at[j, k], (right, frame))

    def share(j, k, source):
        part = pl.ds(*spans[j])
        return remote(source.at[k, part], mid_out.at[core, k, part], share_send.at[j, k], share_recv.at[j, k], (sibling, frame))

    def share_from(j, k):
        part = pl.ds(*spans[j])
        return remote(mine.at[k, part], mid_out.at[1 - core, k, part], share_send.at[j, k], share_recv.at[j, k], (sibling, frame))

    def keep(j, k):
        part = pl.ds(*spans[j])
        return pltpu.make_async_copy(mine.at[k, part], mid_out.at[core, k, part], own_sem.at[j])

    def kpair():
        return remote(kmine.at[:, 1 - core], ksib, ksib_send, ksib_recv, (sibling, frame))

    def across(hop, k):
        other = lax.rem(frame + hop, frames)
        return remote(kmine.at[other, core, k], ky.at[hop - 1, k], y_send.at[hop - 1, k], y_recv.at[hop - 1, k], (items, other))

    def kring(k):
        return remote(kmine.at[frame, core, k], krx.at[k], krs_send.at[k], krs_recv.at[k], (right, frame))

    def kgather(k, source):
        return remote(source, kv_out.at[core, k], kag_send.at[k], kag_recv.at[k], (right, frame))

    def kshare(k, source):
        return remote(source, kv_out.at[core, k], kshare_send.at[k], kshare_recv.at[k], (sibling, frame))

    def kshare_from(k):
        return remote(kmine.at[frame, core, k], kv_out.at[1 - core, k], kshare_send.at[k], kshare_recv.at[k], (sibling, frame))

    def kkeep(k):
        return pltpu.make_async_copy(kmine.at[frame, core, k], kv_out.at[core, k], own_sem.at[len(spans)])

    def rs_tick(step, j, first=False):
        k = chunk(-step)
        if j == 0:
            load(k).wait()
            pair(k).wait_recv()
        start, size = spans[j]
        part = pl.ds(start, size)
        parts = [mine.at[k, part], sib.at[k, part]]
        if not first:
            ring(j, k).wait_recv()
            parts.append(rx.at[k, part])
        add_into(mine.at[k, part], parts, size)

    def rs_send_on(step, j):
        ring(j, chunk(-step)).start()

    def rs_step(step, j, first=False):
        rs_tick(step, j, first)
        rs_send_on(step, j)

    def rs_last(j):
        k = chunk(1)
        rs_tick(chips - 1, j)
        gather(j, k, mine).start()
        share(j, k, mine).start()
        keep(j, k).start()

    def ag_step(step, j):
        k = chunk(1 - step)
        gather(j, k, mine).wait_recv()
        if step < chips - 1:
            gather(j, k, mid_out.at[core]).start()
        share(j, k, mid_out.at[core]).start()

    def k_step(step):
        k = chunk(-step)
        if step < chips:
            parts = [kmine.at[frame, core, k], ksib.at[frame, k]]
            for hop in range(1, frames):
                across(hop, k).wait_recv()
                parts.append(ky.at[hop - 1, k])
            if step > 0:
                kring(k).wait_recv()
                parts.append(krx.at[k])
            add_into(kmine.at[frame, core, k], parts, kv_rows)
            if step < chips - 1:
                kring(k).start()
            else:
                kgather(k, kmine.at[frame, core, k]).start()
                kshare(k, kmine.at[frame, core, k]).start()
                kkeep(k).start()
        else:
            kgather(k, kmine.at[frame, core, k]).wait_recv()
            if step < 2 * chips - 2:
                kgather(k, kv_out.at[core, k]).start()
            kshare(k, kv_out.at[core, k]).start()

    def across_step(step):
        k = chunk(-step)
        for hop in range(1, frames):
            other = lax.rem(frame + hop, frames)
            add_into(kmine.at[other, core, k], [kmine.at[other, core, k], ksib.at[other, k]], kv_rows)
            across(hop, k).start()

    def tok_load(i):
        return pltpu.make_async_copy(tokens_ref.at[i], tokens.at[lax.rem(i, 2)], tok_sem.at[lax.rem(i, 2)])

    def kv_load(i):
        return pltpu.make_async_copy(kv_ref.at[i], kv.at[lax.rem(i, 2)], kv_sem.at[lax.rem(i, 2)])

    def token_save(i, b):
        slot = lax.rem(b, 2)
        return pltpu.make_async_copy(
            token_stage.at[slot], token_out.at[i, pl.ds(pl.multiple_of(b * LANES, LANES), LANES), :], out_sem.at[slot]
        )

    def start_stage(index, carry):
        pair(sib_chunk(-index)).start()
        load(chunk(-index)).start()
        return carry

    tok_load(0).start()
    kv_load(0).start()
    query = query_ref[...]
    scaled = query * jnp.bfloat16(factor)
    for h in range(HEADS):
        queries[h] = scaled[:, h * head : (h + 1) * head]
    queries_t[...] = scaled.T
    d_query[...] = jnp.zeros_like(d_query)
    gain_sum[...] = jnp.zeros_like(gain_sum)
    pl.semaphore_wait(barrier, 3 + frames - 1)
    lax.fori_loop(0, chips, start_stage, 0)

    def attend(i, heads):
        slot = lax.rem(i, 2)
        columns = pl.ds(pl.multiple_of(i * rows, rows), rows)
        latent_window = pl.ds(pl.multiple_of(i * latents, latents), latents)
        for h in heads:
            keys_at, values_at = pl.ds(h * head, head), pl.ds(width + h * head, head)
            keys, values = kv[slot, keys_at, :], kv[slot, values_at, :]
            d_heard_t = d_heard_ref[keys_at, latent_window]
            probs = jnp.exp(nn(queries[h], keys) - log_ref[i, :, h : h + 1])
            d_probs = nn(d_heard_t.T, values)
            d_scores = (probs * (d_probs - delta_ref[i, :, h : h + 1])).astype(jnp.bfloat16)
            d_kv[keys_at, columns] = nn(queries_t[keys_at, :], d_scores).astype(jnp.bfloat16)
            d_kv[values_at, columns] = nn(d_heard_t, probs.astype(jnp.bfloat16)).astype(jnp.bfloat16)
            d_query[keys_at, :] += nt(keys, d_scores)

    def norm_tokens(i):
        tok_load(i).wait()

        def norm_block(b, carry):
            window = pl.ds(pl.multiple_of(b * LANES, LANES), LANES)
            columns = tokens[lax.rem(i, 2), window, :].T.astype(jnp.float32)
            block, inverse = norm_down(columns)
            normed[pl.ds(0, width), window] = block
            normed[pl.ds(width, 8), window] = jnp.broadcast_to(inverse, (8, LANES))
            tok_in[:, pl.ds(pl.multiple_of(i * rows + b * LANES, LANES), LANES)] = (block * gain_ref[...]).astype(jnp.bfloat16)
            return carry

        lax.fori_loop(0, rows // LANES, norm_block, 0)

    def token_back(i):
        columns = pl.ds(pl.multiple_of(i * rows, rows), rows)

        def product(b, carry):
            window = pl.ds(pl.multiple_of(b * BLOCK, BLOCK), BLOCK)
            incoming[window, :] = nn(w_ref[window, :], d_kv[:, columns])
            return carry

        lax.fori_loop(0, width // BLOCK, product, 0)

        def back_block(b, carry):
            window = pl.ds(pl.multiple_of(b * LANES, LANES), LANES)
            block = normed[pl.ds(0, width), window]
            arriving = incoming[:, window]
            gain_sum[...] += arriving * block
            result = norm_down_back(arriving, block, normed[pl.ds(width, 1), window], gain_ref[...])

            @pl.when((i > 0) | (b > 1))
            def _():
                token_save(i, b).wait()

            token_stage[lax.rem(b, 2)] = result.T.astype(jnp.bfloat16)
            token_save(i, b).start()
            return carry

        lax.fori_loop(0, rows // LANES, back_block, 0)

    for j in range(len(spans)):
        rs_step(0, j, True)

    def one_item(i, carry):
        kv_load(i).wait()

        @pl.when(i + 1 < count)
        def _():
            kv_load(i + 1).start()
            tok_load(i + 1).start()

        norm_tokens(i)
        attend(i, range(HEADS // 2))
        rs_step(i + 1, 0)
        attend(i, range(HEADS // 2, HEADS))
        token_back(i)
        for j in range(1, len(spans)):
            rs_step(i + 1, j)
        return carry

    lax.fori_loop(0, count, one_item, 0)

    per_piece = width // (2 * chips)
    small = 2 * latents // (2 * chips)
    d_query[...] = d_query[...] * factor
    q_total = d_query[...]
    q_normed, q_inverse = norm_down(latent_ref[...].astype(jnp.float32).T)
    q_incoming = nn_exact(wq_ref[...], q_total)
    lane = lax.broadcasted_iota(jnp.int32, (width, LANES), 1)
    gain_columns = gains_ref[...]
    gain_columns = jnp.where(lane == 2, jnp.sum(gain_sum[...], axis=-1, keepdims=True), gain_columns)
    gain_columns = jnp.where(lane == 3, jnp.sum(q_incoming * q_normed, axis=-1, keepdims=True), gain_columns)
    gain_rows = gain_columns.T[:8]
    latent_rows = norm_down_back(q_incoming, q_normed, q_inverse, qgain_ref[...]).T
    query_rows = q_total.T
    for f in range(frames):
        mask = (frame == f).astype(jnp.float32)
        mine_columns = slice(f * own, (f + 1) * own)
        latent_part = latent_rows[:, mine_columns] + mask * d_latent_ref[:, mine_columns]
        both = jnp.concatenate([query_rows[:, mine_columns], latent_part], axis=0)
        kmine[f, :, :, pl.ds(2 * per_piece, small), :] = both.reshape(2, chips, small, own)
        row = lax.broadcasted_iota(jnp.int32, (8, own), 0)
        gain_block = gain_rows[:, mine_columns] * jnp.where(row < 2, mask, 1.0)
        kmine[f, :, :, pl.ds(2 * per_piece + small, 8), :] = jnp.zeros((2, chips, 8, own), jnp.float32)
        kmine[f, 0, 0, pl.ds(2 * per_piece + small, 8), :] = gain_block

    def keyval_block(f, b):
        source = d_kv.at[pl.ds((2 * f + b) * own, own), :]
        size = width // 2
        for start in range(0, width, size):
            block = nt(tok_in[pl.ds(start, size), :], source[...])
            for piece in range(size // per_piece):
                at = start // per_piece + piece
                kmine[f, at // chips, at % chips, pl.ds(b * per_piece, per_piece), :] = block[piece * per_piece : (piece + 1) * per_piece]

    done = count + 1
    blocks = [(f, b) for f in range(frames) for b in range(2)]
    for index, (f, b) in enumerate(blocks):
        keyval_block(f, b)
        if index % 2 == 1 and index + 1 < len(blocks) and done < chips - 1:
            rs_step(done, 0)
            for j in range(1, len(spans)):
                rs_step(done, j)
            done += 1
    kpair().start()
    for step in range(done, chips - 1):
        rs_step(step, 0)
        if step == done:
            kpair().wait_recv()
            for order in range(chips):
                across_step(order)
        for j in range(1, len(spans)):
            rs_step(step, j)
    for j in range(len(spans)):
        rs_last(j)
    kdone = 0
    for step in range(1, chips):
        for j in range(len(spans)):
            ag_step(step, j)
            if kdone < 2 * chips - 1:
                k_step(kdone)
                kdone += 1
    for step in range(kdone, 2 * chips - 1):
        k_step(step)

    def drain(k, carry):
        pair(k).wait_send()
        for j in range(len(spans)):
            share(j, k, mine).wait_send()
            share_from(j, k).wait_recv()
        kshare(k, kmine.at[frame, core, k]).wait_send()
        kshare_from(k).wait_recv()
        for hop in range(1, frames):
            across(hop, k).wait_send()
        return carry

    lax.fori_loop(0, chips, drain, 0)

    def drain_ring(step, carry):
        for j in range(len(spans)):
            ring(j, chunk(-step)).wait_send()
            gather(j, chunk(1 - step), mine).wait_send()
        kring(chunk(-step)).wait_send()
        kgather(chunk(1 - step), kmine.at[frame, core, 0]).wait_send()
        return carry

    lax.fori_loop(0, chips - 1, drain_ring, 0)
    kpair().wait_send()
    for j in range(len(spans)):
        keep(j, chunk(1)).wait()
    kkeep(chunk(1)).wait()
    for b in range(2):
        token_save(0, b).wait()


def backward(frames, mid, tokens, kv, d_heard, log_total, delta, query, w_keyval, tok_gain, latent_init, query_gain, w_query, d_latent, gains):
    chips, mid_rows, own = mid.shape[1:]
    items, rows, width = tokens.shape
    latents = latent_init.shape[0]
    kv_rows = 2 * width // (2 * chips) + 2 * latents // (2 * chips) + 8
    step = mid_rows // 8 // STREAMS * 8
    spans = tuple((j * step, step if j + 1 < STREAMS else mid_rows - j * step) for j in range(STREAMS))
    dma = pltpu.SemaphoreType.DMA
    peers = max(frames - 1, 1)
    n = len(spans)
    f32, bf16 = jnp.float32, jnp.bfloat16
    vmem = pl.BlockSpec(memory_space=pltpu.VMEM)
    anywhere = pl.BlockSpec(memory_space=pl.ANY)
    scratch = [
        pltpu.VMEM((chips, mid_rows, own), f32), pltpu.VMEM((chips, mid_rows, own), f32), pltpu.VMEM((chips, mid_rows, own), f32),
        pltpu.VMEM((frames, 2, chips, kv_rows, own), f32), pltpu.VMEM((frames, chips, kv_rows, own), f32),
        pltpu.VMEM((peers, chips, kv_rows, own), f32), pltpu.VMEM((chips, kv_rows, own), f32),
        pltpu.VMEM((2, rows, width), bf16),
        pltpu.VMEM((2, 2 * width, rows), bf16),
        pltpu.VMEM((width, items * rows), bf16),
        pltpu.VMEM((2 * width, items * rows), bf16),
        pltpu.VMEM((width + 8, rows), f32),
        pltpu.VMEM((width, rows), f32),
        pltpu.VMEM((HEADS, latents, width // HEADS), bf16),
        pltpu.VMEM((width, latents), bf16),
        pltpu.VMEM((width, latents), f32),
        pltpu.VMEM((width, LANES), f32),
        pltpu.VMEM((2, LANES, width), bf16),
        dma((chips,)), dma((chips,)), dma((chips,)),
        dma((n, chips)), dma((n, chips)), dma((n, chips)), dma((n, chips)), dma((n, chips)), dma((n, chips)), dma((n + 1,)),
        dma, dma,
        dma((peers, chips)), dma((peers, chips)),
        dma((chips,)), dma((chips,)), dma((chips,)), dma((chips,)), dma((chips,)), dma((chips,)),
        dma((2,)), dma((2,)), dma((2,)),
    ]
    return pl.pallas_call(
        functools.partial(backward_kernel, chips, frames, spans),
        out_shape=(
            jax.ShapeDtypeStruct(mid.shape, f32),
            jax.ShapeDtypeStruct((2, chips, kv_rows, own), f32),
            jax.ShapeDtypeStruct(tokens.shape, bf16),
        ),
        in_specs=[anywhere] * 3 + [vmem] * 11,
        out_specs=(anywhere,) * 3,
        scratch_shapes=scratch,
        compiler_params=pltpu.CompilerParams(collective_id=0, has_side_effects=True, vmem_limit_bytes=62 * 2**20),
        name="backward",
    )(
        mid, tokens, kv, d_heard, log_total, delta, query, w_keyval, tok_gain[:, None], latent_init,
        query_gain[:, None], w_query, d_latent, gains,
    )


def unpack_kernel(mid_ref, kv_ref, latent_ref, qgain_ref, *rest):
    outs, (query_out, total, sem) = rest[:-3], rest[-3:]
    pieces, _, own = mid_ref.shape
    copies = []

    def place(source, offset, out):
        rows, columns = out.shape
        size = rows // pieces
        view = out.reshape(pieces, size, columns)
        for b in range(columns // own):
            copies.append(
                pltpu.make_async_copy(
                    source.at[:, pl.ds(offset + b * size, size), :], view.at[:, :, pl.ds(b * own, own)], sem.at[len(copies)]
                )
            )
        return offset + size * columns // own

    offset = 0
    for out in outs[:5]:
        offset = place(mid_ref, offset, out)
    offset = place(kv_ref, 0, outs[5])
    latents = outs[6].shape[0]
    small = 2 * latents // pieces
    half = pieces // 2
    copies.append(
        pltpu.make_async_copy(
            kv_ref.at[pl.ds(half, half), pl.ds(offset, small), :], outs[6].reshape(half, small, own), sem.at[len(copies)]
        )
    )
    query = pltpu.make_async_copy(kv_ref.at[pl.ds(0, half), pl.ds(offset, small), :], total, sem.at[len(copies)])
    query.start()
    for copy in copies:
        copy.start()
    normed, _ = norm_down(latent_ref[...].astype(jnp.float32).T)
    query_in = (normed * qgain_ref[...]).astype(jnp.bfloat16)
    query.wait()
    query_out[...] = nn_exact(query_in, total[...].reshape(latents, own))
    for copy in copies:
        copy.wait()


def unpack_all(mid, kv, latent_init, query_gain, shapes):
    f32 = jnp.float32
    own = mid.shape[-1]
    latents, width = latent_init.shape
    pieces = mid.shape[0]
    vmem = pl.BlockSpec(memory_space=pltpu.VMEM)
    anywhere = pl.BlockSpec(memory_space=pl.ANY)
    count = sum(columns // own for _, columns in shapes) + 2
    return pl.pallas_call(
        unpack_kernel,
        out_shape=tuple(jax.ShapeDtypeStruct(shape, f32) for shape in shapes) + (
            jax.ShapeDtypeStruct((latents, own), f32), jax.ShapeDtypeStruct((width, own), f32)),
        in_specs=[anywhere] * 2 + [vmem] * 2,
        out_specs=(anywhere,) * (len(shapes) + 1) + (vmem,),
        scratch_shapes=[pltpu.VMEM((pieces // 2, 2 * latents // pieces, own), f32), pltpu.SemaphoreType.DMA((count,))],
        compiler_params=pltpu.CompilerParams(vmem_limit_bytes=16 * 2**20),
        name="unpack_all",
    )(mid, kv, latent_init, query_gain[:, None])


def unpack(packed, rows, columns):
    pieces, _, width = packed.shape
    split = packed.reshape(pieces, columns // width, rows // pieces, width)
    return jnp.swapaxes(split, 1, 2).reshape(rows, columns)


def cut(packed, shapes):
    start, out = 0, []
    for rows, columns in shapes:
        count = rows * columns // packed.shape[-1] // packed.shape[0]
        out.append(unpack(packed[:, start : start + count], rows, columns))
        start += count
    return out


def shards(
    tokens,
    skip,
    latent_init,
    tok_gain,
    query_gain,
    mlp_gain,
    self_gain,
    w_query,
    w_keyval,
    w_out,
    w_up,
    w_down,
    w_self_qkv,
    w_self_out,
    grad_out,
):
    frames, pieces = lax.axis_size("frames"), lax.axis_size("items")
    latents, width = latent_init.shape
    hidden = w_up.shape[1]
    own = width // frames
    kv, heard, log_total, query = cross_forward(frames, tokens, w_keyval, tok_gain, latent_init, query_gain, w_query)
    mid, out_latents, d_heard, delta, d_latent, gains = middle(
        frames, pieces, heard, skip, latent_init, grad_out, mlp_gain, self_gain, w_out, w_up, w_down, w_self_qkv, w_self_out
    )
    mid_sum, kv_sum, token_grad = backward(
        frames, mid.reshape(2, pieces // 2, mid.shape[1], own), tokens, kv, d_heard, log_total, delta, query,
        w_keyval, tok_gain, latent_init, query_gain, w_query, d_latent, gains,
    )
    mid_sum = mid_sum.reshape(mid.shape)
    kv_sum = kv_sum.reshape((pieces,) + kv_sum.shape[2:])
    shapes = (
        (width, own),
        (width, hidden // frames),
        (hidden, own),
        (width, 3 * own),
        (width, own),
        (width, 2 * own),
    )
    if own % LANES == 0:
        *sums, latent_grad, grad_query = unpack_all(mid_sum, kv_sum, latent_init, query_gain, shapes)
    else:
        sums = cut(mid_sum, shapes[:5])
        keyval_sum, small = cut(kv_sum, (shapes[5], (2 * latents, own)))
        sums.append(keyval_sum)
        latent_grad = small[latents:]
        normed, _ = norm_down(latent_init.astype(jnp.float32).T)
        query_in = (normed * query_gain[:, None]).astype(jnp.bfloat16)
        grad_query = jnp.dot(query_in.astype(jnp.float32), small[:latents], precision=lax.Precision.HIGHEST)
    gain_rows = kv_sum[0, -8:]
    return (
        out_latents,
        token_grad,
        latent_grad,
        gain_rows[2],
        gain_rows[3],
        gain_rows[0],
        gain_rows[1],
        grad_query,
        sums[5],
        sums[0],
        sums[1],
        sums[2],
        sums[3],
        sums[4],
    )


def solution(mesh):
    in_specs = (
        P("items", "frames", None),
        P("items"),
        P(),
        P(),
        P(),
        P(),
        P(),
        P(),
        P(),
        P(),
        P(),
        P(),
        P(),
        P(),
        P("items", None, None),
    )
    out_specs = (
        P("items", "frames", None),
        P("items", "frames", None),
        P(None, "frames"),
        P("frames"),
        P("frames"),
        P("frames"),
        P("frames"),
        P(None, "frames"),
        P(None, "frames"),
        P(None, "frames"),
        P(None, "frames"),
        P(None, "frames"),
        P(None, "frames"),
        P(None, "frames"),
    )
    return jax.shard_map(shards, mesh=mesh, in_specs=in_specs, out_specs=out_specs, check_vma=False)
```

```python
import functools

import jax
import jax.numpy as jnp
from jax import lax
from jax.experimental import pallas as pl
from jax.experimental.pallas import tpu as pltpu
from jax.sharding import PartitionSpec as P

MESH = pl.DeviceIdType.MESH
HEADS = 12
EPSILON = 1e-05
LANES = 128
BLOCK = 256
STREAMS = 3


def nn(left, right):
    return lax.dot_general(left, right, (((1,), (0,)), ((), ())), preferred_element_type=jnp.float32)


def nt(left, right):
    return lax.dot_general(left, right, (((1,), (1,)), ((), ())), preferred_element_type=jnp.float32)


def norm_down(columns):
    centered = columns - jnp.mean(columns, axis=0, keepdims=True)
    inverse = lax.rsqrt(jnp.mean(centered * centered, axis=0, keepdims=True) + EPSILON)
    return centered * inverse, inverse


def gelu_parts(value):
    slope = (2 / jnp.pi) ** 0.5
    square = value * value
    tanh = jnp.tanh(slope * value * (1.0 + 0.044715 * square))
    half = 0.5 + 0.5 * tanh
    bend = (0.5 * slope) * (1.0 + (3 * 0.044715) * square)
    return value * half, half + value * (1.0 - tanh * tanh) * bend


def norm_down_back(incoming, normed, inverse, gain):
    scaled = incoming * gain
    average = jnp.mean(scaled, axis=0, keepdims=True)
    along = jnp.mean(scaled * normed, axis=0, keepdims=True)
    return inverse * (scaled - average - normed * along)


def gain_columns(gain_ref):
    return jnp.broadcast_to(gain_ref[...].reshape(1, -1), (LANES, gain_ref.shape[0])).T


def loop(count, body):
    def step(index, carry):
        body(index)
        return carry

    lax.fori_loop(0, count, step, 0)


def window_at(index, size):
    return pl.ds(pl.multiple_of(index * size, size), size)


def forward_kernel(
    frames, groups,
    tokens_ref, skip_ref, latent_ref, tok_gain_ref, query_gain_ref, mlp_gain_ref, self_gain_ref,
    w_query_ref, w_keyval_ref, w_out_ref, w_up_ref, w_down_ref, w_qkv_ref, w_self_ref, grad_ref,
    kv_out, log_out, query_out, mid_out, latents_out, d_heard_out, delta_out, d_latent_out, gain_out, arrived,
    tokens, tok_in, queries, sent, got,
    w_out, w_out_t, w_self, w_self_t, w_qkv, tall, up_down, down_up,
    heard, cross, mlp_in, act, slope, after, self_in, triple, mixed, cotangent, d_mixed, d_triple, branch, rows_f32,
    tok_gain, mlp_gain, self_gain, stage,
    tok_sem, kv_sem, y_send, y_recv, w_sem, stage_sem, got_sem,
):
    items, rows, width = tokens_ref.shape
    latents = latent_ref.shape[0]
    hidden = w_up_ref.shape[1]
    head = width // HEADS
    factor = head ** -0.5
    own = width // frames
    stat = sent.shape[1] - width
    pieces = mid_out.shape[0]
    item = lax.axis_index("items")
    frame = lax.axis_index("frames")

    barrier = pltpu.get_barrier_semaphore()
    for hop in range(1, frames):
        pl.semaphore_signal(barrier, inc=1, device_id=(item, lax.rem(frame + hop, frames)), device_id_type=MESH)

    wide = 2 * width
    load_query = pltpu.make_async_copy(w_query_ref, w_self_t, w_sem.at[0])
    load_keyval = pltpu.make_async_copy(w_keyval_ref, down_up.at[:, pl.ds(0, wide)], w_sem.at[1])
    load_self = pltpu.make_async_copy(w_self_ref, w_self, w_sem.at[2])
    load_out = pltpu.make_async_copy(w_out_ref, w_out, w_sem.at[3])
    load_qkv = pltpu.make_async_copy(w_qkv_ref, w_qkv, w_sem.at[4])
    load_up = pltpu.make_async_copy(w_up_ref, down_up, w_sem.at[5])
    load_down_again = pltpu.make_async_copy(w_down_ref, up_down, w_sem.at[6])
    load_up_again = pltpu.make_async_copy(w_up_ref, down_up, w_sem.at[7])

    def load_tokens(i):
        return pltpu.make_async_copy(tokens_ref.at[i], tokens.at[lax.rem(i, 2)], tok_sem.at[lax.rem(i, 2)])

    def load_down(part):
        return pltpu.make_async_copy(w_down_ref.at[pl.ds(part * rows, rows), :], tokens.at[part % 2], tok_sem.at[part % 2])

    def kv_at(i):
        return pl.ds(pl.multiple_of(lax.rem(i, 2) * wide, wide), wide)

    def save_kv(i):
        return pltpu.make_async_copy(act.at[kv_at(i), pl.ds(0, rows)], kv_out.at[i], kv_sem.at[lax.rem(i, 2)])

    def across(i, hop):
        return pltpu.make_async_remote_copy(
            src_ref=sent.at[i], dst_ref=(arrived if frames > 2 else got).at[hop - 1, i], send_sem=y_send.at[hop - 1, i], recv_sem=y_recv.at[hop - 1, i],
            device_id=(item, lax.rem(frame + hop, frames)), device_id_type=MESH,
        )

    load_tokens(0).start()
    load_query.start()
    load_keyval.start()
    load_tokens(1).start()
    for copy in (load_self, load_out, load_qkv):
        copy.start()

    latent_t = latent_ref[...].astype(jnp.float32).T
    query_normed, _ = norm_down(latent_t)
    query_in = (query_normed * gain_columns(query_gain_ref)).T.astype(jnp.bfloat16)
    tok_gain[...] = gain_columns(tok_gain_ref)
    mlp_gain[...] = gain_columns(mlp_gain_ref)
    self_gain[...] = gain_columns(self_gain_ref)
    load_query.wait()
    query = nn(query_in, w_self_t[...]).astype(jnp.bfloat16)
    query_out[...] = query
    scaled = query * jnp.bfloat16(factor)
    for h in range(HEADS):
        queries[h] = scaled[:, h * head : (h + 1) * head]
    load_keyval.wait()
    for block in range(wide // BLOCK):
        window = pl.ds(block * BLOCK, BLOCK)
        tall[window, :] = down_up[:, window].T
    load_up.start()
    pl.semaphore_wait(barrier, frames - 1)

    def heard_item(i):
        slot = lax.rem(i, 2)
        load_tokens(i).wait()

        def norm_block(b):
            window = window_at(b, LANES)
            normed, _ = norm_down(tokens[slot, window, :].T.astype(jnp.float32))
            tok_in[:, window] = (normed * tok_gain[...]).astype(jnp.bfloat16)

        loop(rows // LANES, norm_block)

        @pl.when(i + 2 < items)
        def _():
            load_tokens(i + 2).start()

        @pl.when(i >= 2)
        def _():
            save_kv(i - 2).wait()

        base = pl.multiple_of(slot * wide, wide)
        for block in range(wide // BLOCK):
            act[pl.ds(base + block * BLOCK, BLOCK), pl.ds(0, rows)] = nn(
                tall[pl.ds(block * BLOCK, BLOCK), :], tok_in[...]
            ).astype(jnp.bfloat16)
        save_kv(i).start()
        lane = lax.broadcasted_iota(jnp.int32, (latents, LANES), 1)
        stats = jnp.zeros((latents, LANES), jnp.float32)
        for h in range(HEADS):
            scores = nn(queries[h], act[pl.ds(base + h * head, head), pl.ds(0, rows)])
            most = jnp.max(scores, axis=-1, keepdims=True)
            shifted = jnp.exp(scores - most)
            total = jnp.sum(shifted, axis=-1, keepdims=True)
            stats = jnp.where(lane == h, most, stats)
            stats = jnp.where(lane == h + stat // 2, total, stats)
            sent[i, pl.ds(h * head, head), :] = nt(
                act[pl.ds(base + width + h * head, head), pl.ds(0, rows)], shifted.astype(jnp.bfloat16)
            )
        sent[i, pl.ds(width, stat), :] = stats.T[:stat]
        for hop in range(1, frames):
            across(i, hop).start()

    loop(items, heard_item)
    load_down(0).start()
    load_down(1).start()

    def turn(source, target, count):
        def block(b):
            window = window_at(b, BLOCK)
            target[window, :] = source[:, window].T

        loop(count // BLOCK, block)

    load_self.wait()

    def load_cotangent(i):
        cotangent[:, window_at(i, latents)] = grad_ref[i].T

    loop(items, load_cotangent)
    for block in range(width // BLOCK):
        window = pl.ds(block * BLOCK, BLOCK)
        d_mixed[window, :] = nn(w_self[window, :], cotangent[...]).astype(jnp.bfloat16)
    turn(w_self, w_self_t, width)
    load_out.wait()
    turn(w_out, w_out_t, width)
    load_up.wait()
    turn(down_up, up_down, hidden)
    for part in range(hidden // rows):
        load_down(part).wait()
        for block in range(rows // BLOCK):
            down_up[:, pl.ds(part * rows + block * BLOCK, BLOCK)] = tokens[part % 2, pl.ds(block * BLOCK, BLOCK), :].T
        if part + 2 < hidden // rows:
            load_down(part + 2).start()
    load_qkv.wait()
    turn(w_qkv, tall, 3 * width)
    for i in range(max(items - 2, 0), items):
        save_kv(i).wait()

    def combine(i):
        for hop in range(1, frames):
            across(i, hop).wait_send()
            across(i, hop).wait_recv()
            if frames > 2:
                near = pltpu.make_async_copy(arrived.at[hop - 1, i], got.at[hop - 1, 0], got_sem)
                near.start()
                near.wait()
        parts = [sent.at[i]] + [got.at[hop, 0 if frames > 2 else i] for hop in range(frames - 1)]
        highs = [part[pl.ds(width, stat // 2), :] for part in parts]
        sums = [part[pl.ds(width + stat // 2, stat // 2), :] for part in parts]
        most = functools.reduce(jnp.maximum, highs)
        total = functools.reduce(jnp.add, [low * jnp.exp(high - most) for high, low in zip(highs, sums)])
        log_total = most + jnp.log(total)
        scales = [jnp.exp(high - log_total) for high in highs]
        for h in range(HEADS):
            window = pl.ds(h * head, head)
            together = functools.reduce(
                jnp.add, [part[window, :] * scale[h : h + 1] for part, scale in zip(parts, scales)]
            )
            sent[i, window, :] = together
            heard[window, window_at(i, latents)] = together.astype(jnp.bfloat16)
        padded = jnp.concatenate([log_total, jnp.zeros((LANES - stat // 2, latents), jnp.float32)], axis=0)
        log_out[i] = padded.T

    def attend(i):
        window = window_at(i, latents)
        for first in range(0, HEADS, 4):
            at = [[pl.ds(third * width + h * head, head) for third in range(3)] for h in range(first, first + 4)]
            query = [triple[where[0], window] * jnp.bfloat16(factor) for where in at]
            key = [triple[where[1], window] for where in at]
            value = [triple[where[2], window] for where in at]
            d_mix = [d_mixed[where[0], window] for where in at]
            scores = [nn(k.T, q) for k, q in zip(key, query)]
            d_probs = [nn(v.T, d) for v, d in zip(value, d_mix)]
            shifted = [jnp.exp(s - jnp.max(s, axis=0, keepdims=True)) for s in scores]
            probs = [s * (1.0 / jnp.sum(s, axis=0, keepdims=True)) for s in shifted]
            low = [p.astype(jnp.bfloat16) for p in probs]
            mix = [nn(v, p) for v, p in zip(value, low)]
            delta = [jnp.sum(d.astype(jnp.float32) * m, axis=0, keepdims=True) for d, m in zip(d_mix, mix)]
            d_scores = [(p * (d - x)).astype(jnp.bfloat16) for p, d, x in zip(probs, d_probs, delta)]
            d_query = [nn(k, d) * factor for k, d in zip(key, d_scores)]
            d_key = [nt(q, d) for q, d in zip(query, d_scores)]
            d_value = [nt(d, p) for d, p in zip(d_mix, low)]
            for where, m, dq, dk, dv in zip(at, mix, d_query, d_key, d_value):
                mixed[where[0], window] = m.astype(jnp.bfloat16)
                d_triple[where[0], window] = dq.astype(jnp.bfloat16)
                d_triple[where[1], window] = dk.astype(jnp.bfloat16)
                d_triple[where[2], window] = dv.astype(jnp.bfloat16)

    def forward_group(group):
        size = items // groups
        first = group * size
        columns = pl.ds(first * latents, size * latents)

        def each_item(body):
            loop(size, lambda i: body(first + i))

        def each_block(count, body):
            loop(count // BLOCK, lambda b: body(window_at(b, BLOCK)))

        each_item(combine)

        def out_block(window):
            cross[window, columns] = nn(w_out_t[window, :], heard[:, columns])

        each_block(width, out_block)

        def cross_item(i):
            window = window_at(i, latents)
            keep = (1 - skip_ref[i]).astype(jnp.float32)
            total = latent_ref[...].astype(jnp.float32).T + keep * cross[:, window]
            cross[:, window] = total
            normed, _ = norm_down(total)
            mlp_in[:, window] = (normed * mlp_gain[...]).astype(jnp.bfloat16)

        each_item(cross_item)

        def up_block(window):
            value, bend = gelu_parts(nn(up_down[window, :], mlp_in[:, columns]))
            act[window, columns] = value.astype(jnp.bfloat16)
            slope[window, columns] = bend

        each_block(hidden, up_block)
        if group == groups - 1:
            load_down_again.start()

        def down_block(window):
            after[window, columns] = cross[window, columns] + nn(down_up[window, :], act[:, columns])

        each_block(width, down_block)
        if group == groups - 1:
            load_up_again.start()

        def after_item(i):
            window = window_at(i, latents)
            normed, _ = norm_down(after[:, window])
            self_in[:, window] = (normed * self_gain[...]).astype(jnp.bfloat16)

        each_item(after_item)

        def triple_block(window):
            triple[window, columns] = nn(tall[window, :], self_in[:, columns]).astype(jnp.bfloat16)

        each_block(3 * width, triple_block)
        each_item(attend)

    for group in range(groups):
        forward_group(group)

    def each_item(body):
        loop(items, lambda i: body(i, window_at(i, latents)))

    def each_block(count, body):
        loop(count // BLOCK, lambda b: body(window_at(b, BLOCK)))

    pending = {}

    def put(first_piece, count, offset, left, right):
        size = width // count
        slot = len(pending) % stage.shape[0]
        for key in [key for key in pending if key % stage.shape[0] == slot and pending[key] is not None]:
            pending[key].wait()
            pending[key] = None
        view = stage.at[slot]
        view[...] = nt(left[...], right[...])
        copy = pltpu.make_async_copy(
            view.reshape(count, size, own), mid_out.at[pl.ds(first_piece, count), pl.ds(offset, size)], stage_sem.at[slot]
        )
        copy.start()
        pending[len(pending)] = copy

    up_rows, down_rows = width // pieces, hidden // pieces
    first_up = up_rows
    first_down = first_up + up_rows * (hidden // width)
    first_qkv = first_down + down_rows
    first_self = first_qkv + 3 * up_rows
    my_columns = pl.multiple_of(frame * own, own)
    put(0, pieces, first_self, mixed, cotangent.at[pl.ds(my_columns, own), :])
    for third in range(3):
        put(0, pieces, first_qkv + third * up_rows, self_in, d_triple.at[pl.ds(3 * my_columns + third * own, own), :])

    def self_block(window):
        rows_f32[window, :] = nn(w_qkv[window, :], d_triple[...])

    each_block(width, self_block)
    gain_out[...] = jnp.zeros_like(gain_out)
    lane = lax.broadcasted_iota(jnp.int32, (width, LANES), 1)

    def self_back(i, window):
        normed, inverse = norm_down(after[:, window])
        incoming = rows_f32[:, window]
        gain_out[...] += jnp.where(lane == 1, jnp.sum(incoming * normed, axis=-1, keepdims=True), 0.0)
        d_after = cotangent[:, window].astype(jnp.float32) + norm_down_back(incoming, normed, inverse, self_gain[...])
        branch[:, window] = d_after.astype(jnp.bfloat16)
        rows_f32[:, window] = d_after

    each_item(self_back)

    def latents_block(window):
        after[window, :] = after[window, :] + nn(w_self_t[window, :], mixed[...])

    each_block(width, latents_block)
    share = latents // frames

    def latents_item(i, window):
        d_latent_out[...] = after[:, window].T
        latents_out[i] = d_latent_out[pl.ds(pl.multiple_of(frame * share, share), share), :].astype(jnp.bfloat16)

    each_item(latents_item)
    for group in range(hidden // width):
        count = pieces * width // hidden
        put(group * count, count, first_down, act.at[pl.ds(group * width, width), :], branch.at[pl.ds(my_columns, own), :])
    load_down_again.wait()

    def hidden_block(window):
        triple[window, :] = (nn(up_down[window, :], branch[...]) * slope[window, :]).astype(jnp.bfloat16)

    each_block(hidden, hidden_block)
    for part in range(hidden // width):
        put(0, pieces, first_up + part * up_rows, mlp_in, triple.at[pl.ds(frame * (hidden // frames) + part * own, own), :])
    load_up_again.wait()

    def mlp_block(window):
        after[window, :] = nn(down_up[window, :], triple[...])

    each_block(width, mlp_block)
    d_latent_out[...] = jnp.zeros_like(d_latent_out)

    def mlp_back(i, window):
        normed, inverse = norm_down(cross[:, window])
        incoming = after[:, window]
        gain_out[...] += jnp.where(lane == 0, jnp.sum(incoming * normed, axis=-1, keepdims=True), 0.0)
        d_cross = rows_f32[:, window] + norm_down_back(incoming, normed, inverse, mlp_gain[...])
        d_latent_out[...] += d_cross.T
        keep = (1 - skip_ref[i]).astype(jnp.float32)
        branch[:, window] = (keep * d_cross).astype(jnp.bfloat16)

    each_item(mlp_back)
    put(0, pieces, 0, heard, branch.at[pl.ds(my_columns, own), :])

    def heard_block(window):
        d_heard_out[window, :] = nn(w_out[window, :], branch[...]).astype(jnp.bfloat16)

    each_block(width, heard_block)

    def delta_item(i, window):
        product = d_heard_out[:, window].astype(jnp.float32) * sent[i, pl.ds(0, width), :]
        sums = jnp.sum(product.reshape(HEADS, head, latents), axis=1)
        padded = jnp.concatenate([sums, jnp.zeros((LANES - HEADS, latents), jnp.float32)], axis=0)
        delta_out[i] = padded.T

    each_item(delta_item)
    for copy in pending.values():
        if copy is not None:
            copy.wait()


def forward(
    frames, pieces, tokens, skip, latent_init, tok_gain, query_gain, mlp_gain, self_gain,
    w_query, w_keyval, w_out, w_up, w_down, w_self_qkv, w_self_out, grad_out,
):
    items, rows, width = tokens.shape
    latents = latent_init.shape[0]
    hidden = w_up.shape[1]
    own = width // frames
    columns = items * latents
    mid_rows = (5 * width + 2 * hidden) // pieces
    bf16, f32 = jnp.bfloat16, jnp.float32
    vmem = pl.BlockSpec(memory_space=pltpu.VMEM)
    anywhere = pl.BlockSpec(memory_space=pl.ANY)
    dma = pltpu.SemaphoreType.DMA
    peers = max(frames - 1, 1)
    return pl.pallas_call(
        functools.partial(forward_kernel, frames, 2 if items % 2 == 0 else 1),
        out_shape=(
            jax.ShapeDtypeStruct((items, 2 * width, rows), bf16),
            jax.ShapeDtypeStruct((items, latents, LANES), f32),
            jax.ShapeDtypeStruct((latents, width), bf16),
            jax.ShapeDtypeStruct((pieces, mid_rows, own), f32),
            jax.ShapeDtypeStruct((items, latents // frames, width), bf16),
            jax.ShapeDtypeStruct((width, columns), bf16),
            jax.ShapeDtypeStruct((items, latents, LANES), f32),
            jax.ShapeDtypeStruct((latents, width), f32),
            jax.ShapeDtypeStruct((width, LANES), f32),
            jax.ShapeDtypeStruct((peers, items if frames > 2 else 1, width + 32, latents), f32),
        ),
        in_specs=[anywhere, pl.BlockSpec(memory_space=pltpu.SMEM)] + [vmem] * 5 + [anywhere] * 7 + [vmem],
        out_specs=(anywhere, vmem, vmem, anywhere) + (vmem,) * 5 + (anywhere,),
        scratch_shapes=[
            pltpu.VMEM((2, rows, width), bf16),
            pltpu.VMEM((width, rows), bf16),
            pltpu.VMEM((HEADS, latents, width // HEADS), bf16),
            pltpu.VMEM((items, width + 32, latents), f32),
            pltpu.VMEM((peers, 1 if frames > 2 else items, width + 32, latents), f32),
        ]
        + [pltpu.VMEM((width, width), bf16)] * 4
        + [
            pltpu.VMEM((width, 3 * width), bf16),
            pltpu.VMEM((3 * width, width), bf16),
            pltpu.VMEM((hidden, width), bf16),
            pltpu.VMEM((width, hidden), bf16),
            pltpu.VMEM((width, columns), bf16),
            pltpu.VMEM((width, columns), f32),
            pltpu.VMEM((width, columns), bf16),
            pltpu.VMEM((hidden, max(columns, rows)), bf16),
            pltpu.VMEM((hidden, columns), f32),
            pltpu.VMEM((width, columns), f32),
            pltpu.VMEM((width, columns), bf16),
            pltpu.VMEM((hidden, columns), bf16),
            pltpu.VMEM((width, columns), bf16),
            pltpu.VMEM((width, columns), bf16),
            pltpu.VMEM((width, columns), bf16),
            pltpu.VMEM((3 * width, columns), bf16),
            pltpu.VMEM((width, columns), bf16),
            pltpu.VMEM((width, columns), f32),
            pltpu.VMEM((width, LANES), f32),
            pltpu.VMEM((width, LANES), f32),
            pltpu.VMEM((width, LANES), f32),
            pltpu.VMEM((2, width, own), f32),
            dma((2,)), dma((2,)), dma((peers, items)), dma((peers, items)), dma((8,)), dma((2,)), dma,
        ],
        compiler_params=pltpu.CompilerParams(collective_id=1, has_side_effects=True, vmem_limit_bytes=62 * 2**20),
        name="forward",
    )(
        tokens, skip, latent_init, tok_gain, query_gain, mlp_gain, self_gain,
        w_query, w_keyval, w_out, w_up, w_down, w_self_qkv, w_self_out, grad_out,
    )


def add_into(target, parts, rows):
    step = next(size for size in (104, 80, 64, 48, 40, 24, 16, 8) if rows % size == 0)

    def body(index, carry):
        window = pl.ds(pl.multiple_of(index * step, 8), step)
        total = parts[0][window]
        for part in parts[1:]:
            total = total + part[window]
        target[window] = total
        return carry

    lax.fori_loop(0, rows // step, body, 0)


def nn_exact(left, right):
    total = jnp.zeros((left.shape[0], right.shape[1]), jnp.float32)
    rest = right
    for _ in range(3):
        part = rest.astype(jnp.bfloat16)
        total = total + nn(left, part)
        rest = rest - part.astype(jnp.float32)
    return total


def backward_kernel(
    chips, frames, spans,
    mid_ref, tokens_ref, kv_ref, d_heard_ref, log_ref, delta_ref, query_ref,
    w_ref, gain_ref, latent_ref, qgain_ref, wq_ref, d_latent_ref, gains_ref,
    mid_out, kv_out, token_out,
    mine, sib, rx, kmine, ksib, ky, krx,
    tokens, kv, tok_in, d_kv, normed, incoming, queries, queries_t, d_query, gain_sum, tok_gain, token_stage,
    ld_sem, sib_send, sib_recv, rs_send, rs_recv, ag_send, ag_recv, share_send, share_recv, own_sem,
    ksib_send, ksib_recv, y_send, y_recv, krs_send, krs_recv, kag_send, kag_recv, kshare_send, kshare_recv,
    tok_sem, kv_sem, out_sem,
):
    items = lax.axis_index("items")
    frame = lax.axis_index("frames")
    core = lax.rem(items, 2)
    chip = items // 2
    column = lax.rem(chip, 2)
    line = chip // 2
    place = line + column * (chips - 1 - 2 * line)
    way = 1 - 2 * core
    count, rows, width = tokens_ref.shape
    latents = latent_ref.shape[0]
    head = width // HEADS
    factor = head ** -0.5
    own = width // frames
    kv_rows = krx.shape[1]

    def device_at(position):
        position = lax.rem(position + 2 * chips, chips)
        far = position // (chips // 2)
        return (2 * (position + far * (chips - 1 - 2 * position)) + far) * 2 + core

    right, left = device_at(place + way), device_at(place - way)
    sibling = items + way

    def chunk(offset):
        return lax.rem(place + way * offset + 2 * chips, chips)

    def sib_chunk(offset):
        return lax.rem(place - way * offset + 2 * chips, chips)

    barrier = pltpu.get_barrier_semaphore()
    for peer in (left, right, sibling):
        pl.semaphore_signal(barrier, inc=1, device_id=(peer, frame), device_id_type=MESH)
    for hop in range(1, frames):
        pl.semaphore_signal(barrier, inc=1, device_id=(items, lax.rem(frame + hop, frames)), device_id_type=MESH)

    def remote(src, dst, send, recv, peer):
        return pltpu.make_async_remote_copy(
            src_ref=src, dst_ref=dst, send_sem=send, recv_sem=recv, device_id=peer, device_id_type=MESH
        )

    def load(k):
        return pltpu.make_async_copy(mid_ref.at[core, k], mine.at[k], ld_sem.at[k])

    def pair(k):
        return remote(mid_ref.at[1 - core, k], sib.at[k], sib_send.at[k], sib_recv.at[k], (sibling, frame))

    def ring(j, k):
        part = pl.ds(*spans[j])
        return remote(mine.at[k, part], rx.at[k, part], rs_send.at[j, k], rs_recv.at[j, k], (right, frame))

    def gather(j, k, source):
        part = pl.ds(*spans[j])
        return remote(source.at[k, part], mid_out.at[core, k, part], ag_send.at[j, k], ag_recv.at[j, k], (right, frame))

    def share(j, k, source):
        part = pl.ds(*spans[j])
        return remote(source.at[k, part], mid_out.at[core, k, part], share_send.at[j, k], share_recv.at[j, k], (sibling, frame))

    def share_from(j, k):
        part = pl.ds(*spans[j])
        return remote(mine.at[k, part], mid_out.at[1 - core, k, part], share_send.at[j, k], share_recv.at[j, k], (sibling, frame))

    def keep(j, k):
        part = pl.ds(*spans[j])
        return pltpu.make_async_copy(mine.at[k, part], mid_out.at[core, k, part], own_sem.at[j])

    def kpair():
        return remote(kmine.at[:, 1 - core], ksib, ksib_send, ksib_recv, (sibling, frame))

    def across(hop, k):
        other = lax.rem(frame + hop, frames)
        return remote(kmine.at[other, core, k], ky.at[hop - 1, k], y_send.at[hop - 1, k], y_recv.at[hop - 1, k], (items, other))

    def kring(k):
        return remote(kmine.at[frame, core, k], krx.at[k], krs_send.at[k], krs_recv.at[k], (right, frame))

    def kgather(k, source):
        return remote(source, kv_out.at[core, k], kag_send.at[k], kag_recv.at[k], (right, frame))

    def kshare(k, source):
        return remote(source, kv_out.at[core, k], kshare_send.at[k], kshare_recv.at[k], (sibling, frame))

    def kshare_from(k):
        return remote(kmine.at[frame, core, k], kv_out.at[1 - core, k], kshare_send.at[k], kshare_recv.at[k], (sibling, frame))

    def kkeep(k):
        return pltpu.make_async_copy(kmine.at[frame, core, k], kv_out.at[core, k], own_sem.at[len(spans)])

    def rs_tick(step, j, first=False):
        k = chunk(-step)
        if j == 0:
            load(k).wait()
            pair(k).wait_recv()
        start, size = spans[j]
        part = pl.ds(start, size)
        parts = [mine.at[k, part], sib.at[k, part]]
        if not first:
            ring(j, k).wait_recv()
            parts.append(rx.at[k, part])
        add_into(mine.at[k, part], parts, size)

    def rs_send_on(step, j):
        ring(j, chunk(-step)).start()

    def rs_step(step, j, first=False):
        rs_tick(step, j, first)
        rs_send_on(step, j)

    def rs_last(j):
        k = chunk(1)
        rs_tick(chips - 1, j)
        gather(j, k, mine).start()
        share(j, k, mine).start()
        keep(j, k).start()

    def ag_step(step, j):
        k = chunk(1 - step)
        gather(j, k, mine).wait_recv()
        if step < chips - 1:
            gather(j, k, mid_out.at[core]).start()
        share(j, k, mid_out.at[core]).start()

    def k_step(step):
        k = chunk(-step)
        if step < chips:
            parts = [kmine.at[frame, core, k], ksib.at[frame, k]]
            for hop in range(1, frames):
                across(hop, k).wait_recv()
                parts.append(ky.at[hop - 1, k])
            if step > 0:
                kring(k).wait_recv()
                parts.append(krx.at[k])
            add_into(kmine.at[frame, core, k], parts, kv_rows)
            if step < chips - 1:
                kring(k).start()
            else:
                kgather(k, kmine.at[frame, core, k]).start()
                kshare(k, kmine.at[frame, core, k]).start()
                kkeep(k).start()
        else:
            kgather(k, kmine.at[frame, core, k]).wait_recv()
            if step < 2 * chips - 2:
                kgather(k, kv_out.at[core, k]).start()
            kshare(k, kv_out.at[core, k]).start()

    def across_step(step):
        k = chunk(-step)
        for hop in range(1, frames):
            other = lax.rem(frame + hop, frames)
            add_into(kmine.at[other, core, k], [kmine.at[other, core, k], ksib.at[other, k]], kv_rows)
            across(hop, k).start()

    def tok_load(i):
        return pltpu.make_async_copy(tokens_ref.at[i], tokens.at[lax.rem(i, 2)], tok_sem.at[lax.rem(i, 2)])

    def kv_load(i):
        return pltpu.make_async_copy(kv_ref.at[i], kv.at[lax.rem(i, 2)], kv_sem.at[lax.rem(i, 2)])

    def token_save(i, b):
        slot = lax.rem(b, 2)
        return pltpu.make_async_copy(
            token_stage.at[slot], token_out.at[i, pl.ds(pl.multiple_of(b * LANES, LANES), LANES), :], out_sem.at[slot]
        )

    def start_stage(index, carry):
        pair(sib_chunk(-index)).start()
        load(chunk(-index)).start()
        return carry

    tok_load(0).start()
    kv_load(0).start()
    query = query_ref[...]
    scaled = query * jnp.bfloat16(factor)
    for h in range(HEADS):
        queries[h] = scaled[:, h * head : (h + 1) * head]
    queries_t[...] = scaled.T
    tok_gain[...] = gain_columns(gain_ref)
    d_query[...] = jnp.zeros_like(d_query)
    gain_sum[...] = jnp.zeros_like(gain_sum)
    pl.semaphore_wait(barrier, 3 + frames - 1)
    lax.fori_loop(0, chips, start_stage, 0)

    def attend(i, heads):
        slot = lax.rem(i, 2)
        columns = pl.ds(pl.multiple_of(i * rows, rows), rows)
        latent_window = pl.ds(pl.multiple_of(i * latents, latents), latents)
        for h in heads:
            keys_at, values_at = pl.ds(h * head, head), pl.ds(width + h * head, head)
            keys, values = kv[slot, keys_at, :], kv[slot, values_at, :]
            d_heard_t = d_heard_ref[keys_at, latent_window]
            probs = jnp.exp(nn(queries[h], keys) - log_ref[i, :, h : h + 1])
            d_probs = nn(d_heard_t.T, values)
            d_scores = (probs * (d_probs - delta_ref[i, :, h : h + 1])).astype(jnp.bfloat16)
            d_kv[keys_at, columns] = nn(queries_t[keys_at, :], d_scores).astype(jnp.bfloat16)
            d_kv[values_at, columns] = nn(d_heard_t, probs.astype(jnp.bfloat16)).astype(jnp.bfloat16)
            d_query[keys_at, :] += nt(keys, d_scores)

    def norm_tokens(i):
        tok_load(i).wait()

        def norm_block(b, carry):
            window = pl.ds(pl.multiple_of(b * LANES, LANES), LANES)
            columns = tokens[lax.rem(i, 2), window, :].T.astype(jnp.float32)
            block, inverse = norm_down(columns)
            normed[pl.ds(0, width), window] = block
            normed[pl.ds(width, 8), window] = jnp.broadcast_to(inverse, (8, LANES))
            tok_in[:, pl.ds(pl.multiple_of(i * rows + b * LANES, LANES), LANES)] = (block * tok_gain[...]).astype(jnp.bfloat16)
            return carry

        lax.fori_loop(0, rows // LANES, norm_block, 0)

    def token_back(i):
        columns = pl.ds(pl.multiple_of(i * rows, rows), rows)

        def product(b, carry):
            window = pl.ds(pl.multiple_of(b * BLOCK, BLOCK), BLOCK)
            incoming[window, :] = nn(w_ref[window, :], d_kv[:, columns])
            return carry

        lax.fori_loop(0, width // BLOCK, product, 0)

        def back_block(b, carry):
            window = pl.ds(pl.multiple_of(b * LANES, LANES), LANES)
            block = normed[pl.ds(0, width), window]
            arriving = incoming[:, window]
            gain_sum[...] += arriving * block
            result = norm_down_back(arriving, block, normed[pl.ds(width, 1), window], tok_gain[...])

            @pl.when((i > 0) | (b > 1))
            def _():
                token_save(i, b).wait()

            token_stage[lax.rem(b, 2)] = result.T.astype(jnp.bfloat16)
            token_save(i, b).start()
            return carry

        lax.fori_loop(0, rows // LANES, back_block, 0)

    for j in range(len(spans)):
        rs_step(0, j, True)

    def one_item(i, carry):
        kv_load(i).wait()

        @pl.when(i + 1 < count)
        def _():
            kv_load(i + 1).start()
            tok_load(i + 1).start()

        norm_tokens(i)
        attend(i, range(HEADS // 2))
        rs_step(i + 1, 0)
        attend(i, range(HEADS // 2, HEADS))
        token_back(i)
        for j in range(1, len(spans)):
            rs_step(i + 1, j)
        return carry

    lax.fori_loop(0, count, one_item, 0)

    per_piece = width // (2 * chips)
    small = 2 * latents // (2 * chips)
    d_query[...] = d_query[...] * factor
    q_total = d_query[...]
    q_normed, q_inverse = norm_down(latent_ref[...].astype(jnp.float32).T)
    q_incoming = nn_exact(wq_ref[...], q_total)
    lane = lax.broadcasted_iota(jnp.int32, (width, LANES), 1)
    all_gains = gains_ref[...]
    all_gains = jnp.where(lane == 2, jnp.sum(gain_sum[...], axis=-1, keepdims=True), all_gains)
    all_gains = jnp.where(lane == 3, jnp.sum(q_incoming * q_normed, axis=-1, keepdims=True), all_gains)
    gain_rows = all_gains.T[:8]
    latent_rows = norm_down_back(q_incoming, q_normed, q_inverse, gain_columns(qgain_ref)).T
    query_rows = q_total.T
    for f in range(frames):
        mask = (frame == f).astype(jnp.float32)
        mine_columns = slice(f * own, (f + 1) * own)
        latent_part = latent_rows[:, mine_columns] + mask * d_latent_ref[:, mine_columns]
        both = jnp.concatenate([query_rows[:, mine_columns], latent_part], axis=0)
        kmine[f, :, :, pl.ds(2 * per_piece, small), :] = both.reshape(2, chips, small, own)
        row = lax.broadcasted_iota(jnp.int32, (8, own), 0)
        gain_block = gain_rows[:, mine_columns] * jnp.where(row < 2, mask, 1.0)
        kmine[f, :, :, pl.ds(2 * per_piece + small, 8), :] = jnp.zeros((2, chips, 8, own), jnp.float32)
        kmine[f, 0, 0, pl.ds(2 * per_piece + small, 8), :] = gain_block

    def keyval_block(f, b):
        source = d_kv.at[pl.ds((2 * f + b) * own, own), :]
        size = width // 2
        for start in range(0, width, size):
            block = nt(tok_in[pl.ds(start, size), :], source[...])
            for piece in range(size // per_piece):
                at = start // per_piece + piece
                kmine[f, at // chips, at % chips, pl.ds(b * per_piece, per_piece), :] = block[piece * per_piece : (piece + 1) * per_piece]

    done = count + 1
    blocks = [(f, b) for f in range(frames) for b in range(2)]
    for index, (f, b) in enumerate(blocks):
        keyval_block(f, b)
        if index % 2 == 1 and index + 1 < len(blocks) and done < chips - 1:
            rs_step(done, 0)
            for j in range(1, len(spans)):
                rs_step(done, j)
            done += 1
    kpair().start()
    for step in range(done, chips - 1):
        rs_step(step, 0)
        if step == done:
            kpair().wait_recv()
            for order in range(chips):
                across_step(order)
        for j in range(1, len(spans)):
            rs_step(step, j)
    for j in range(len(spans)):
        rs_last(j)
    kdone = 0
    for step in range(1, chips):
        for j in range(len(spans)):
            ag_step(step, j)
            if kdone < 2 * chips - 1:
                k_step(kdone)
                kdone += 1
    for step in range(kdone, 2 * chips - 1):
        k_step(step)

    def drain(k, carry):
        pair(k).wait_send()
        for j in range(len(spans)):
            share(j, k, mine).wait_send()
            share_from(j, k).wait_recv()
        kshare(k, kmine.at[frame, core, k]).wait_send()
        kshare_from(k).wait_recv()
        for hop in range(1, frames):
            across(hop, k).wait_send()
        return carry

    lax.fori_loop(0, chips, drain, 0)

    def drain_ring(step, carry):
        for j in range(len(spans)):
            ring(j, chunk(-step)).wait_send()
            gather(j, chunk(1 - step), mine).wait_send()
        kring(chunk(-step)).wait_send()
        kgather(chunk(1 - step), kmine.at[frame, core, 0]).wait_send()
        return carry

    lax.fori_loop(0, chips - 1, drain_ring, 0)
    kpair().wait_send()
    for j in range(len(spans)):
        keep(j, chunk(1)).wait()
    kkeep(chunk(1)).wait()
    for b in range(2):
        token_save(0, b).wait()


def backward(frames, mid, tokens, kv, d_heard, log_total, delta, query, w_keyval, tok_gain, latent_init, query_gain, w_query, d_latent, gains):
    chips, mid_rows, own = mid.shape[1:]
    items, rows, width = tokens.shape
    latents = latent_init.shape[0]
    kv_rows = 2 * width // (2 * chips) + 2 * latents // (2 * chips) + 8
    step = mid_rows // 8 // STREAMS * 8
    spans = tuple((j * step, step if j + 1 < STREAMS else mid_rows - j * step) for j in range(STREAMS))
    dma = pltpu.SemaphoreType.DMA
    peers = max(frames - 1, 1)
    n = len(spans)
    f32, bf16 = jnp.float32, jnp.bfloat16
    vmem = pl.BlockSpec(memory_space=pltpu.VMEM)
    anywhere = pl.BlockSpec(memory_space=pl.ANY)
    scratch = [
        pltpu.VMEM((chips, mid_rows, own), f32), pltpu.VMEM((chips, mid_rows, own), f32), pltpu.VMEM((chips, mid_rows, own), f32),
        pltpu.VMEM((frames, 2, chips, kv_rows, own), f32), pltpu.VMEM((frames, chips, kv_rows, own), f32),
        pltpu.VMEM((peers, chips, kv_rows, own), f32), pltpu.VMEM((chips, kv_rows, own), f32),
        pltpu.VMEM((2, rows, width), bf16),
        pltpu.VMEM((2, 2 * width, rows), bf16),
        pltpu.VMEM((width, items * rows), bf16),
        pltpu.VMEM((2 * width, items * rows), bf16),
        pltpu.VMEM((width + 8, rows), f32),
        pltpu.VMEM((width, rows), f32),
        pltpu.VMEM((HEADS, latents, width // HEADS), bf16),
        pltpu.VMEM((width, latents), bf16),
        pltpu.VMEM((width, latents), f32),
        pltpu.VMEM((width, LANES), f32),
        pltpu.VMEM((width, LANES), f32),
        pltpu.VMEM((2, LANES, width), bf16),
        dma((chips,)), dma((chips,)), dma((chips,)),
        dma((n, chips)), dma((n, chips)), dma((n, chips)), dma((n, chips)), dma((n, chips)), dma((n, chips)), dma((n + 1,)),
        dma, dma,
        dma((peers, chips)), dma((peers, chips)),
        dma((chips,)), dma((chips,)), dma((chips,)), dma((chips,)), dma((chips,)), dma((chips,)),
        dma((2,)), dma((2,)), dma((2,)),
    ]
    return pl.pallas_call(
        functools.partial(backward_kernel, chips, frames, spans),
        out_shape=(
            jax.ShapeDtypeStruct(mid.shape, f32),
            jax.ShapeDtypeStruct((2, chips, kv_rows, own), f32),
            jax.ShapeDtypeStruct(tokens.shape, bf16),
        ),
        in_specs=[anywhere] * 3 + [vmem] * 11,
        out_specs=(anywhere,) * 3,
        scratch_shapes=scratch,
        compiler_params=pltpu.CompilerParams(collective_id=0, has_side_effects=True, vmem_limit_bytes=62 * 2**20),
        name="backward",
    )(
        mid, tokens, kv, d_heard, log_total, delta, query, w_keyval, tok_gain, latent_init,
        query_gain, w_query, d_latent, gains,
    )


def unpack_kernel(mid_ref, kv_ref, latent_ref, qgain_ref, *rest):
    outs, (query_out, *gain_outs), (blocks, total, tail, in_sem, out_sem) = rest[:7], rest[7:12], rest[12:]
    pieces, _, own = mid_ref.shape
    loads, stores = [], []

    def place(source, offset, out):
        rows, columns = out.shape
        size = rows // pieces
        view = out.reshape(pieces, size, columns)
        for b in range(columns // own):
            at = len(loads)
            area = blocks.at[pl.ds(starts[at], pieces * size), :].reshape(pieces, size, own)
            loads.append(pltpu.make_async_copy(source.at[:, pl.ds(offset + b * size, size), :], area, in_sem.at[at]))
            stores.append(pltpu.make_async_copy(area, view.at[:, :, pl.ds(b * own, own)], out_sem.at[at]))
        return offset + size * columns // own

    starts, start = [], 0
    for out in outs[:6]:
        rows, columns = out.shape
        for b in range(columns // own):
            starts.append(start)
            start += rows
    offset = 0
    for out in outs[:5]:
        offset = place(mid_ref, offset, out)
    offset = place(kv_ref, 0, outs[5])
    latents = outs[6].shape[0]
    small = 2 * latents // pieces
    half = pieces // 2
    query = pltpu.make_async_copy(kv_ref.at[:, pl.ds(offset, small), :], total, in_sem.at[len(loads)])
    gains = pltpu.make_async_copy(kv_ref.at[0, pl.ds(offset + small, 8), :], tail, in_sem.at[len(loads) + 1])
    query.start()
    gains.start()
    for copy in loads:
        copy.start()
    normed, _ = norm_down(latent_ref[...].astype(jnp.float32).T)
    query_in = (normed * gain_columns(qgain_ref)).astype(jnp.bfloat16)
    query.wait()
    query_out[...] = nn_exact(query_in, total[pl.ds(0, half)].reshape(latents, own))
    outs[6][...] = total[pl.ds(half, half)].reshape(latents, own)
    gains.wait()
    for out, row in zip(gain_outs, (2, 3, 0, 1)):
        out[...] = tail[row]
    for load, store in zip(loads, stores):
        load.wait()
        store.start()
    for store in stores:
        store.wait()


def unpack_all(mid, kv, latent_init, query_gain, shapes):
    f32 = jnp.float32
    own = mid.shape[-1]
    latents, width = latent_init.shape
    pieces = mid.shape[0]
    vmem = pl.BlockSpec(memory_space=pltpu.VMEM)
    anywhere = pl.BlockSpec(memory_space=pl.ANY)
    count = sum(columns // own for _, columns in shapes)
    size = sum(rows * columns // own for rows, columns in shapes)
    return pl.pallas_call(
        unpack_kernel,
        out_shape=tuple(jax.ShapeDtypeStruct(shape, f32) for shape in shapes) + (
            jax.ShapeDtypeStruct((latents, own), f32), jax.ShapeDtypeStruct((width, own), f32))
        + (jax.ShapeDtypeStruct((own,), f32),) * 4,
        in_specs=[anywhere] * 2 + [vmem] * 2,
        out_specs=(anywhere,) * len(shapes) + (vmem,) * 6,
        scratch_shapes=[
            pltpu.VMEM((size, own), f32), pltpu.VMEM((pieces, 2 * latents // pieces, own), f32), pltpu.VMEM((8, own), f32),
            pltpu.SemaphoreType.DMA((count + 2,)), pltpu.SemaphoreType.DMA((count,)),
        ],
        compiler_params=pltpu.CompilerParams(vmem_limit_bytes=60 * 2**20),
        name="unpack_all",
    )(mid, kv, latent_init, query_gain)


def unpack(packed, rows, columns):
    pieces, _, width = packed.shape
    split = packed.reshape(pieces, columns // width, rows // pieces, width)
    return jnp.swapaxes(split, 1, 2).reshape(rows, columns)


def cut(packed, shapes):
    start, out = 0, []
    for rows, columns in shapes:
        count = rows * columns // packed.shape[-1] // packed.shape[0]
        out.append(unpack(packed[:, start : start + count], rows, columns))
        start += count
    return out


def shards(
    tokens,
    skip,
    latent_init,
    tok_gain,
    query_gain,
    mlp_gain,
    self_gain,
    w_query,
    w_keyval,
    w_out,
    w_up,
    w_down,
    w_self_qkv,
    w_self_out,
    grad_out,
):
    frames, pieces = lax.axis_size("frames"), lax.axis_size("items")
    latents, width = latent_init.shape
    hidden = w_up.shape[1]
    own = width // frames
    kv, log_total, query, mid, out_latents, d_heard, delta, d_latent, gains, _ = forward(
        frames, pieces, tokens, skip, latent_init, tok_gain, query_gain, mlp_gain, self_gain,
        w_query, w_keyval, w_out, w_up, w_down, w_self_qkv, w_self_out, grad_out,
    )
    mid_sum, kv_sum, token_grad = backward(
        frames, mid.reshape(2, pieces // 2, mid.shape[1], own), tokens, kv, d_heard, log_total, delta, query,
        w_keyval, tok_gain, latent_init, query_gain, w_query, d_latent, gains,
    )
    mid_sum = mid_sum.reshape(mid.shape)
    kv_sum = kv_sum.reshape((pieces,) + kv_sum.shape[2:])
    shapes = (
        (width, own),
        (width, hidden // frames),
        (hidden, own),
        (width, 3 * own),
        (width, own),
        (width, 2 * own),
    )
    if own % LANES == 0:
        *sums, latent_grad, grad_query, gain_tok, gain_query, gain_mlp, gain_self = unpack_all(
            mid_sum, kv_sum, latent_init, query_gain, shapes
        )
    else:
        sums = cut(mid_sum, shapes[:5])
        keyval_sum, small = cut(kv_sum, (shapes[5], (2 * latents, own)))
        sums.append(keyval_sum)
        latent_grad = small[latents:]
        normed, _ = norm_down(latent_init.astype(jnp.float32).T)
        query_in = (normed * query_gain[:, None]).astype(jnp.bfloat16)
        grad_query = jnp.dot(query_in.astype(jnp.float32), small[:latents], precision=lax.Precision.HIGHEST)
        gain_mlp, gain_self, gain_tok, gain_query = [kv_sum[0, row - 8] for row in range(4)]
    return (
        out_latents,
        token_grad,
        latent_grad,
        gain_tok,
        gain_query,
        gain_mlp,
        gain_self,
        grad_query,
        sums[5],
        sums[0],
        sums[1],
        sums[2],
        sums[3],
        sums[4],
    )


def solution(mesh):
    in_specs = (
        P("items", "frames", None),
        P("items"),
        P(),
        P(),
        P(),
        P(),
        P(),
        P(),
        P(),
        P(),
        P(),
        P(),
        P(),
        P(),
        P("items", None, None),
    )
    out_specs = (
        P("items", "frames", None),
        P("items", "frames", None),
        P(None, "frames"),
        P("frames"),
        P("frames"),
        P("frames"),
        P("frames"),
        P(None, "frames"),
        P(None, "frames"),
        P(None, "frames"),
        P(None, "frames"),
        P(None, "frames"),
        P(None, "frames"),
        P(None, "frames"),
    )
    return jax.shard_map(shards, mesh=mesh, in_specs=in_specs, out_specs=out_specs, check_vma=False)
```

```python
import functools

import jax
import jax.numpy as jnp
from jax import lax
from jax.experimental import pallas as pl
from jax.experimental.pallas import tpu as pltpu
from jax.sharding import PartitionSpec as P

MESH = pl.DeviceIdType.MESH
HEADS = 12
EPSILON = 1e-05
LANES = 128
BLOCK = 256


def nn(left, right):
    return lax.dot_general(left, right, (((1,), (0,)), ((), ())), preferred_element_type=jnp.float32)


def nt(left, right):
    return lax.dot_general(left, right, (((1,), (1,)), ((), ())), preferred_element_type=jnp.float32)


def norm_down(columns):
    centered = columns - jnp.mean(columns, axis=0, keepdims=True)
    inverse = lax.rsqrt(jnp.mean(centered * centered, axis=0, keepdims=True) + EPSILON)
    return centered * inverse, inverse


def gelu(value):
    slope = (2 / jnp.pi) ** 0.5
    tanh = jnp.tanh(value * (slope + (slope * 0.044715) * (value * value)))
    return value * (0.5 + 0.5 * tanh)


def norm_down_back(incoming, normed, inverse, gain):
    scaled = incoming * gain
    average = jnp.mean(scaled, axis=0, keepdims=True)
    along = jnp.mean(scaled * normed, axis=0, keepdims=True)
    return inverse * (scaled - average - normed * along)


def gain_columns(gain_ref):
    return jnp.broadcast_to(gain_ref[...].reshape(1, -1), (LANES, gain_ref.shape[0])).T


def loop(count, body):
    def step(index, carry):
        body(index)
        return carry

    lax.fori_loop(0, count, step, 0)


def window_at(index, size):
    return pl.ds(pl.multiple_of(index * size, size), size)


def forward_kernel(
    frames, groups,
    tokens_ref, skip_ref, latent_ref, tok_gain_ref, query_gain_ref, mlp_gain_ref, self_gain_ref,
    w_query_ref, w_keyval_ref, w_out_ref, w_up_ref, w_down_ref, w_qkv_ref, w_self_ref, grad_ref,
    kv_out, log_out, query_out, mid_out, latents_out, act_out, hidden_out, mlp_out, cross_out, after_out, cot_out, heard_out,
    heard_f32_out, d_triple_out, arrived,
    tokens, tok_in, queries, sent, got,
    w_out, w_out_t, w_self, w_self_t, w_qkv, tall, up_down, down_up,
    heard, cross, mlp_in, act, hidden_rows, after, self_in, triple, mixed, cotangent, d_mixed, d_triple, heard_f32, turned,
    tok_gain, mlp_gain, self_gain, stage,
    tok_sem, kv_sem, y_send, y_recv, w_sem, stage_sem, got_sem, save_sem,
):
    items, rows, width = tokens_ref.shape
    latents = latent_ref.shape[0]
    hidden = w_up_ref.shape[1]
    head = width // HEADS
    factor = head ** -0.5
    own = width // frames
    stat = sent.shape[1] - width
    pieces = mid_out.shape[0]
    item = lax.axis_index("items")
    frame = lax.axis_index("frames")

    barrier = pltpu.get_barrier_semaphore()
    for hop in range(1, frames):
        pl.semaphore_signal(barrier, inc=1, device_id=(item, lax.rem(frame + hop, frames)), device_id_type=MESH)

    wide = 2 * width
    load_query = pltpu.make_async_copy(w_query_ref, w_self_t, w_sem.at[0])
    load_keyval = pltpu.make_async_copy(w_keyval_ref, down_up.at[:, pl.ds(0, wide)], w_sem.at[1])
    load_self = pltpu.make_async_copy(w_self_ref, w_self, w_sem.at[2])
    load_out = pltpu.make_async_copy(w_out_ref, w_out, w_sem.at[3])
    load_qkv = pltpu.make_async_copy(w_qkv_ref, w_qkv, w_sem.at[4])
    load_up = pltpu.make_async_copy(w_up_ref, down_up, w_sem.at[5])

    def load_tokens(i):
        return pltpu.make_async_copy(tokens_ref.at[i], tokens.at[lax.rem(i, 2)], tok_sem.at[lax.rem(i, 2)])

    def load_down(part):
        return pltpu.make_async_copy(w_down_ref.at[pl.ds(part * rows, rows), :], tokens.at[part % 2], tok_sem.at[part % 2])

    def kv_at(i):
        return pl.ds(pl.multiple_of(lax.rem(i, 2) * wide, wide), wide)

    def save_kv(i):
        return pltpu.make_async_copy(act.at[kv_at(i), pl.ds(0, rows)], kv_out.at[i], kv_sem.at[lax.rem(i, 2)])

    def across(i, hop):
        return pltpu.make_async_remote_copy(
            src_ref=sent.at[i], dst_ref=(arrived if frames > 2 else got).at[hop - 1, i], send_sem=y_send.at[hop - 1, i], recv_sem=y_recv.at[hop - 1, i],
            device_id=(item, lax.rem(frame + hop, frames)), device_id_type=MESH,
        )

    load_tokens(0).start()
    load_query.start()
    load_keyval.start()
    load_tokens(1).start()
    for copy in (load_self, load_out, load_qkv):
        copy.start()

    latent_t = latent_ref[...].astype(jnp.float32).T
    query_normed, _ = norm_down(latent_t)
    query_in = (query_normed * gain_columns(query_gain_ref)).T.astype(jnp.bfloat16)
    tok_gain[...] = gain_columns(tok_gain_ref)
    mlp_gain[...] = gain_columns(mlp_gain_ref)
    self_gain[...] = gain_columns(self_gain_ref)
    load_query.wait()
    query = nn(query_in, w_self_t[...]).astype(jnp.bfloat16)
    query_out[...] = query
    scaled = query * jnp.bfloat16(factor)
    for h in range(HEADS):
        queries[h] = scaled[:, h * head : (h + 1) * head]
    load_keyval.wait()
    for block in range(wide // BLOCK):
        window = pl.ds(block * BLOCK, BLOCK)
        tall[window, :] = down_up[:, window].T
    load_up.start()
    pl.semaphore_wait(barrier, frames - 1)

    def heard_item(i):
        slot = lax.rem(i, 2)
        load_tokens(i).wait()

        def norm_block(b):
            window = window_at(b, LANES)
            normed, _ = norm_down(tokens[slot, window, :].T.astype(jnp.float32))
            tok_in[:, window] = (normed * tok_gain[...]).astype(jnp.bfloat16)

        loop(rows // LANES, norm_block)

        @pl.when(i + 2 < items)
        def _():
            load_tokens(i + 2).start()

        @pl.when(i >= 2)
        def _():
            save_kv(i - 2).wait()

        base = pl.multiple_of(slot * wide, wide)
        for block in range(wide // BLOCK):
            act[pl.ds(base + block * BLOCK, BLOCK), pl.ds(0, rows)] = nn(
                tall[pl.ds(block * BLOCK, BLOCK), :], tok_in[...]
            ).astype(jnp.bfloat16)
        save_kv(i).start()
        lane = lax.broadcasted_iota(jnp.int32, (latents, LANES), 1)
        stats = jnp.zeros((latents, LANES), jnp.float32)
        for h in range(HEADS):
            scores = nn(queries[h], act[pl.ds(base + h * head, head), pl.ds(0, rows)])
            most = jnp.max(scores, axis=-1, keepdims=True)
            shifted = jnp.exp(scores - most)
            total = jnp.sum(shifted, axis=-1, keepdims=True)
            stats = jnp.where(lane == h, most, stats)
            stats = jnp.where(lane == h + stat // 2, total, stats)
            sent[i, pl.ds(h * head, head), :] = nt(
                act[pl.ds(base + width + h * head, head), pl.ds(0, rows)], shifted.astype(jnp.bfloat16)
            )
        sent[i, pl.ds(width, stat), :] = stats.T[:stat]
        for hop in range(1, frames):
            across(i, hop).start()

    loop(items, heard_item)
    load_down(0).start()
    load_down(1).start()

    def turn(source, target, count):
        def block(b):
            window = window_at(b, BLOCK)
            target[window, :] = source[:, window].T

        loop(count // BLOCK, block)

    load_self.wait()

    def load_cotangent(i):
        cotangent[:, window_at(i, latents)] = grad_ref[i].T

    loop(items, load_cotangent)
    for block in range(width // BLOCK):
        window = pl.ds(block * BLOCK, BLOCK)
        d_mixed[window, :] = nn(w_self[window, :], cotangent[...]).astype(jnp.bfloat16)
    turn(w_self, w_self_t, width)
    load_out.wait()
    turn(w_out, w_out_t, width)
    load_up.wait()
    turn(down_up, up_down, hidden)
    for part in range(hidden // rows):
        load_down(part).wait()
        for block in range(rows // BLOCK):
            down_up[:, pl.ds(part * rows + block * BLOCK, BLOCK)] = tokens[part % 2, pl.ds(block * BLOCK, BLOCK), :].T
        if part + 2 < hidden // rows:
            load_down(part + 2).start()
    load_qkv.wait()
    turn(w_qkv, tall, 3 * width)
    for i in range(max(items - 2, 0), items):
        save_kv(i).wait()

    def combine(i):
        for hop in range(1, frames):
            across(i, hop).wait_send()
            across(i, hop).wait_recv()
            if frames > 2:
                near = pltpu.make_async_copy(arrived.at[hop - 1, i], got.at[hop - 1, 0], got_sem)
                near.start()
                near.wait()
        parts = [sent.at[i]] + [got.at[hop, 0 if frames > 2 else i] for hop in range(frames - 1)]
        highs = [part[pl.ds(width, stat // 2), :] for part in parts]
        sums = [part[pl.ds(width + stat // 2, stat // 2), :] for part in parts]
        most = functools.reduce(jnp.maximum, highs)
        total = functools.reduce(jnp.add, [low * jnp.exp(high - most) for high, low in zip(highs, sums)])
        log_total = most + jnp.log(total)
        scales = [jnp.exp(high - log_total) for high in highs]
        for h in range(HEADS):
            window = pl.ds(h * head, head)
            together = functools.reduce(
                jnp.add, [part[window, :] * scale[h : h + 1] for part, scale in zip(parts, scales)]
            )
            heard_f32[window, window_at(i, latents)] = together
            heard[window, window_at(i, latents)] = together.astype(jnp.bfloat16)
        padded = jnp.concatenate([log_total, jnp.zeros((LANES - stat // 2, latents), jnp.float32)], axis=0)
        log_out[i] = padded.T

    def attend(i):
        window = window_at(i, latents)
        for first in range(0, HEADS, 4):
            at = [[pl.ds(third * width + h * head, head) for third in range(3)] for h in range(first, first + 4)]
            query = [triple[where[0], window] * jnp.bfloat16(factor) for where in at]
            key = [triple[where[1], window] for where in at]
            value = [triple[where[2], window] for where in at]
            d_mix = [d_mixed[where[0], window] for where in at]
            scores = [nn(k.T, q) for k, q in zip(key, query)]
            d_probs = [nn(v.T, d) for v, d in zip(value, d_mix)]
            shifted = [jnp.exp(s - jnp.max(s, axis=0, keepdims=True)) for s in scores]
            probs = [s * (1.0 / jnp.sum(s, axis=0, keepdims=True)) for s in shifted]
            low = [p.astype(jnp.bfloat16) for p in probs]
            mix = [nn(v, p) for v, p in zip(value, low)]
            delta = [jnp.sum(d.astype(jnp.float32) * m, axis=0, keepdims=True) for d, m in zip(d_mix, mix)]
            d_scores = [(p * (d - x)).astype(jnp.bfloat16) for p, d, x in zip(probs, d_probs, delta)]
            d_query = [nn(k, d) * factor for k, d in zip(key, d_scores)]
            d_key = [nt(q, d) for q, d in zip(query, d_scores)]
            d_value = [nt(d, p) for d, p in zip(d_mix, low)]
            for where, m, dq, dk, dv in zip(at, mix, d_query, d_key, d_value):
                mixed[where[0], window] = m.astype(jnp.bfloat16)
                d_triple[where[0], window] = dq.astype(jnp.bfloat16)
                d_triple[where[1], window] = dk.astype(jnp.bfloat16)
                d_triple[where[2], window] = dv.astype(jnp.bfloat16)

    def forward_group(group):
        size = items // groups
        first = group * size
        columns = pl.ds(first * latents, size * latents)

        def each_item(body):
            loop(size, lambda i: body(first + i))

        def each_block(count, body):
            loop(count // BLOCK, lambda b: body(window_at(b, BLOCK)))

        each_item(combine)

        def out_block(window):
            cross[window, columns] = nn(w_out_t[window, :], heard[:, columns])

        each_block(width, out_block)

        def cross_item(i):
            window = window_at(i, latents)
            keep = (1 - skip_ref[i]).astype(jnp.float32)
            total = latent_ref[...].astype(jnp.float32).T + keep * cross[:, window]
            cross[:, window] = total
            normed, _ = norm_down(total)
            mlp_in[:, window] = (normed * mlp_gain[...]).astype(jnp.bfloat16)

        each_item(cross_item)

        def up_block(window):
            value = nn(up_down[window, :], mlp_in[:, columns])
            hidden_rows[window, columns] = value
            act[window, columns] = gelu(value).astype(jnp.bfloat16)

        each_block(hidden, up_block)
        if group == groups - 1:
            for at in range(5):
                saves[at].start()

        def down_block(window):
            after[window, columns] = cross[window, columns] + nn(down_up[window, :], act[:, columns])

        each_block(width, down_block)
        if group == groups - 1:
            saves[5].start()

        def after_item(i):
            window = window_at(i, latents)
            normed, _ = norm_down(after[:, window])
            self_in[:, window] = (normed * self_gain[...]).astype(jnp.bfloat16)

        each_item(after_item)

        def triple_block(window):
            triple[window, columns] = nn(tall[window, :], self_in[:, columns]).astype(jnp.bfloat16)

        each_block(3 * width, triple_block)
        each_item(attend)

    saves = [
        pltpu.make_async_copy(source, target, save_sem.at[at])
        for at, (source, target) in enumerate(
            (
                (hidden_rows, hidden_out), (act.at[:, pl.ds(0, items * latents)], act_out), (mlp_in, mlp_out), (cross, cross_out),
                (heard_f32, heard_f32_out), (after, after_out), (heard, heard_out), (cotangent, cot_out), (d_triple, d_triple_out),
            )
        )
    ]
    saves[7].start()
    for group in range(groups):
        forward_group(group)
    saves[8].start()
    saves[6].start()

    pending = {}

    def put(first_piece, count, offset, left, right):
        size = width // count
        slot = len(pending) % stage.shape[0]
        for key in [key for key in pending if key % stage.shape[0] == slot and pending[key] is not None]:
            pending[key].wait()
            pending[key] = None
        view = stage.at[slot]
        view[...] = nt(left[...], right[...])
        copy = pltpu.make_async_copy(
            view.reshape(count, size, own), mid_out.at[pl.ds(first_piece, count), pl.ds(offset, size)], stage_sem.at[slot]
        )
        copy.start()
        pending[len(pending)] = copy

    size = width // pieces
    my_columns = pl.multiple_of(frame * own, own)
    for third in range(3):
        put(0, pieces, third * size, self_in, d_triple.at[pl.ds(3 * my_columns + third * own, own), :])
    put(0, pieces, 3 * size, mixed, cotangent.at[pl.ds(my_columns, own), :])

    share = latents // frames

    def latents_item(i):
        window = window_at(i, latents)
        for block in range(width // BLOCK):
            piece = pl.ds(block * BLOCK, BLOCK)
            turned[:, piece] = (after[piece, window] + nn(w_self_t[piece, :], mixed[:, window])).T
        latents_out[i] = turned[pl.ds(pl.multiple_of(frame * share, share), share), :].astype(jnp.bfloat16)

    loop(items, latents_item)
    for copy in saves:
        copy.wait()
    for copy in pending.values():
        if copy is not None:
            copy.wait()


def forward(
    frames, pieces, tokens, skip, latent_init, tok_gain, query_gain, mlp_gain, self_gain,
    w_query, w_keyval, w_out, w_up, w_down, w_self_qkv, w_self_out, grad_out,
):
    items, rows, width = tokens.shape
    latents = latent_init.shape[0]
    hidden = w_up.shape[1]
    own = width // frames
    columns = items * latents
    mid_rows = 4 * width // pieces
    bf16, f32 = jnp.bfloat16, jnp.float32
    vmem = pl.BlockSpec(memory_space=pltpu.VMEM)
    anywhere = pl.BlockSpec(memory_space=pl.ANY)
    dma = pltpu.SemaphoreType.DMA
    peers = max(frames - 1, 1)
    return pl.pallas_call(
        functools.partial(forward_kernel, frames, 2 if items % 2 == 0 else 1),
        out_shape=(
            jax.ShapeDtypeStruct((items, 2 * width, rows), bf16),
            jax.ShapeDtypeStruct((items, latents, LANES), f32),
            jax.ShapeDtypeStruct((latents, width), bf16),
            jax.ShapeDtypeStruct((pieces, mid_rows, own), f32),
            jax.ShapeDtypeStruct((items, latents // frames, width), bf16),
            jax.ShapeDtypeStruct((hidden, columns), bf16),
            jax.ShapeDtypeStruct((hidden, columns), f32),
            jax.ShapeDtypeStruct((width, columns), bf16),
            jax.ShapeDtypeStruct((width, columns), f32),
            jax.ShapeDtypeStruct((width, columns), f32),
            jax.ShapeDtypeStruct((width, columns), bf16),
            jax.ShapeDtypeStruct((width, columns), bf16),
            jax.ShapeDtypeStruct((width, columns), f32),
            jax.ShapeDtypeStruct((3 * width, columns), bf16),
            jax.ShapeDtypeStruct((peers, items if frames > 2 else 1, width + 32, latents), f32),
        ),
        in_specs=[anywhere, pl.BlockSpec(memory_space=pltpu.SMEM)] + [vmem] * 5 + [anywhere] * 7 + [vmem],
        out_specs=(anywhere, vmem, vmem, anywhere, vmem) + (anywhere,) * 10,
        scratch_shapes=[
            pltpu.VMEM((2, rows, width), bf16),
            pltpu.VMEM((width, rows), bf16),
            pltpu.VMEM((HEADS, latents, width // HEADS), bf16),
            pltpu.VMEM((items, width + 32, latents), f32),
            pltpu.VMEM((peers, 1 if frames > 2 else items, width + 32, latents), f32),
        ]
        + [pltpu.VMEM((width, width), bf16)] * 4
        + [
            pltpu.VMEM((width, 3 * width), bf16),
            pltpu.VMEM((3 * width, width), bf16),
            pltpu.VMEM((hidden, width), bf16),
            pltpu.VMEM((width, hidden), bf16),
            pltpu.VMEM((width, columns), bf16),
            pltpu.VMEM((width, columns), f32),
            pltpu.VMEM((width, columns), bf16),
            pltpu.VMEM((hidden, max(columns, rows)), bf16),
            pltpu.VMEM((hidden, columns), f32),
            pltpu.VMEM((width, columns), f32),
            pltpu.VMEM((width, columns), bf16),
            pltpu.VMEM((hidden, columns), bf16),
            pltpu.VMEM((width, columns), bf16),
            pltpu.VMEM((width, columns), bf16),
            pltpu.VMEM((width, columns), bf16),
            pltpu.VMEM((3 * width, columns), bf16),
            pltpu.VMEM((width, columns), f32),
            pltpu.VMEM((latents, width), f32),
            pltpu.VMEM((width, LANES), f32),
            pltpu.VMEM((width, LANES), f32),
            pltpu.VMEM((width, LANES), f32),
            pltpu.VMEM((2, width, own), f32),
            dma((2,)), dma((2,)), dma((peers, items)), dma((peers, items)), dma((8,)), dma((2,)), dma, dma((9,)),
        ],
        compiler_params=pltpu.CompilerParams(collective_id=1, has_side_effects=True, vmem_limit_bytes=62 * 2**20),
        name="forward",
    )(
        tokens, skip, latent_init, tok_gain, query_gain, mlp_gain, self_gain,
        w_query, w_keyval, w_out, w_up, w_down, w_self_qkv, w_self_out, grad_out,
    )


def add_into(target, parts, rows):
    step = next(size for size in (96, 80, 64, 60, 48, 40, 24, 16, 8) if rows % size == 0 and size % 8 == 0)

    def body(index):
        window = window_at(index, step)
        total = parts[0][window]
        for part in parts[1:]:
            total = total + part[window]
        target[window] = total

    loop(rows // step, body)


def gelu_slope(value):
    slope = (2 / jnp.pi) ** 0.5
    square = value * value
    tanh = jnp.tanh(value * (slope + (slope * 0.044715) * square))
    half = 0.5 + 0.5 * tanh
    bend = value * (2 * slope + (6 * slope * 0.044715) * square)
    return half + half * (1.0 - half) * bend


def nn_exact(left, right):
    total = jnp.zeros((left.shape[0], right.shape[1]), jnp.float32)
    rest = right
    for _ in range(3):
        part = rest.astype(jnp.bfloat16)
        total = total + nn(left, part)
        rest = rest - part.astype(jnp.float32)
    return total


def backward_kernel(
    chips, frames, streams,
    loc_a, tokens_ref, kv_ref, act_ref, hidden_ref, mlp_ref, cross_ref, after_ref, cot_ref, heard_ref, heard_f32_ref, dtri_ref,
    w_qkv_ref, w_up_ref, w_down_ref, w_out_ref, w_keyval_ref, w_query_ref,
    skip_ref, log_ref, query_ref, latent_ref, tok_gain_ref, query_gain_ref, mlp_gain_ref, self_gain_ref,
    *rest,
):
    outs, rest = rest[:12], rest[12:]
    sums, token_out, (loc_b, loc_c, loc_d), sibs = outs[:4], outs[4], outs[5:8], outs[8:12]
    locs = (loc_a, loc_b, loc_c, loc_d)
    (
        flat, tall, w_square, act, pool, mlp_in, heard, cotangent, branch, d_heard, queries, queries_t, token_stage,
        hidden_stage, after, cross, rows_f32, incoming, stage, small_stage, d_query, gain_sum, tok_gain, mlp_gain, self_gain,
        d_latent, gain_cols, delta, inverse, y_mine, y_sib, ky,
    ), rest = rest[:32], rest[32:]
    n = len(streams)
    mines, sib_slots, rxs = rest[:n], rest[n : 2 * n], rest[2 * n : 3 * n]
    (
        pair_send, pair_recv, ld_sem, ls_sem, rs_send, rs_recv, ag_send, ag_recv, share_send, share_recv, own_sem,
        kpair_send, kpair_recv, y_send, y_recv, y_sem, in_sem, tok_sem, kv_sem, out_sem, hidden_sem, stage_sem, small_sem,
    ) = rest[3 * n :]

    item_index = lax.axis_index("items")
    frame = lax.axis_index("frames")
    core = lax.rem(item_index, 2)
    chip = item_index // 2
    column = lax.rem(chip, 2)
    line = chip // 2
    place = line + column * (chips - 1 - 2 * line)
    way = 1 - 2 * core
    count, rows, width = tokens_ref.shape
    latents = latent_ref.shape[0]
    hidden = hidden_ref.shape[0]
    head = width // HEADS
    factor = head ** -0.5
    own = width // frames
    pieces = 2 * chips
    per_piece = width // pieces
    kv_rows = loc_d.shape[3]
    last = n - 1

    def device_at(position):
        position = lax.rem(position + 2 * chips, chips)
        far = position // (chips // 2)
        return (2 * (position + far * (chips - 1 - 2 * position)) + far) * 2 + core

    right, left = device_at(place + way), device_at(place - way)
    sibling = item_index + way

    def chunk(offset):
        return lax.rem(place + way * offset + 4 * chips, chips)

    def sib_chunk(offset):
        return lax.rem(place - way * offset + 4 * chips, chips)

    barrier = pltpu.get_barrier_semaphore()
    for peer in (left, right, sibling):
        pl.semaphore_signal(barrier, inc=1, device_id=(peer, frame), device_id_type=MESH)
    for hop in range(1, frames):
        pl.semaphore_signal(barrier, inc=1, device_id=(item_index, lax.rem(frame + hop, frames)), device_id_type=MESH)

    def remote(src, dst, send, recv, peer):
        return pltpu.make_async_remote_copy(
            src_ref=src, dst_ref=dst, send_sem=send, recv_sem=recv, device_id=peer, device_id_type=MESH
        )

    def pair(source, k):
        return remote(
            locs[source].at[1 - core, k], sibs[source].at[k], pair_send.at[source, k], pair_recv.at[source, k], (sibling, frame)
        )

    def frame_at(hop):
        return lax.rem(frame + hop, frames)

    def pair_frame(hop, k):
        f = frame_at(hop)
        return remote(
            loc_d.at[f, 1 - core, k], sibs[3].at[f, k], kpair_send.at[hop - 1, k], kpair_recv.at[hop - 1, k], (sibling, frame)
        )

    def start_pairs(source):
        loop(chips, lambda index: pair(source, sib_chunk(-index)).start())

    def part_of(j):
        source, start, size = streams[j]
        return source, pl.ds(start, size)

    def load_mine(j, k, slot):
        source, part = part_of(j)
        src = loc_d.at[frame, core, k, part] if source == 3 else locs[source].at[core, k, part]
        return pltpu.make_async_copy(src, mines[j].at[slot], ld_sem.at[j, slot])

    def load_sib(j, k, slot):
        source, part = part_of(j)
        src = sibs[3].at[frame, k, part] if source == 3 else sibs[source].at[k, part]
        return pltpu.make_async_copy(src, sib_slots[j].at[slot], ls_sem.at[j, slot])

    def ring(j, k, slot):
        return remote(mines[j].at[slot], rxs[j].at[k], rs_send.at[j, slot], rs_recv.at[j, k], (right, frame))

    def own_at(j, k):
        source, part = part_of(j)
        return sums[source].at[core, k, part]

    def gather(j, k, src):
        return remote(src, own_at(j, k), ag_send.at[j, k], ag_recv.at[j, k], (right, frame))

    def share(j, k, src):
        return remote(src, own_at(j, k), share_send.at[j, k], share_recv.at[j, k], (sibling, frame))

    def share_from(j, k):
        source, part = part_of(j)
        return remote(mines[j].at[0], sums[source].at[1 - core, k, part], share_send.at[j, k], share_recv.at[j, k], (sibling, frame))

    def keep(j, k, slot):
        return pltpu.make_async_copy(mines[j].at[slot], own_at(j, k), own_sem.at[j])

    def across(hop, k):
        other = lax.rem(frame + hop, frames)
        return remote(y_mine.at[k], ky.at[hop - 1, k], y_send.at[hop - 1, k], y_recv.at[hop - 1, k], (item_index, other))

    def prefetch(j, op):
        k, slot = chunk(-op), lax.rem(op, 2)
        source, part = part_of(j)
        if source < 3 and (j == 0 or streams[j - 1][0] != source):
            pair(source, k).wait_recv()
        load_mine(j, k, slot).start()
        load_sib(j, k, slot).start()

    def when(condition, body):
        if isinstance(condition, (bool, int)):
            if condition:
                body()
        else:
            pl.when(condition)(body)

    def tick(j, op):
        source, part = part_of(j)
        size = streams[j][2]
        slot = lax.rem(op, 2)

        def reduce_op():
            k = chunk(-op)
            load_mine(j, k, slot).wait()
            load_sib(j, k, slot).wait()
            parts = [mines[j].at[slot], sib_slots[j].at[slot]]
            if source == 3:
                for hop in range(1, frames):
                    across(hop, k).wait_recv()
                    parts.append(ky.at[hop - 1, k])
            if not (isinstance(op, int) and op == 0):
                ring(j, k, slot).wait_recv()
                parts.append(rxs[j].at[k])
            add_into(mines[j].at[slot], parts, size)

            def pass_on():
                ring(j, k, slot).start()
                if isinstance(op, int) and op == 0:
                    prefetch(j, op + 1)
                else:
                    ring(j, k, 1 - slot).wait_send()
                    prefetch(j, op + 1)

            def finish():
                gather(j, k, mines[j].at[slot]).start()
                share(j, k, mines[j].at[slot]).start()
                keep(j, k, slot).start()

            when(op < chips - 1, pass_on)
            when(op == chips - 1, finish)

        def gather_op():
            k = chunk(-op)
            gather(j, k, mines[j].at[0]).wait_recv()

            def forward_on():
                gather(j, k, own_at(j, k)).start()

            when(op < 2 * chips - 2, forward_on)
            share(j, k, own_at(j, k)).start()

        when(op < chips, reduce_op)
        when((op >= chips) & (op < 2 * chips - 1) if not isinstance(op, int) else chips <= op < 2 * chips - 1, gather_op)

    third = 3 * width
    names = [
        (dtri_ref, pool.at[pl.ds(hidden, third), :]),
        (w_qkv_ref, flat.at[:, pl.ds(0, third)]),
        (after_ref, after),
        (cot_ref, cotangent),
        (act_ref, act),
        (w_down_ref, tall),
        (mlp_ref, mlp_in),
        (cross_ref, cross),
        (heard_ref, heard),
        (w_out_ref, w_square),
        (w_up_ref, flat),
        (heard_f32_ref, cross),
        (w_query_ref, w_square),
        (w_keyval_ref.at[:, pl.ds(0, width)], tall.at[pl.ds(2 * rows, width), :]),
        (w_keyval_ref.at[:, pl.ds(width, width)], tall.at[pl.ds(2 * rows + width, width), :]),
    ]
    copies = [pltpu.make_async_copy(src, dst, in_sem.at[at]) for at, (src, dst) in enumerate(names)]
    (
        get_dtri, get_qkv, get_after, get_cot, get_act, get_down, get_mlp, get_cross, get_heard, get_out, get_up, get_heard_f32,
        get_query, get_keys, get_values,
    ) = copies

    def load_hidden(b):
        slot = lax.rem(b, 4)
        return pltpu.make_async_copy(hidden_ref.at[window_at(b, BLOCK), :], hidden_stage.at[slot], hidden_sem.at[slot])

    def tok_load(i):
        slot = lax.rem(i, 2)
        return pltpu.make_async_copy(tokens_ref.at[i], tall.at[window_at(slot, rows), :], tok_sem.at[slot])

    def kv_load(i):
        slot = lax.rem(i, 2)
        return pltpu.make_async_copy(kv_ref.at[i], act.at[window_at(slot, 2 * width), pl.ds(0, rows)], kv_sem.at[slot])

    def token_save(i, b):
        slot = lax.rem(b, 2)
        return pltpu.make_async_copy(token_stage.at[slot], token_out.at[i, window_at(b, LANES), :], out_sem.at[slot])

    for copy in (get_dtri, get_qkv, get_after, get_cot, get_act, get_down, get_mlp, get_cross, get_heard, get_out):
        copy.start()
    for b in range(3):
        load_hidden(b).start()
    pl.semaphore_wait(barrier, 3 + frames - 1)
    start_pairs(0)
    tok_gain[...] = gain_columns(tok_gain_ref)
    mlp_gain[...] = gain_columns(mlp_gain_ref)
    self_gain[...] = gain_columns(self_gain_ref)
    scaled = query_ref[...] * jnp.bfloat16(factor)
    for h in range(HEADS):
        queries[h] = scaled[:, h * head : (h + 1) * head]
    queries_t[...] = scaled.T
    d_query[...] = jnp.zeros_like(d_query)
    gain_sum[...] = jnp.zeros_like(gain_sum)
    gain_cols[...] = jnp.zeros_like(gain_cols)
    d_latent[...] = jnp.zeros_like(d_latent)
    prefetch(0, 0)

    done = [0] * n

    def advance(*which):
        for j in which:
            if done[j] < 2 * chips - 1:
                tick(j, done[j])
                done[j] += 1

    def each_item(body):
        loop(count, lambda i: body(i, window_at(i, latents)))

    def each_block(first, total, body):
        loop(total // BLOCK, lambda b: body(b + first, window_at(b + first, BLOCK)))

    pending = {}

    def put(target, left, right):
        slot = len(pending) % stage.shape[0]
        for key in [key for key in pending if key % stage.shape[0] == slot and pending[key] is not None]:
            pending[key].wait()
            pending[key] = None
        view = stage.at[slot]
        view[...] = nt(left[...], right[...])
        put_start(target, slot)

    def put_start(target, slot):
        copy = pltpu.make_async_copy(stage.at[slot].reshape(*target.shape), target, stage_sem.at[slot])
        copy.start()
        pending[len(pending)] = copy

    def put_done():
        for key in pending:
            if pending[key] is not None:
                pending[key].wait()
                pending[key] = None

    my_columns = pl.multiple_of(frame * own, own)
    lane = lax.broadcasted_iota(jnp.int32, (width, LANES), 1)

    get_dtri.wait()
    get_qkv.wait()
    advance(0)

    def self_block(b, window):
        incoming[window, :] = nn(flat[window, pl.ds(0, third)], pool[pl.ds(hidden, third), :])

    each_block(0, width, self_block)
    get_up.start()
    get_after.wait()
    get_cot.wait()

    def self_back(i, window):
        normed, inverse_row = norm_down(after[:, window])
        arriving = incoming[:, window]
        gain_cols[...] += jnp.where(lane == 1, jnp.sum(arriving * normed, axis=-1, keepdims=True), 0.0)
        d_after = cotangent[:, window].astype(jnp.float32) + norm_down_back(arriving, normed, inverse_row, self_gain[...])
        branch[:, window] = d_after.astype(jnp.bfloat16)
        rows_f32[:, window] = d_after

    each_item(self_back)
    advance(0)
    get_act.wait()
    groups = hidden // width
    for group in range(groups):
        size = hidden // pieces
        span = pieces // groups
        target = loc_b.at[group * span // chips, pl.ds(group * span % chips, span)] if span <= chips else None
        put(target, act.at[pl.ds(group * width, width), :], branch.at[pl.ds(my_columns, own), :])
    put_done()
    start_pairs(1)
    kv_load(0).start()
    get_down.wait()

    def hidden_block(b, window):
        load_hidden(b).wait()

        @pl.when(b + 3 < hidden // BLOCK)
        def _():
            load_hidden(b + 3).start()

        d_act = nn(tall[window, :], branch[...])
        pool[window, :] = (d_act * gelu_slope(hidden_stage[lax.rem(b, 4)])).astype(jnp.bfloat16)

    half = hidden // BLOCK // 2
    each_block(0, half * BLOCK, hidden_block)
    advance(0)
    prefetch(1, 0)
    each_block(half, hidden - half * BLOCK, hidden_block)
    advance(1)
    tok_load(0).start()
    get_keys.start()
    get_values.start()
    get_mlp.wait()
    advance(0)
    for part in range(groups):
        source = pool.at[pl.ds(frame * (hidden // frames) + part * own, own), :]
        put(loc_c.at[:, :, pl.ds(part * per_piece, per_piece)], mlp_in, source)
        if part == groups // 2 - 1:
            advance(1)
    get_up.wait()
    advance(0)

    def mlp_block(b, window):
        incoming[window, :] = nn(flat[window, :], pool[pl.ds(0, hidden), :])

    each_block(0, width, mlp_block)
    get_cross.wait()
    advance(1)

    def mlp_back(i, window):
        normed, inverse_row = norm_down(cross[:, window])
        arriving = incoming[:, window]
        gain_cols[...] += jnp.where(lane == 0, jnp.sum(arriving * normed, axis=-1, keepdims=True), 0.0)
        d_cross = rows_f32[:, window] + norm_down_back(arriving, normed, inverse_row, mlp_gain[...])
        d_latent[...] += d_cross.T
        keep_item = (1 - skip_ref[i]).astype(jnp.float32)
        branch[:, window] = (keep_item * d_cross).astype(jnp.bfloat16)

    each_item(mlp_back)
    get_heard_f32.start()
    get_heard.wait()
    advance(0)
    put(loc_c.at[:, :, pl.ds(groups * per_piece, per_piece)], heard, branch.at[pl.ds(my_columns, own), :])
    put_done()
    start_pairs(2)
    get_out.wait()

    def heard_block(b, window):
        d_heard[window, :] = nn(w_square[window, :], branch[...]).astype(jnp.bfloat16)

    each_block(0, width, heard_block)
    get_query.start()
    get_heard_f32.wait()
    advance(1)

    def delta_item(i, window):
        product = d_heard[:, window].astype(jnp.float32) * cross[:, window]
        sums_of = jnp.sum(product.reshape(HEADS, head, latents), axis=1)
        padded = jnp.concatenate([sums_of, jnp.zeros((LANES - HEADS, latents), jnp.float32)], axis=0)
        delta[i] = padded.T

    each_item(delta_item)
    prefetch(2, 0)
    get_keys.wait()
    get_values.wait()
    advance(0, 2)

    def attend(i, heads):
        base = pl.multiple_of(lax.rem(i, 2) * 2 * width, 2 * width)
        target = pl.multiple_of(i * 2 * width, 2 * width)
        latent_window = window_at(i, latents)
        for h in heads:
            keys_at = pl.ds(h * head, head)
            keys = act[pl.ds(base + h * head, head), pl.ds(0, rows)]
            values = act[pl.ds(base + width + h * head, head), pl.ds(0, rows)]
            d_heard_t = d_heard[keys_at, latent_window]
            probs = jnp.exp(nn(queries[h], keys) - log_ref[i, :, h : h + 1])
            d_probs = nn(d_heard_t.T, values)
            d_scores = (probs * (d_probs - delta[i, :, h : h + 1])).astype(jnp.bfloat16)
            pool[pl.ds(target + h * head, head), pl.ds(0, rows)] = nn(queries_t[keys_at, :], d_scores).astype(jnp.bfloat16)
            pool[pl.ds(target + width + h * head, head), pl.ds(0, rows)] = nn(d_heard_t, probs.astype(jnp.bfloat16)).astype(
                jnp.bfloat16
            )
            d_query[keys_at, :] += nt(keys, d_scores)

    def norm_tokens(i):
        tok_load(i).wait()
        base = pl.multiple_of(lax.rem(i, 2) * rows, rows)

        def norm_block(b):
            window = window_at(b, LANES)
            columns = tall[pl.ds(base + b * LANES, LANES), :].T.astype(jnp.float32)
            block, inverse_row = norm_down(columns)
            after[:, window] = block
            inverse[:, window] = jnp.broadcast_to(inverse_row, (8, LANES))
            flat[:, pl.ds(pl.multiple_of(i * rows + b * LANES, LANES), LANES)] = (block * tok_gain[...]).astype(jnp.bfloat16)

        loop(rows // LANES, norm_block)

    def token_back(i):
        base = pl.multiple_of(i * 2 * width, 2 * width)

        def product(b):
            window = window_at(b, BLOCK)
            keys_w = tall[pl.ds(pl.multiple_of(2 * rows + b * BLOCK, BLOCK), BLOCK), :]
            values_w = tall[pl.ds(pl.multiple_of(2 * rows + width + b * BLOCK, BLOCK), BLOCK), :]
            incoming[window, :] = nn(keys_w, pool[pl.ds(base, width), pl.ds(0, rows)]) + nn(
                values_w, pool[pl.ds(base + width, width), pl.ds(0, rows)]
            )

        loop(width // BLOCK, product)

        def back_block(b):
            window = window_at(b, LANES)
            block = after[:, window]
            arriving = incoming[:, window]
            gain_sum[...] += arriving * block
            result = norm_down_back(arriving, block, inverse[pl.ds(0, 1), window], tok_gain[...])

            @pl.when((i > 0) | (b > 1))
            def _():
                token_save(i, b).wait()

            token_stage[lax.rem(b, 2)] = result.T.astype(jnp.bfloat16)
            token_save(i, b).start()

        loop(rows // LANES, back_block)

    base_ops = list(done)

    def one_item(i):
        kv_load(i).wait()

        @pl.when(i + 1 < count)
        def _():
            kv_load(i + 1).start()
            tok_load(i + 1).start()

        norm_tokens(i)
        attend(i, range(HEADS // 2))
        tick(1, base_ops[1] + i)
        attend(i, range(HEADS // 2, HEADS))
        tick(2, base_ops[2] + i)
        token_back(i)
        tick(0, base_ops[0] + i)

    loop(count, one_item)
    for j in range(last):
        done[j] = base_ops[j] + count

    small = 2 * latents // pieces
    get_query.wait()
    d_query[...] = d_query[...] * factor
    q_total = d_query[...]
    q_normed, q_inverse = norm_down(latent_ref[...].astype(jnp.float32).T)
    q_incoming = nn_exact(w_square[...], q_total)
    all_gains = gain_cols[...]
    all_gains = jnp.where(lane == 2, jnp.sum(gain_sum[...], axis=-1, keepdims=True), all_gains)
    all_gains = jnp.where(lane == 3, jnp.sum(q_incoming * q_normed, axis=-1, keepdims=True), all_gains)
    gain_rows = all_gains.T[:8]
    latent_rows = norm_down_back(q_incoming, q_normed, q_inverse, gain_columns(query_gain_ref)).T
    query_rows = q_total.T
    for f in range(frames):
        mask = (frame == f).astype(jnp.float32)
        mine_columns = slice(f * own, (f + 1) * own)
        latent_part = latent_rows[:, mine_columns] + mask * d_latent[:, mine_columns]
        both = jnp.concatenate([query_rows[:, mine_columns], latent_part], axis=0)
        small_stage[f, :, :, pl.ds(0, small), :] = both.reshape(2, chips, small, own)
        row = lax.broadcasted_iota(jnp.int32, (8, own), 0)
        gain_block = gain_rows[:, mine_columns] * jnp.where(row < 2, mask, 1.0)
        small_stage[f, :, :, pl.ds(small, 8), :] = jnp.zeros((2, chips, 8, own), jnp.float32)
        small_stage[f, 0, 0, pl.ds(small, 8), :] = gain_block
    put_small = pltpu.make_async_copy(small_stage, loc_d.at[:, :, :, pl.ds(2 * per_piece, small + 8)], small_sem)
    put_small.start()
    advance(1)
    for hop in range(1, frames + 1):
        f = frame_at(hop)
        for b in range(2):
            slot = len(pending) % stage.shape[0]
            for key in [key for key in pending if key % stage.shape[0] == slot and pending[key] is not None]:
                pending[key].wait()
                pending[key] = None
            first_row = pl.multiple_of((2 * f + b) * own, own)
            source = jnp.concatenate(
                [pool[pl.ds(i * 2 * width + first_row, own), pl.ds(0, rows)] for i in range(count)], axis=1
            )
            stage[slot] = nt(flat[:, pl.ds(0, count * rows)], source)
            put_start(loc_d.at[f, :, :, pl.ds(b * per_piece, per_piece)], slot)
        if hop == 1:
            put_small.wait()
        put_done()
        loop(chips, lambda index: pair_frame(hop, sib_chunk(-index)).start())
        if hop <= 2:
            advance(2 if hop == 1 else 0)
    advance(1)
    for hop in range(1, frames):
        other = frame_at(hop)
        if hop > 1:
            for k in range(chips):
                across(hop - 1, k).wait_send()
        for k in range(chips):
            pair_frame(hop, k).wait_recv()
        one = pltpu.make_async_copy(loc_d.at[other, core], y_mine, y_sem.at[0])
        two = pltpu.make_async_copy(sibs[3].at[other], y_sib, y_sem.at[1])
        one.start()
        two.start()
        one.wait()
        two.wait()

        def send_across(index, hop=hop):
            k = chunk(-index)
            add_into(y_mine.at[k], [y_mine.at[k], y_sib.at[k]], kv_rows)
            across(hop, k).start()

        loop(chips, send_across)
    advance(2)
    for k in range(chips):
        pair_frame(frames, k).wait_recv()
    load_mine(last, chunk(0), 0).start()
    load_sib(last, chunk(0), 0).start()
    advance(0)
    total = 2 * chips - 1
    others = sum(total - done[j] for j in range(last))
    turns, taken = total - done[last], 0
    for turn in range(turns):
        while taken * turns < (turn + 1) * others:
            j = max(range(last), key=lambda j: (total - done[j]) * (streams[j][2] + 160))
            advance(j)
            taken += 1
        advance(last)

    def drain(k):
        for source in range(3):
            pair(source, k).wait_send()
        for hop in range(1, frames + 1):
            pair_frame(hop, k).wait_send()
        for j in range(n):
            share(j, k, mines[j].at[0]).wait_send()
            share_from(j, k).wait_recv()
        if frames > 1:
            across(frames - 1, k).wait_send()

    loop(chips, drain)

    def drain_ring(step):
        for j in range(n):
            gather(j, chunk(1 - step), mines[j].at[0]).wait_send()

    loop(chips - 1, drain_ring)
    for j in range(n):
        ring(j, 0, (chips - 2) % 2).wait_send()
        keep(j, chunk(1), (chips - 1) % 2).wait()
    for b in range(2):
        token_save(0, b).wait()


def backward(
    frames, first, tokens, kv, act, hidden, mlp_in, cross, after, cotangent, heard, heard_f32, d_triple, skip, log_total, query,
    latent_init, tok_gain, query_gain, mlp_gain, self_gain, w_query, w_keyval, w_out, w_up, w_down, w_self_qkv,
):
    chips, first_rows, own = first.shape[1:]
    items, rows, width = tokens.shape
    latents = latent_init.shape[0]
    hidden_width, columns = hidden.shape
    pieces = 2 * chips
    per_piece = width // pieces
    kv_rows = 2 * per_piece + 2 * latents // pieces + 8
    source_rows = (first_rows, hidden_width // pieces, per_piece * (hidden_width // width + 1), kv_rows)
    streams = tuple((source, 0, size) for source, size in enumerate(source_rows))
    n = len(streams)
    dma = pltpu.SemaphoreType.DMA
    peers = max(frames - 1, 1)
    f32, bf16 = jnp.float32, jnp.bfloat16
    vmem = pl.BlockSpec(memory_space=pltpu.VMEM)
    anywhere = pl.BlockSpec(memory_space=pl.ANY)
    wide = max(columns, rows)
    scratch = [
        pltpu.VMEM((width, max(hidden_width, items * rows)), bf16),
        pltpu.VMEM((max(hidden_width, 2 * rows + 2 * width), width), bf16),
        pltpu.VMEM((width, width), bf16),
        pltpu.VMEM((max(hidden_width, 4 * width), wide), bf16),
        pltpu.VMEM((max(hidden_width + 3 * width, items * 2 * width), wide), bf16),
        pltpu.VMEM((width, columns), bf16),
        pltpu.VMEM((width, columns), bf16),
        pltpu.VMEM((width, columns), bf16),
        pltpu.VMEM((width, columns), bf16),
        pltpu.VMEM((width, columns), bf16),
        pltpu.VMEM((HEADS, latents, width // HEADS), bf16),
        pltpu.VMEM((width, latents), bf16),
        pltpu.VMEM((2, LANES, width), bf16),
        pltpu.VMEM((4, BLOCK, columns), f32),
        pltpu.VMEM((width, wide), f32),
        pltpu.VMEM((width, columns), f32),
        pltpu.VMEM((width, columns), f32),
        pltpu.VMEM((width, wide), f32),
        pltpu.VMEM((2, width, own), f32),
        pltpu.VMEM((frames, 2, chips, 2 * latents // pieces + 8, own), f32),
        pltpu.VMEM((width, latents), f32),
        pltpu.VMEM((width, LANES), f32),
        pltpu.VMEM((width, LANES), f32),
        pltpu.VMEM((width, LANES), f32),
        pltpu.VMEM((width, LANES), f32),
        pltpu.VMEM((latents, width), f32),
        pltpu.VMEM((width, LANES), f32),
        pltpu.VMEM((items, latents, LANES), f32),
        pltpu.VMEM((8, rows), f32),
        pltpu.VMEM((chips, kv_rows, own), f32),
        pltpu.VMEM((chips, kv_rows, own), f32),
        pltpu.VMEM((peers, chips, kv_rows, own), f32),
    ]
    scratch += [pltpu.VMEM((2, size, own), f32) for _, _, size in streams]
    scratch += [pltpu.VMEM((2, size, own), f32) for _, _, size in streams]
    scratch += [pltpu.VMEM((chips, size, own), f32) for _, _, size in streams]
    scratch += [
        dma((3, chips)), dma((3, chips)), dma((n, 2)), dma((n, 2)), dma((n, 2)), dma((n, chips)),
        dma((n, chips)), dma((n, chips)), dma((n, chips)), dma((n, chips)), dma((n,)),
        dma((frames, chips)), dma((frames, chips)), dma((peers, chips)), dma((peers, chips)), dma((2,)), dma((15,)), dma((2,)), dma((2,)), dma((2,)), dma((4,)), dma((2,)), dma,
    ]
    shape = jax.ShapeDtypeStruct
    summed = tuple(shape((2, chips, size, own), f32) for size in source_rows)
    return pl.pallas_call(
        functools.partial(backward_kernel, chips, frames, streams),
        out_shape=summed
        + (shape(tokens.shape, bf16),)
        + summed[1:3]
        + (shape((frames, 2, chips, kv_rows, own), f32),)
        + tuple(shape((chips, size, own), f32) for size in source_rows[:3])
        + (shape((frames, chips, kv_rows, own), f32),),
        in_specs=[anywhere] * 18 + [pl.BlockSpec(memory_space=pltpu.SMEM)] + [vmem] * 7,
        out_specs=(anywhere,) * 12,
        scratch_shapes=scratch,
        compiler_params=pltpu.CompilerParams(collective_id=0, has_side_effects=True, vmem_limit_bytes=62 * 2**20),
        name="backward",
    )(
        first, tokens, kv, act, hidden, mlp_in, cross, after, cotangent, heard, heard_f32, d_triple,
        w_self_qkv, w_up, w_down, w_out, w_keyval, w_query, skip, log_total, query, latent_init,
        tok_gain, query_gain, mlp_gain, self_gain,
    )


def unpack_kernel(first_ref, second_ref, third_ref, kv_ref, latent_ref, qgain_ref, *rest):
    outs, (query_out, *gain_outs), (blocks, total, tail, in_sem, out_sem) = rest[:7], rest[7:12], rest[12:]
    pieces, _, own = first_ref.shape
    loads, stores = [], []

    def place(source, offset, out):
        rows, columns = out.shape
        size = rows // pieces
        view = out.reshape(pieces, size, columns)
        for b in range(columns // own):
            at = len(loads)
            area = blocks.at[pl.ds(starts[at], pieces * size), :].reshape(pieces, size, own)
            loads.append(pltpu.make_async_copy(source.at[:, pl.ds(offset + b * size, size), :], area, in_sem.at[at]))
            stores.append(pltpu.make_async_copy(area, view.at[:, :, pl.ds(b * own, own)], out_sem.at[at]))
        return offset + size * columns // own

    starts, start = [], 0
    for out in outs[:6]:
        rows, columns = out.shape
        for b in range(columns // own):
            starts.append(start)
            start += rows
    place(first_ref, place(first_ref, 0, outs[0]), outs[1])
    place(second_ref, 0, outs[2])
    place(third_ref, place(third_ref, 0, outs[3]), outs[4])
    offset = place(kv_ref, 0, outs[5])
    latents = outs[6].shape[0]
    small = 2 * latents // pieces
    half = pieces // 2
    query = pltpu.make_async_copy(kv_ref.at[:, pl.ds(offset, small), :], total, in_sem.at[len(loads)])
    gains = pltpu.make_async_copy(kv_ref.at[0, pl.ds(offset + small, 8), :], tail, in_sem.at[len(loads) + 1])
    query.start()
    gains.start()
    for copy in loads:
        copy.start()
    normed, _ = norm_down(latent_ref[...].astype(jnp.float32).T)
    query_in = (normed * gain_columns(qgain_ref)).astype(jnp.bfloat16)
    query.wait()
    query_out[...] = nn_exact(query_in, total[pl.ds(0, half)].reshape(latents, own))
    outs[6][...] = total[pl.ds(half, half)].reshape(latents, own)
    gains.wait()
    for out, row in zip(gain_outs, (2, 3, 0, 1)):
        out[...] = tail[row]
    for load, store in zip(loads, stores):
        load.wait()
        store.start()
    for store in stores:
        store.wait()


def unpack_all(sums, latent_init, query_gain, shapes):
    f32 = jnp.float32
    own = sums[0].shape[-1]
    latents, width = latent_init.shape
    pieces = sums[0].shape[0]
    vmem = pl.BlockSpec(memory_space=pltpu.VMEM)
    anywhere = pl.BlockSpec(memory_space=pl.ANY)
    count = sum(columns // own for _, columns in shapes)
    size = sum(rows * columns // own for rows, columns in shapes)
    return pl.pallas_call(
        unpack_kernel,
        out_shape=tuple(jax.ShapeDtypeStruct(shape, f32) for shape in shapes) + (
            jax.ShapeDtypeStruct((latents, own), f32), jax.ShapeDtypeStruct((width, own), f32))
        + (jax.ShapeDtypeStruct((own,), f32),) * 4,
        in_specs=[anywhere] * 4 + [vmem] * 2,
        out_specs=(anywhere,) * len(shapes) + (vmem,) * 6,
        scratch_shapes=[
            pltpu.VMEM((size, own), f32), pltpu.VMEM((pieces, 2 * latents // pieces, own), f32), pltpu.VMEM((8, own), f32),
            pltpu.SemaphoreType.DMA((count + 2,)), pltpu.SemaphoreType.DMA((count,)),
        ],
        compiler_params=pltpu.CompilerParams(vmem_limit_bytes=60 * 2**20),
        name="unpack_all",
    )(*sums, latent_init, query_gain)


def unpack(packed, rows, columns):
    pieces, _, width = packed.shape
    split = packed.reshape(pieces, columns // width, rows // pieces, width)
    return jnp.swapaxes(split, 1, 2).reshape(rows, columns)


def cut(packed, shapes):
    start, out = 0, []
    for rows, columns in shapes:
        count = rows * columns // packed.shape[-1] // packed.shape[0]
        out.append(unpack(packed[:, start : start + count], rows, columns))
        start += count
    return out


def shards(
    tokens,
    skip,
    latent_init,
    tok_gain,
    query_gain,
    mlp_gain,
    self_gain,
    w_query,
    w_keyval,
    w_out,
    w_up,
    w_down,
    w_self_qkv,
    w_self_out,
    grad_out,
):
    frames, pieces = lax.axis_size("frames"), lax.axis_size("items")
    latents, width = latent_init.shape
    hidden = w_up.shape[1]
    own = width // frames
    kv, log_total, query, first, out_latents, act, hidden_rows, mlp_in, cross, after, cotangent, heard, heard_f32, d_triple, _ = forward(
        frames, pieces, tokens, skip, latent_init, tok_gain, query_gain, mlp_gain, self_gain,
        w_query, w_keyval, w_out, w_up, w_down, w_self_qkv, w_self_out, grad_out,
    )
    *sums, token_grad = backward(
        frames, first.reshape((2, pieces // 2) + first.shape[1:]), tokens, kv, act, hidden_rows, mlp_in, cross, after, cotangent,
        heard, heard_f32, d_triple, skip, log_total, query, latent_init, tok_gain, query_gain, mlp_gain, self_gain,
        w_query, w_keyval, w_out, w_up, w_down, w_self_qkv,
    )[:5]
    sums = [array.reshape((pieces,) + array.shape[2:]) for array in sums]
    shapes = ((width, 3 * own), (width, own), (hidden, own), (width, hidden // frames), (width, own), (width, 2 * own))
    if own % LANES == 0:
        *grads, latent_grad, grad_query, gain_tok, gain_query, gain_mlp, gain_self = unpack_all(
            sums, latent_init, query_gain, shapes
        )
    else:
        grads = cut(sums[0], shapes[:2]) + cut(sums[1], shapes[2:3]) + cut(sums[2], shapes[3:5])
        keyval_sum, small = cut(sums[3], (shapes[5], (2 * latents, own)))
        grads.append(keyval_sum)
        latent_grad = small[latents:]
        normed, _ = norm_down(latent_init.astype(jnp.float32).T)
        query_in = (normed * query_gain[:, None]).astype(jnp.bfloat16)
        grad_query = jnp.dot(query_in.astype(jnp.float32), small[:latents], precision=lax.Precision.HIGHEST)
        gain_mlp, gain_self, gain_tok, gain_query = [sums[3][0, row - 8] for row in range(4)]
    return (
        out_latents,
        token_grad,
        latent_grad,
        gain_tok,
        gain_query,
        gain_mlp,
        gain_self,
        grad_query,
        grads[5],
        grads[4],
        grads[3],
        grads[2],
        grads[0],
        grads[1],
    )


def solution(mesh):
    in_specs = (
        P("items", "frames", None),
        P("items"),
        P(),
        P(),
        P(),
        P(),
        P(),
        P(),
        P(),
        P(),
        P(),
        P(),
        P(),
        P(),
        P("items", None, None),
    )
    out_specs = (
        P("items", "frames", None),
        P("items", "frames", None),
        P(None, "frames"),
        P("frames"),
        P("frames"),
        P("frames"),
        P("frames"),
        P(None, "frames"),
        P(None, "frames"),
        P(None, "frames"),
        P(None, "frames"),
        P(None, "frames"),
        P(None, "frames"),
        P(None, "frames"),
    )
    return jax.shard_map(shards, mesh=mesh, in_specs=in_specs, out_specs=out_specs, check_vma=False)
```

```python
import functools

import jax
import jax.numpy as jnp
from jax import lax
from jax.experimental import pallas as pl
from jax.experimental.pallas import tpu as pltpu
from jax.sharding import PartitionSpec as P

MESH = pl.DeviceIdType.MESH
HEADS = 12
EPSILON = 1e-05
LANES = 128
BLOCK = 256


def nn(left, right):
    return lax.dot_general(left, right, (((1,), (0,)), ((), ())), preferred_element_type=jnp.float32)


def nt(left, right):
    return lax.dot_general(left, right, (((1,), (1,)), ((), ())), preferred_element_type=jnp.float32)


def norm_down(columns):
    centered = columns - jnp.mean(columns, axis=0, keepdims=True)
    inverse = lax.rsqrt(jnp.mean(centered * centered, axis=0, keepdims=True) + EPSILON)
    return centered * inverse, inverse


def gelu(value):
    slope = (2 / jnp.pi) ** 0.5
    tanh = jnp.tanh(value * (slope + (slope * 0.044715) * (value * value)))
    return value * (0.5 + 0.5 * tanh)


def norm_down_back(incoming, normed, inverse, gain):
    scaled = incoming * gain
    average = jnp.mean(scaled, axis=0, keepdims=True)
    along = jnp.mean(scaled * normed, axis=0, keepdims=True)
    return inverse * (scaled - average - normed * along)


def gain_columns(gain_ref):
    return jnp.broadcast_to(gain_ref[...].reshape(1, -1), (LANES, gain_ref.shape[0])).T


def loop(count, body):
    def step(index, carry):
        body(index)
        return carry

    lax.fori_loop(0, count, step, 0)


def window_at(index, size):
    return pl.ds(pl.multiple_of(index * size, size), size)


def forward_kernel(
    frames, groups,
    tokens_ref, skip_ref, latent_ref, tok_gain_ref, query_gain_ref, mlp_gain_ref, self_gain_ref,
    w_query_ref, w_keyval_ref, w_out_ref, w_up_ref, w_down_ref, w_qkv_ref, w_self_ref, grad_ref,
    kv_out, log_out, query_out, mid_out, latents_out, act_out, hidden_out, mlp_out, cross_out, after_out, cot_out, heard_out,
    heard_f32_out, d_triple_out, arrived,
    tokens, tok_in, queries, sent, got,
    w_out, w_out_t, w_self, w_self_t, w_qkv, tall, up_down, down_up,
    heard, cross, mlp_in, act, hidden_rows, after, self_in, triple, mixed, cotangent, d_mixed, d_triple, heard_f32, turned,
    tok_gain, mlp_gain, self_gain, stage,
    tok_sem, kv_sem, y_send, y_recv, w_sem, stage_sem, got_sem, save_sem,
):
    items, rows, width = tokens_ref.shape
    latents = latent_ref.shape[0]
    hidden = w_up_ref.shape[1]
    head = width // HEADS
    factor = head ** -0.5
    own = width // frames
    stat = sent.shape[1] - width
    pieces = mid_out.shape[0]
    item = lax.axis_index("items")
    frame = lax.axis_index("frames")

    barrier = pltpu.get_barrier_semaphore()
    for hop in range(1, frames):
        pl.semaphore_signal(barrier, inc=1, device_id=(item, lax.rem(frame + hop, frames)), device_id_type=MESH)

    wide = 2 * width
    load_query = pltpu.make_async_copy(w_query_ref, w_self_t, w_sem.at[0])
    load_keyval = pltpu.make_async_copy(w_keyval_ref, down_up.at[:, pl.ds(0, wide)], w_sem.at[1])
    load_self = pltpu.make_async_copy(w_self_ref, w_self, w_sem.at[2])
    load_out = pltpu.make_async_copy(w_out_ref, w_out, w_sem.at[3])
    load_qkv = pltpu.make_async_copy(w_qkv_ref, w_qkv, w_sem.at[4])
    load_up = pltpu.make_async_copy(w_up_ref, down_up, w_sem.at[5])

    def load_tokens(i):
        return pltpu.make_async_copy(tokens_ref.at[i], tokens.at[lax.rem(i, 2)], tok_sem.at[lax.rem(i, 2)])

    columns_all = items * latents
    spare = width - columns_all
    third = 3 * width
    loads_down = [
        pltpu.make_async_copy(w_down_ref.at[:, pl.ds(0, columns_all)], triple, w_sem.at[6]),
        pltpu.make_async_copy(
            w_down_ref.at[pl.ds(0, third), pl.ds(columns_all, spare)], d_triple.at[:, pl.ds(0, spare)], w_sem.at[7]
        ),
        pltpu.make_async_copy(
            w_down_ref.at[pl.ds(third, hidden - third), pl.ds(columns_all, spare)],
            d_triple.at[pl.ds(0, hidden - third), pl.ds(spare, spare)],
            w_sem.at[8],
        ),
    ]

    def kv_at(i):
        return pl.ds(pl.multiple_of(lax.rem(i, 2) * wide, wide), wide)

    def save_kv(i):
        return pltpu.make_async_copy(act.at[kv_at(i), pl.ds(0, rows)], kv_out.at[i], kv_sem.at[lax.rem(i, 2)])

    def across(i, hop):
        return pltpu.make_async_remote_copy(
            src_ref=sent.at[i], dst_ref=(arrived if frames > 2 else got).at[hop - 1, i], send_sem=y_send.at[hop - 1, i], recv_sem=y_recv.at[hop - 1, i],
            device_id=(item, lax.rem(frame + hop, frames)), device_id_type=MESH,
        )

    load_tokens(0).start()
    load_query.start()
    load_keyval.start()
    load_tokens(1).start()
    for copy in (load_self, load_out, load_qkv):
        copy.start()

    latent_t = latent_ref[...].astype(jnp.float32).T
    query_normed, _ = norm_down(latent_t)
    query_in = (query_normed * gain_columns(query_gain_ref)).T.astype(jnp.bfloat16)
    tok_gain[...] = gain_columns(tok_gain_ref)
    mlp_gain[...] = gain_columns(mlp_gain_ref)
    self_gain[...] = gain_columns(self_gain_ref)
    load_query.wait()
    query = nn(query_in, w_self_t[...]).astype(jnp.bfloat16)
    query_out[...] = query
    scaled = query * jnp.bfloat16(factor)
    for h in range(HEADS):
        queries[h] = scaled[:, h * head : (h + 1) * head]
    load_keyval.wait()
    for block in range(wide // BLOCK):
        window = pl.ds(block * BLOCK, BLOCK)
        tall[window, :] = down_up[:, window].T
    load_up.start()
    for copy in loads_down:
        copy.start()
    pl.semaphore_wait(barrier, frames - 1)

    def heard_item(i):
        slot = lax.rem(i, 2)
        load_tokens(i).wait()

        def norm_block(b):
            window = window_at(b, LANES)
            normed, _ = norm_down(tokens[slot, window, :].T.astype(jnp.float32))
            tok_in[:, window] = (normed * tok_gain[...]).astype(jnp.bfloat16)

        loop(rows // LANES, norm_block)

        @pl.when(i + 2 < items)
        def _():
            load_tokens(i + 2).start()

        @pl.when(i >= 2)
        def _():
            save_kv(i - 2).wait()

        base = pl.multiple_of(slot * wide, wide)
        for block in range(wide // BLOCK):
            act[pl.ds(base + block * BLOCK, BLOCK), pl.ds(0, rows)] = nn(
                tall[pl.ds(block * BLOCK, BLOCK), :], tok_in[...]
            ).astype(jnp.bfloat16)
        save_kv(i).start()
        lane = lax.broadcasted_iota(jnp.int32, (latents, LANES), 1)
        stats = jnp.zeros((latents, LANES), jnp.float32)
        for h in range(HEADS):
            scores = nn(queries[h], act[pl.ds(base + h * head, head), pl.ds(0, rows)])
            most = jnp.max(scores, axis=-1, keepdims=True)
            shifted = jnp.exp(scores - most)
            total = jnp.sum(shifted, axis=-1, keepdims=True)
            stats = jnp.where(lane == h, most, stats)
            stats = jnp.where(lane == h + stat // 2, total, stats)
            sent[i, pl.ds(h * head, head), :] = nt(
                act[pl.ds(base + width + h * head, head), pl.ds(0, rows)], shifted.astype(jnp.bfloat16)
            )
        sent[i, pl.ds(width, stat), :] = stats.T[:stat]
        for hop in range(1, frames):
            across(i, hop).start()

    loop(items, heard_item)

    def turn(source, target, count):
        def block(b):
            window = window_at(b, BLOCK)
            target[window, :] = source[:, window].T

        loop(count // BLOCK, block)

    load_self.wait()

    def load_cotangent(i):
        cotangent[:, window_at(i, latents)] = grad_ref[i].T

    loop(items, load_cotangent)
    for block in range(width // BLOCK):
        window = pl.ds(block * BLOCK, BLOCK)
        d_mixed[window, :] = nn(w_self[window, :], cotangent[...]).astype(jnp.bfloat16)
    turn(w_self, w_self_t, width)
    load_out.wait()
    turn(w_out, w_out_t, width)
    load_up.wait()
    turn(down_up, up_down, hidden)
    for copy in loads_down:
        copy.wait()

    def turn_down(b):
        window = window_at(b, BLOCK)
        down_up[pl.ds(0, columns_all), window] = triple[window, :].T

    loop(hidden // BLOCK, turn_down)
    for b in range(hidden // BLOCK):
        window = pl.ds(b * BLOCK, BLOCK)
        if b * BLOCK < third:
            down_up[pl.ds(columns_all, spare), window] = d_triple[window, pl.ds(0, spare)].T
        else:
            down_up[pl.ds(columns_all, spare), window] = d_triple[pl.ds(b * BLOCK - third, BLOCK), pl.ds(spare, spare)].T
    load_qkv.wait()
    turn(w_qkv, tall, 3 * width)
    for i in range(max(items - 2, 0), items):
        save_kv(i).wait()

    def combine(i):
        for hop in range(1, frames):
            across(i, hop).wait_send()
            across(i, hop).wait_recv()
            if frames > 2:
                near = pltpu.make_async_copy(arrived.at[hop - 1, i], got.at[hop - 1, 0], got_sem)
                near.start()
                near.wait()
        parts = [sent.at[i]] + [got.at[hop, 0 if frames > 2 else i] for hop in range(frames - 1)]
        highs = [part[pl.ds(width, stat // 2), :] for part in parts]
        sums = [part[pl.ds(width + stat // 2, stat // 2), :] for part in parts]
        most = functools.reduce(jnp.maximum, highs)
        total = functools.reduce(jnp.add, [low * jnp.exp(high - most) for high, low in zip(highs, sums)])
        log_total = most + jnp.log(total)
        scales = [jnp.exp(high - log_total) for high in highs]
        for h in range(HEADS):
            window = pl.ds(h * head, head)
            together = functools.reduce(
                jnp.add, [part[window, :] * scale[h : h + 1] for part, scale in zip(parts, scales)]
            )
            heard_f32[window, window_at(i, latents)] = together
            heard[window, window_at(i, latents)] = together.astype(jnp.bfloat16)
        padded = jnp.concatenate([log_total, jnp.zeros((LANES - stat // 2, latents), jnp.float32)], axis=0)
        log_out[i] = padded.T

    def attend(i):
        window = window_at(i, latents)
        for first in range(0, HEADS, 4):
            at = [[pl.ds(third * width + h * head, head) for third in range(3)] for h in range(first, first + 4)]
            query = [triple[where[0], window] * jnp.bfloat16(factor) for where in at]
            key = [triple[where[1], window] for where in at]
            value = [triple[where[2], window] for where in at]
            d_mix = [d_mixed[where[0], window] for where in at]
            scores = [nn(k.T, q) for k, q in zip(key, query)]
            d_probs = [nn(v.T, d) for v, d in zip(value, d_mix)]
            shifted = [jnp.exp(s - jnp.max(s, axis=0, keepdims=True)) for s in scores]
            probs = [s * (1.0 / jnp.sum(s, axis=0, keepdims=True)) for s in shifted]
            low = [p.astype(jnp.bfloat16) for p in probs]
            mix = [nn(v, p) for v, p in zip(value, low)]
            delta = [jnp.sum(d.astype(jnp.float32) * m, axis=0, keepdims=True) for d, m in zip(d_mix, mix)]
            d_scores = [(p * (d - x)).astype(jnp.bfloat16) for p, d, x in zip(probs, d_probs, delta)]
            d_query = [nn(k, d) * factor for k, d in zip(key, d_scores)]
            d_key = [nt(q, d) for q, d in zip(query, d_scores)]
            d_value = [nt(d, p) for d, p in zip(d_mix, low)]
            for where, m, dq, dk, dv in zip(at, mix, d_query, d_key, d_value):
                mixed[where[0], window] = m.astype(jnp.bfloat16)
                d_triple[where[0], window] = dq.astype(jnp.bfloat16)
                d_triple[where[1], window] = dk.astype(jnp.bfloat16)
                d_triple[where[2], window] = dv.astype(jnp.bfloat16)

    def forward_group(group):
        size = items // groups
        first = group * size
        columns = pl.ds(first * latents, size * latents)

        def each_item(body):
            loop(size, lambda i: body(first + i))

        def each_block(count, body):
            loop(count // BLOCK, lambda b: body(window_at(b, BLOCK)))

        each_item(combine)

        def out_block(window):
            cross[window, columns] = nn(w_out_t[window, :], heard[:, columns])

        each_block(width, out_block)

        def cross_item(i):
            window = window_at(i, latents)
            keep = (1 - skip_ref[i]).astype(jnp.float32)
            total = latent_ref[...].astype(jnp.float32).T + keep * cross[:, window]
            cross[:, window] = total
            normed, _ = norm_down(total)
            mlp_in[:, window] = (normed * mlp_gain[...]).astype(jnp.bfloat16)

        each_item(cross_item)

        def up_block(window):
            value = nn(up_down[window, :], mlp_in[:, columns])
            hidden_rows[window, columns] = value
            act[window, columns] = gelu(value).astype(jnp.bfloat16)

        each_block(hidden, up_block)
        if group == groups - 1:
            for at in range(5):
                saves[at].start()

        def down_block(window):
            after[window, columns] = cross[window, columns] + nn(down_up[window, :], act[:, columns])

        each_block(width, down_block)
        if group == groups - 1:
            saves[5].start()

        def after_item(i):
            window = window_at(i, latents)
            normed, _ = norm_down(after[:, window])
            self_in[:, window] = (normed * self_gain[...]).astype(jnp.bfloat16)

        each_item(after_item)

        def triple_block(window):
            triple[window, columns] = nn(tall[window, :], self_in[:, columns]).astype(jnp.bfloat16)

        each_block(3 * width, triple_block)
        each_item(attend)

    saves = [
        pltpu.make_async_copy(source, target, save_sem.at[at])
        for at, (source, target) in enumerate(
            (
                (hidden_rows, hidden_out), (act.at[:, pl.ds(0, items * latents)], act_out), (mlp_in, mlp_out), (cross, cross_out),
                (heard_f32, heard_f32_out), (after, after_out), (heard, heard_out), (cotangent, cot_out), (d_triple, d_triple_out),
            )
        )
    ]
    saves[7].start()
    for group in range(groups):
        forward_group(group)
    saves[8].start()
    saves[6].start()

    pending = {}

    def put(first_piece, count, offset, left, right):
        size = width // count
        slot = len(pending) % stage.shape[0]
        for key in [key for key in pending if key % stage.shape[0] == slot and pending[key] is not None]:
            pending[key].wait()
            pending[key] = None
        view = stage.at[slot]
        view[...] = nt(left[...], right[...])
        copy = pltpu.make_async_copy(
            view.reshape(count, size, own), mid_out.at[pl.ds(first_piece, count), pl.ds(offset, size)], stage_sem.at[slot]
        )
        copy.start()
        pending[len(pending)] = copy

    size = width // pieces
    my_columns = pl.multiple_of(frame * own, own)
    for third in range(3):
        put(0, pieces, third * size, self_in, d_triple.at[pl.ds(3 * my_columns + third * own, own), :])
    put(0, pieces, 3 * size, mixed, cotangent.at[pl.ds(my_columns, own), :])

    share = latents // frames

    def latents_item(i):
        window = window_at(i, latents)
        for block in range(width // BLOCK):
            piece = pl.ds(block * BLOCK, BLOCK)
            turned[:, piece] = (after[piece, window] + nn(w_self_t[piece, :], mixed[:, window])).T
        latents_out[i] = turned[pl.ds(pl.multiple_of(frame * share, share), share), :].astype(jnp.bfloat16)

    loop(items, latents_item)
    for copy in saves:
        copy.wait()
    for copy in pending.values():
        if copy is not None:
            copy.wait()


def forward(
    frames, pieces, tokens, skip, latent_init, tok_gain, query_gain, mlp_gain, self_gain,
    w_query, w_keyval, w_out, w_up, w_down, w_self_qkv, w_self_out, grad_out,
):
    items, rows, width = tokens.shape
    latents = latent_init.shape[0]
    hidden = w_up.shape[1]
    own = width // frames
    columns = items * latents
    mid_rows = 4 * width // pieces
    bf16, f32 = jnp.bfloat16, jnp.float32
    vmem = pl.BlockSpec(memory_space=pltpu.VMEM)
    anywhere = pl.BlockSpec(memory_space=pl.ANY)
    dma = pltpu.SemaphoreType.DMA
    peers = max(frames - 1, 1)
    return pl.pallas_call(
        functools.partial(forward_kernel, frames, 2 if items % 2 == 0 else 1),
        out_shape=(
            jax.ShapeDtypeStruct((items, 2 * width, rows), bf16),
            jax.ShapeDtypeStruct((items, latents, LANES), f32),
            jax.ShapeDtypeStruct((latents, width), bf16),
            jax.ShapeDtypeStruct((pieces, mid_rows, own), f32),
            jax.ShapeDtypeStruct((items, latents // frames, width), bf16),
            jax.ShapeDtypeStruct((hidden, columns), bf16),
            jax.ShapeDtypeStruct((hidden, columns), f32),
            jax.ShapeDtypeStruct((width, columns), bf16),
            jax.ShapeDtypeStruct((width, columns), f32),
            jax.ShapeDtypeStruct((width, columns), f32),
            jax.ShapeDtypeStruct((width, columns), bf16),
            jax.ShapeDtypeStruct((width, columns), bf16),
            jax.ShapeDtypeStruct((width, columns), f32),
            jax.ShapeDtypeStruct((3 * width, columns), bf16),
            jax.ShapeDtypeStruct((peers, items if frames > 2 else 1, width + 32, latents), f32),
        ),
        in_specs=[anywhere, pl.BlockSpec(memory_space=pltpu.SMEM)] + [vmem] * 5 + [anywhere] * 7 + [vmem],
        out_specs=(anywhere, vmem, vmem, anywhere, vmem) + (anywhere,) * 10,
        scratch_shapes=[
            pltpu.VMEM((2, rows, width), bf16),
            pltpu.VMEM((width, rows), bf16),
            pltpu.VMEM((HEADS, latents, width // HEADS), bf16),
            pltpu.VMEM((items, width + 32, latents), f32),
            pltpu.VMEM((peers, 1 if frames > 2 else items, width + 32, latents), f32),
        ]
        + [pltpu.VMEM((width, width), bf16)] * 4
        + [
            pltpu.VMEM((width, 3 * width), bf16),
            pltpu.VMEM((3 * width, width), bf16),
            pltpu.VMEM((hidden, width), bf16),
            pltpu.VMEM((width, hidden), bf16),
            pltpu.VMEM((width, columns), bf16),
            pltpu.VMEM((width, columns), f32),
            pltpu.VMEM((width, columns), bf16),
            pltpu.VMEM((hidden, max(columns, rows)), bf16),
            pltpu.VMEM((hidden, columns), f32),
            pltpu.VMEM((width, columns), f32),
            pltpu.VMEM((width, columns), bf16),
            pltpu.VMEM((hidden, columns), bf16),
            pltpu.VMEM((width, columns), bf16),
            pltpu.VMEM((width, columns), bf16),
            pltpu.VMEM((width, columns), bf16),
            pltpu.VMEM((3 * width, columns), bf16),
            pltpu.VMEM((width, columns), f32),
            pltpu.VMEM((latents, width), f32),
            pltpu.VMEM((width, LANES), f32),
            pltpu.VMEM((width, LANES), f32),
            pltpu.VMEM((width, LANES), f32),
            pltpu.VMEM((2, width, own), f32),
            dma((2,)), dma((2,)), dma((peers, items)), dma((peers, items)), dma((9,)), dma((2,)), dma, dma((9,)),
        ],
        compiler_params=pltpu.CompilerParams(collective_id=1, has_side_effects=True, vmem_limit_bytes=62 * 2**20),
        name="forward",
    )(
        tokens, skip, latent_init, tok_gain, query_gain, mlp_gain, self_gain,
        w_query, w_keyval, w_out, w_up, w_down, w_self_qkv, w_self_out, grad_out,
    )


def add_into(target, parts, rows):
    step = next(size for size in (96, 80, 64, 60, 48, 40, 24, 16, 8) if rows % size == 0 and size % 8 == 0)

    def body(index):
        window = window_at(index, step)
        total = parts[0][window]
        for part in parts[1:]:
            total = total + part[window]
        target[window] = total

    loop(rows // step, body)


def gelu_slope(value):
    slope = (2 / jnp.pi) ** 0.5
    square = value * value
    tanh = jnp.tanh(value * (slope + (slope * 0.044715) * square))
    half = 0.5 + 0.5 * tanh
    bend = value * (2 * slope + (6 * slope * 0.044715) * square)
    return half + half * (1.0 - half) * bend


def nn_exact(left, right):
    total = jnp.zeros((left.shape[0], right.shape[1]), jnp.float32)
    rest = right
    for _ in range(3):
        part = rest.astype(jnp.bfloat16)
        total = total + nn(left, part)
        rest = rest - part.astype(jnp.float32)
    return total


def backward_kernel(
    chips, frames, streams,
    loc_a, tokens_ref, kv_ref, act_ref, hidden_ref, mlp_ref, cross_ref, after_ref, cot_ref, heard_ref, heard_f32_ref, dtri_ref,
    w_qkv_ref, w_up_ref, w_down_ref, w_out_ref, w_keyval_ref, w_query_ref,
    skip_ref, log_ref, query_ref, latent_ref, tok_gain_ref, query_gain_ref, mlp_gain_ref, self_gain_ref,
    *rest,
):
    outs, rest = rest[:12], rest[12:]
    sums, token_out, (loc_b, loc_c, loc_d), sibs = outs[:4], outs[4], outs[5:8], outs[8:12]
    locs = (loc_a, loc_b, loc_c, loc_d)
    (
        flat, tall, w_square, act, pool, mlp_in, heard, cotangent, branch, d_heard, queries, queries_t, token_stage,
        hidden_stage, after, cross, rows_f32, incoming, stage, small_stage, d_query, gain_sum, tok_gain, mlp_gain, self_gain,
        d_latent, gain_cols, delta, inverse, y_mine, y_sib, ky,
    ), rest = rest[:32], rest[32:]
    n = len(streams)
    mines, sib_slots, rxs = rest[:n], rest[n : 2 * n], rest[2 * n : 3 * n]
    (
        pair_send, pair_recv, ld_sem, ls_sem, rs_send, rs_recv, ag_send, ag_recv, share_send, share_recv, own_sem, krs_send, krs_recv,
        kpair_send, kpair_recv, y_send, y_recv, y_sem, in_sem, tok_sem, kv_sem, out_sem, hidden_sem, stage_sem, small_sem,
    ) = rest[3 * n :]

    item_index = lax.axis_index("items")
    frame = lax.axis_index("frames")
    core = lax.rem(item_index, 2)
    chip = item_index // 2
    column = lax.rem(chip, 2)
    line = chip // 2
    place = line + column * (chips - 1 - 2 * line)
    way = 1 - 2 * core
    count, rows, width = tokens_ref.shape
    latents = latent_ref.shape[0]
    hidden = hidden_ref.shape[0]
    head = width // HEADS
    factor = head ** -0.5
    own = width // frames
    pieces = 2 * chips
    per_piece = width // pieces
    kv_rows = loc_d.shape[3]
    last = n - 1

    def device_at(position):
        position = lax.rem(position + 2 * chips, chips)
        far = position // (chips // 2)
        return (2 * (position + far * (chips - 1 - 2 * position)) + far) * 2 + core

    right, left = device_at(place + way), device_at(place - way)
    sibling = item_index + way

    def chunk(offset):
        return lax.rem(place + way * offset + 4 * chips, chips)

    def sib_chunk(offset):
        return lax.rem(place - way * offset + 4 * chips, chips)

    barrier = pltpu.get_barrier_semaphore()
    for peer in (left, right, sibling):
        pl.semaphore_signal(barrier, inc=1, device_id=(peer, frame), device_id_type=MESH)
    for hop in range(1, frames):
        pl.semaphore_signal(barrier, inc=1, device_id=(item_index, lax.rem(frame + hop, frames)), device_id_type=MESH)

    def remote(src, dst, send, recv, peer):
        return pltpu.make_async_remote_copy(
            src_ref=src, dst_ref=dst, send_sem=send, recv_sem=recv, device_id=peer, device_id_type=MESH
        )

    def pair(source, k):
        return remote(
            locs[source].at[1 - core, k], sibs[source].at[k], pair_send.at[source, k], pair_recv.at[source, k], (sibling, frame)
        )

    def frame_at(hop):
        return lax.rem(frame + hop, frames)

    def pair_frame(hop, k):
        f = frame_at(hop)
        return remote(
            loc_d.at[f, 1 - core, k], sibs[3].at[f, k], kpair_send.at[hop - 1, k], kpair_recv.at[hop - 1, k], (sibling, frame)
        )

    def start_pairs(source):
        loop(chips, lambda index: pair(source, sib_chunk(-index)).start())

    def part_of(j):
        source, start, size = streams[j]
        return source, pl.ds(start, size)

    def load_mine(j, k, slot):
        source, part = part_of(j)
        return pltpu.make_async_copy(locs[source].at[core, k, part], mines[j].at[slot], ld_sem.at[j, slot])

    def load_sib(j, k, slot):
        source, part = part_of(j)
        return pltpu.make_async_copy(sibs[source].at[k, part], sib_slots[j].at[slot], ls_sem.at[j, slot])

    def ring(j, k, slot):
        return remote(mines[j].at[slot], rxs[j].at[k], rs_send.at[j, slot], rs_recv.at[j, k], (right, frame))

    def own_at(j, k):
        source, part = part_of(j)
        return sums[source].at[core, k, part]

    def gather(j, k, src):
        return remote(src, own_at(j, k), ag_send.at[j, k], ag_recv.at[j, k], (right, frame))

    def share(j, k, src):
        return remote(src, own_at(j, k), share_send.at[j, k], share_recv.at[j, k], (sibling, frame))

    def share_from(j, k):
        source, part = part_of(j)
        return remote(mines[j].at[0], sums[source].at[1 - core, k, part], share_send.at[j, k], share_recv.at[j, k], (sibling, frame))

    def keep(j, k, slot):
        return pltpu.make_async_copy(mines[j].at[slot], own_at(j, k), own_sem.at[j])

    def across(hop, k):
        other = lax.rem(frame + hop, frames)
        return remote(y_mine.at[k], ky.at[hop - 1, k], y_send.at[hop - 1, k], y_recv.at[hop - 1, k], (item_index, other))

    def prefetch(j, op):
        k, slot = chunk(-op), lax.rem(op, 2)
        source, part = part_of(j)
        pair(source, k).wait_recv()
        load_mine(j, k, slot).start()
        load_sib(j, k, slot).start()

    def when(condition, body):
        if isinstance(condition, (bool, int)):
            if condition:
                body()
        else:
            pl.when(condition)(body)

    def tick(j, op):
        source, part = part_of(j)
        size = streams[j][2]
        slot = lax.rem(op, 2)

        def reduce_op():
            k = chunk(-op)
            load_mine(j, k, slot).wait()
            load_sib(j, k, slot).wait()
            parts = [mines[j].at[slot], sib_slots[j].at[slot]]
            if not (isinstance(op, int) and op == 0):
                ring(j, k, slot).wait_recv()
                parts.append(rxs[j].at[k])
            add_into(mines[j].at[slot], parts, size)

            def pass_on():
                ring(j, k, slot).start()
                if isinstance(op, int) and op == 0:
                    prefetch(j, op + 1)
                else:
                    ring(j, k, 1 - slot).wait_send()
                    prefetch(j, op + 1)

            def finish():
                gather(j, k, mines[j].at[slot]).start()
                share(j, k, mines[j].at[slot]).start()
                keep(j, k, slot).start()

            when(op < chips - 1, pass_on)
            when(op == chips - 1, finish)

        def gather_op():
            k = chunk(-op)
            gather(j, k, mines[j].at[0]).wait_recv()

            def forward_on():
                gather(j, k, own_at(j, k)).start()

            when(op < 2 * chips - 2, forward_on)
            share(j, k, own_at(j, k)).start()

        when(op < chips, reduce_op)
        when((op >= chips) & (op < 2 * chips - 1) if not isinstance(op, int) else chips <= op < 2 * chips - 1, gather_op)

    ahead = chips // 2
    behind = chips - 1 - ahead
    kmine, krx = mines[last], rxs[last]

    def kv_ring(flow, k, arriving_own):
        peer = (right, left)[flow]
        slot = chips if flow == 1 and arriving_own else k
        return remote(kmine.at[k], krx.at[slot], krs_send.at[flow, k], krs_recv.at[flow, k], (peer, frame))

    def kv_gather(flow, k, src):
        return remote(src, sums[3].at[core, k], ag_send.at[last + flow, k], ag_recv.at[last + flow, k], ((right, left)[flow], frame))

    def kv_total(k, arrived):
        parts = [kmine.at[k], y_sib.at[k]]
        for hop in range(1, frames):
            across(hop, k).wait_recv()
            parts.append(ky.at[hop - 1, k])
        add_into(kmine.at[k], parts + arrived, kv_rows)

    def kv_tick(op):
        if op < ahead:
            for flow, length in ((0, ahead), (1, behind)):
                distance = length - op
                if distance < 1:
                    continue
                k = chunk(distance if flow == 0 else -distance)
                arrived = []
                if op > 0:
                    kv_ring(flow, k, False).wait_recv()
                    arrived.append(krx.at[k])
                kv_total(k, arrived)
                kv_ring(flow, k, distance == 1).start()
        elif op == ahead:
            k = chunk(0)
            kv_ring(0, k, False).wait_recv()
            kv_ring(1, k, True).wait_recv()
            kv_total(k, [krx.at[k], krx.at[chips]])
            for flow in range(2):
                kv_gather(flow, k, kmine.at[k]).start()
            share(last, k, kmine.at[k]).start()
            keep(last, k, k).start()
        else:
            step = op - ahead
            for flow, length in ((0, behind), (1, ahead)):
                if step > length:
                    continue
                k = chunk(-step if flow == 0 else step)
                kv_gather(flow, k, kmine.at[0]).wait_recv()
                if step < length:
                    kv_gather(flow, k, sums[3].at[core, k]).start()
                share(last, k, sums[3].at[core, k]).start()

    kv_order = [0] + [offset for step in range(1, ahead + 1) for offset in ((step, -step) if step <= behind else (step,))]
    kv_order = kv_order[::-1]

    third = 3 * width
    names = [
        (dtri_ref, pool.at[pl.ds(hidden, third), :]),
        (w_qkv_ref, flat.at[:, pl.ds(0, third)]),
        (after_ref, after),
        (cot_ref, cotangent),
        (act_ref, act),
        (w_down_ref, tall),
        (mlp_ref, mlp_in),
        (cross_ref, cross),
        (heard_ref, heard),
        (w_out_ref, w_square),
        (w_up_ref, flat),
        (heard_f32_ref, cross),
        (w_query_ref, w_square),
        (w_keyval_ref.at[:, pl.ds(0, width)], tall.at[pl.ds(2 * rows, width), :]),
        (w_keyval_ref.at[:, pl.ds(width, width)], tall.at[pl.ds(2 * rows + width, width), :]),
    ]
    copies = [pltpu.make_async_copy(src, dst, in_sem.at[at]) for at, (src, dst) in enumerate(names)]
    (
        get_dtri, get_qkv, get_after, get_cot, get_act, get_down, get_mlp, get_cross, get_heard, get_out, get_up, get_heard_f32,
        get_query, get_keys, get_values,
    ) = copies

    def load_hidden(b):
        slot = lax.rem(b, 4)
        return pltpu.make_async_copy(hidden_ref.at[window_at(b, BLOCK), :], hidden_stage.at[slot], hidden_sem.at[slot])

    def tok_load(i):
        slot = lax.rem(i, 2)
        return pltpu.make_async_copy(tokens_ref.at[i], tall.at[window_at(slot, rows), :], tok_sem.at[slot])

    def kv_load(i):
        slot = lax.rem(i, 2)
        return pltpu.make_async_copy(kv_ref.at[i], act.at[window_at(slot, 2 * width), pl.ds(0, rows)], kv_sem.at[slot])

    def token_save(i, b):
        slot = lax.rem(b, 2)
        return pltpu.make_async_copy(token_stage.at[slot], token_out.at[i, window_at(b, LANES), :], out_sem.at[slot])

    for copy in (get_dtri, get_qkv, get_after, get_cot, get_act, get_down, get_mlp, get_cross, get_heard, get_out):
        copy.start()
    for b in range(3):
        load_hidden(b).start()
    pl.semaphore_wait(barrier, 3 + frames - 1)
    start_pairs(0)
    tok_gain[...] = gain_columns(tok_gain_ref)
    mlp_gain[...] = gain_columns(mlp_gain_ref)
    self_gain[...] = gain_columns(self_gain_ref)
    scaled = query_ref[...] * jnp.bfloat16(factor)
    for h in range(HEADS):
        queries[h] = scaled[:, h * head : (h + 1) * head]
    queries_t[...] = scaled.T
    d_query[...] = jnp.zeros_like(d_query)
    gain_sum[...] = jnp.zeros_like(gain_sum)
    gain_cols[...] = jnp.zeros_like(gain_cols)
    d_latent[...] = jnp.zeros_like(d_latent)
    prefetch(0, 0)

    done = [0] * n

    def advance(*which):
        for j in which:
            if done[j] < 2 * chips - 1:
                tick(j, done[j])
                done[j] += 1

    def each_item(body):
        loop(count, lambda i: body(i, window_at(i, latents)))

    def each_block(first, total, body):
        loop(total // BLOCK, lambda b: body(b + first, window_at(b + first, BLOCK)))

    pending = {}

    def put(target, left, right):
        slot = len(pending) % stage.shape[0]
        for key in [key for key in pending if key % stage.shape[0] == slot and pending[key] is not None]:
            pending[key].wait()
            pending[key] = None
        view = stage.at[slot]
        view[...] = nt(left[...], right[...])
        put_start(target, slot)

    def put_start(target, slot):
        copy = pltpu.make_async_copy(stage.at[slot].reshape(*target.shape), target, stage_sem.at[slot])
        copy.start()
        pending[len(pending)] = copy

    def put_done():
        for key in pending:
            if pending[key] is not None:
                pending[key].wait()
                pending[key] = None

    my_columns = pl.multiple_of(frame * own, own)
    lane = lax.broadcasted_iota(jnp.int32, (width, LANES), 1)

    get_dtri.wait()
    get_qkv.wait()
    advance(0)

    def self_block(b, window):
        incoming[window, :] = nn(flat[window, pl.ds(0, third)], pool[pl.ds(hidden, third), :])

    each_block(0, width, self_block)
    get_up.start()
    get_after.wait()
    get_cot.wait()

    def self_back(i, window):
        normed, inverse_row = norm_down(after[:, window])
        arriving = incoming[:, window]
        gain_cols[...] += jnp.where(lane == 1, jnp.sum(arriving * normed, axis=-1, keepdims=True), 0.0)
        d_after = cotangent[:, window].astype(jnp.float32) + norm_down_back(arriving, normed, inverse_row, self_gain[...])
        branch[:, window] = d_after.astype(jnp.bfloat16)
        rows_f32[:, window] = d_after

    each_item(self_back)
    advance(0)
    get_act.wait()
    groups = hidden // width
    for group in range(groups):
        size = hidden // pieces
        span = pieces // groups
        target = loc_b.at[group * span // chips, pl.ds(group * span % chips, span)] if span <= chips else None
        put(target, act.at[pl.ds(group * width, width), :], branch.at[pl.ds(my_columns, own), :])
    put_done()
    start_pairs(1)
    kv_load(0).start()
    get_down.wait()

    def hidden_block(b, window):
        load_hidden(b).wait()

        @pl.when(b + 3 < hidden // BLOCK)
        def _():
            load_hidden(b + 3).start()

        d_act = nn(tall[window, :], branch[...])
        pool[window, :] = (d_act * gelu_slope(hidden_stage[lax.rem(b, 4)])).astype(jnp.bfloat16)

    half = hidden // BLOCK // 2
    each_block(0, half * BLOCK, hidden_block)
    advance(0)
    prefetch(1, 0)
    each_block(half, hidden - half * BLOCK, hidden_block)
    advance(1)
    tok_load(0).start()
    get_keys.start()
    get_values.start()
    get_mlp.wait()
    advance(0)
    for part in range(groups):
        source = pool.at[pl.ds(frame * (hidden // frames) + part * own, own), :]
        put(loc_c.at[:, :, pl.ds(part * per_piece, per_piece)], mlp_in, source)
        if part == groups // 2 - 1:
            advance(1)
    get_up.wait()
    advance(0)

    def mlp_block(b, window):
        incoming[window, :] = nn(flat[window, :], pool[pl.ds(0, hidden), :])

    each_block(0, width, mlp_block)
    get_cross.wait()
    advance(1)

    def mlp_back(i, window):
        normed, inverse_row = norm_down(cross[:, window])
        arriving = incoming[:, window]
        gain_cols[...] += jnp.where(lane == 0, jnp.sum(arriving * normed, axis=-1, keepdims=True), 0.0)
        d_cross = rows_f32[:, window] + norm_down_back(arriving, normed, inverse_row, mlp_gain[...])
        d_latent[...] += d_cross.T
        keep_item = (1 - skip_ref[i]).astype(jnp.float32)
        branch[:, window] = (keep_item * d_cross).astype(jnp.bfloat16)

    each_item(mlp_back)
    get_heard_f32.start()
    get_heard.wait()
    advance(0)
    put(loc_c.at[:, :, pl.ds(groups * per_piece, per_piece)], heard, branch.at[pl.ds(my_columns, own), :])
    put_done()
    start_pairs(2)
    get_out.wait()

    def heard_block(b, window):
        d_heard[window, :] = nn(w_square[window, :], branch[...]).astype(jnp.bfloat16)

    each_block(0, width, heard_block)
    get_query.start()
    get_heard_f32.wait()
    advance(1)

    def delta_item(i, window):
        product = d_heard[:, window].astype(jnp.float32) * cross[:, window]
        sums_of = jnp.sum(product.reshape(HEADS, head, latents), axis=1)
        padded = jnp.concatenate([sums_of, jnp.zeros((LANES - HEADS, latents), jnp.float32)], axis=0)
        delta[i] = padded.T

    each_item(delta_item)
    prefetch(2, 0)
    get_keys.wait()
    get_values.wait()
    advance(0, 2)

    def attend(i, heads):
        base = pl.multiple_of(lax.rem(i, 2) * 2 * width, 2 * width)
        target = pl.multiple_of(i * 2 * width, 2 * width)
        latent_window = window_at(i, latents)
        for h in heads:
            keys_at = pl.ds(h * head, head)
            keys = act[pl.ds(base + h * head, head), pl.ds(0, rows)]
            values = act[pl.ds(base + width + h * head, head), pl.ds(0, rows)]
            d_heard_t = d_heard[keys_at, latent_window]
            probs = jnp.exp(nn(queries[h], keys) - log_ref[i, :, h : h + 1])
            d_probs = nn(d_heard_t.T, values)
            d_scores = (probs * (d_probs - delta[i, :, h : h + 1])).astype(jnp.bfloat16)
            pool[pl.ds(target + h * head, head), pl.ds(0, rows)] = nn(queries_t[keys_at, :], d_scores).astype(jnp.bfloat16)
            pool[pl.ds(target + width + h * head, head), pl.ds(0, rows)] = nn(d_heard_t, probs.astype(jnp.bfloat16)).astype(
                jnp.bfloat16
            )
            d_query[keys_at, :] += nt(keys, d_scores)

    def norm_tokens(i):
        tok_load(i).wait()
        base = pl.multiple_of(lax.rem(i, 2) * rows, rows)

        def norm_block(b):
            window = window_at(b, LANES)
            columns = tall[pl.ds(base + b * LANES, LANES), :].T.astype(jnp.float32)
            block, inverse_row = norm_down(columns)
            after[:, window] = block
            inverse[:, window] = jnp.broadcast_to(inverse_row, (8, LANES))
            flat[:, pl.ds(pl.multiple_of(i * rows + b * LANES, LANES), LANES)] = (block * tok_gain[...]).astype(jnp.bfloat16)

        loop(rows // LANES, norm_block)

    def token_back(i):
        base = pl.multiple_of(i * 2 * width, 2 * width)

        def product(b):
            window = window_at(b, BLOCK)
            keys_w = tall[pl.ds(pl.multiple_of(2 * rows + b * BLOCK, BLOCK), BLOCK), :]
            values_w = tall[pl.ds(pl.multiple_of(2 * rows + width + b * BLOCK, BLOCK), BLOCK), :]
            incoming[window, :] = nn(keys_w, pool[pl.ds(base, width), pl.ds(0, rows)]) + nn(
                values_w, pool[pl.ds(base + width, width), pl.ds(0, rows)]
            )

        loop(width // BLOCK, product)

        def back_block(b):
            window = window_at(b, LANES)
            block = after[:, window]
            arriving = incoming[:, window]
            gain_sum[...] += arriving * block
            result = norm_down_back(arriving, block, inverse[pl.ds(0, 1), window], tok_gain[...])

            @pl.when((i > 0) | (b > 1))
            def _():
                token_save(i, b).wait()

            token_stage[lax.rem(b, 2)] = result.T.astype(jnp.bfloat16)
            token_save(i, b).start()

        loop(rows // LANES, back_block)

    base_ops = list(done)

    def one_item(i):
        kv_load(i).wait()

        @pl.when(i + 1 < count)
        def _():
            kv_load(i + 1).start()
            tok_load(i + 1).start()

        norm_tokens(i)
        attend(i, range(HEADS // 2))
        tick(1, base_ops[1] + i)
        attend(i, range(HEADS // 2, HEADS))
        tick(2, base_ops[2] + i)
        token_back(i)

        tick(0, base_ops[0] + i)

    loop(count, one_item)
    for j in range(last):
        done[j] = base_ops[j] + count

    small = 2 * latents // pieces
    get_query.wait()
    d_query[...] = d_query[...] * factor
    q_total = d_query[...]
    q_normed, q_inverse = norm_down(latent_ref[...].astype(jnp.float32).T)
    q_incoming = nn_exact(w_square[...], q_total)
    all_gains = gain_cols[...]
    all_gains = jnp.where(lane == 2, jnp.sum(gain_sum[...], axis=-1, keepdims=True), all_gains)
    all_gains = jnp.where(lane == 3, jnp.sum(q_incoming * q_normed, axis=-1, keepdims=True), all_gains)
    gain_rows = all_gains.T[:8]
    latent_rows = norm_down_back(q_incoming, q_normed, q_inverse, gain_columns(query_gain_ref)).T
    query_rows = q_total.T
    for f in range(frames):
        mask = (frame == f).astype(jnp.float32)
        mine_columns = slice(f * own, (f + 1) * own)
        latent_part = latent_rows[:, mine_columns] + mask * d_latent[:, mine_columns]
        both = jnp.concatenate([query_rows[:, mine_columns], latent_part], axis=0)
        small_stage[f, :, :, pl.ds(0, small), :] = both.reshape(2, chips, small, own)
        row = lax.broadcasted_iota(jnp.int32, (8, own), 0)
        gain_block = gain_rows[:, mine_columns] * jnp.where(row < 2, mask, 1.0)
        small_stage[f, :, :, pl.ds(small, 8), :] = jnp.zeros((2, chips, 8, own), jnp.float32)
        small_stage[f, 0, 0, pl.ds(small, 8), :] = gain_block
    put_small = pltpu.make_async_copy(small_stage, loc_d.at[:, :, :, pl.ds(2 * per_piece, small + 8)], small_sem)
    put_small.start()
    advance(1)
    for hop in range(1, frames + 1):
        f = frame_at(hop)
        for b in range(2):
            slot = len(pending) % stage.shape[0]
            for key in [key for key in pending if key % stage.shape[0] == slot and pending[key] is not None]:
                pending[key].wait()
                pending[key] = None
            first_row = pl.multiple_of((2 * f + b) * own, own)
            source = jnp.concatenate(
                [pool[pl.ds(i * 2 * width + first_row, own), pl.ds(0, rows)] for i in range(count)], axis=1
            )
            stage[slot] = nt(flat[:, pl.ds(0, count * rows)], source)
            put_start(loc_d.at[f, :, :, pl.ds(b * per_piece, per_piece)], slot)
        if hop == 1:
            put_small.wait()
        put_done()
        loop(chips, lambda index: pair_frame(hop, sib_chunk(-index)).start())
        if hop <= 2:
            advance(2 if hop == 1 else 0)
    advance(1)
    for hop in range(1, frames):
        other = frame_at(hop)
        if hop > 1:
            for k in range(chips):
                across(hop - 1, k).wait_send()
        for k in range(chips):
            pair_frame(hop, k).wait_recv()
        one = pltpu.make_async_copy(loc_d.at[other, core], y_mine, y_sem.at[0])
        two = pltpu.make_async_copy(sibs[3].at[other], y_sib, y_sem.at[1])
        one.start()
        two.start()
        one.wait()
        two.wait()

        for offset in kv_order:
            k = chunk(offset)
            add_into(y_mine.at[k], [y_mine.at[k], y_sib.at[k]], kv_rows)
            across(hop, k).start()
    advance(2)
    for k in range(chips):
        pair_frame(frames, k).wait_recv()
    one = pltpu.make_async_copy(loc_d.at[frame, core], kmine, y_sem.at[0])
    two = pltpu.make_async_copy(sibs[3].at[frame], y_sib, y_sem.at[1])
    one.start()
    two.start()
    advance(0)
    one.wait()
    two.wait()
    total = 2 * chips - 1
    others = sum(total - done[j] for j in range(last))
    turns, taken = chips + 1, 0
    for turn in range(turns):
        kv_tick(turn)
        while taken * turns < (turn + 1) * others:
            j = max(range(last), key=lambda j: (total - done[j]) * (streams[j][2] + 160))
            advance(j)
            taken += 1

    def drain(k):
        for source in range(3):
            pair(source, k).wait_send()
        for hop in range(1, frames + 1):
            pair_frame(hop, k).wait_send()
        for j in range(n):
            share(j, k, mines[j].at[0]).wait_send()
            share_from(j, k).wait_recv()
        if frames > 1:
            across(frames - 1, k).wait_send()

    loop(chips, drain)

    def drain_ring(step):
        for j in range(last):
            gather(j, chunk(1 - step), mines[j].at[0]).wait_send()

    loop(chips - 1, drain_ring)
    for j in range(last):
        ring(j, 0, (chips - 2) % 2).wait_send()
        keep(j, chunk(1), (chips - 1) % 2).wait()
    keep(last, chunk(0), 0).wait()
    for distance in range(1, ahead + 1):
        kv_ring(0, chunk(distance), False).wait_send()
        kv_gather(1, chunk(distance - 1), kmine.at[0]).wait_send()
    for distance in range(1, behind + 1):
        kv_ring(1, chunk(-distance), False).wait_send()
        kv_gather(0, chunk(1 - distance), kmine.at[0]).wait_send()
    for b in range(2):
        token_save(0, b).wait()


def backward(
    frames, first, tokens, kv, act, hidden, mlp_in, cross, after, cotangent, heard, heard_f32, d_triple, skip, log_total, query,
    latent_init, tok_gain, query_gain, mlp_gain, self_gain, w_query, w_keyval, w_out, w_up, w_down, w_self_qkv,
):
    chips, first_rows, own = first.shape[1:]
    items, rows, width = tokens.shape
    latents = latent_init.shape[0]
    hidden_width, columns = hidden.shape
    pieces = 2 * chips
    per_piece = width // pieces
    kv_rows = 2 * per_piece + 2 * latents // pieces + 8
    source_rows = (first_rows, hidden_width // pieces, per_piece * (hidden_width // width + 1), kv_rows)
    streams = tuple((source, 0, size) for source, size in enumerate(source_rows))
    n = len(streams)
    dma = pltpu.SemaphoreType.DMA
    peers = max(frames - 1, 1)
    f32, bf16 = jnp.float32, jnp.bfloat16
    vmem = pl.BlockSpec(memory_space=pltpu.VMEM)
    anywhere = pl.BlockSpec(memory_space=pl.ANY)
    wide = max(columns, rows)
    scratch = [
        pltpu.VMEM((width, max(hidden_width, items * rows)), bf16),
        pltpu.VMEM((max(hidden_width, 2 * rows + 2 * width), width), bf16),
        pltpu.VMEM((width, width), bf16),
        pltpu.VMEM((max(hidden_width, 4 * width), wide), bf16),
        pltpu.VMEM((max(hidden_width + 3 * width, items * 2 * width), wide), bf16),
        pltpu.VMEM((width, columns), bf16),
        pltpu.VMEM((width, columns), bf16),
        pltpu.VMEM((width, columns), bf16),
        pltpu.VMEM((width, columns), bf16),
        pltpu.VMEM((width, columns), bf16),
        pltpu.VMEM((HEADS, latents, width // HEADS), bf16),
        pltpu.VMEM((width, latents), bf16),
        pltpu.VMEM((2, LANES, width), bf16),
        pltpu.VMEM((4, BLOCK, columns), f32),
        pltpu.VMEM((width, wide), f32),
        pltpu.VMEM((width, columns), f32),
        pltpu.VMEM((width, columns), f32),
        pltpu.VMEM((width, wide), f32),
        pltpu.VMEM((2, width, own), f32),
        pltpu.VMEM((frames, 2, chips, 2 * latents // pieces + 8, own), f32),
        pltpu.VMEM((width, latents), f32),
        pltpu.VMEM((width, LANES), f32),
        pltpu.VMEM((width, LANES), f32),
        pltpu.VMEM((width, LANES), f32),
        pltpu.VMEM((width, LANES), f32),
        pltpu.VMEM((latents, width), f32),
        pltpu.VMEM((width, LANES), f32),
        pltpu.VMEM((items, latents, LANES), f32),
        pltpu.VMEM((8, rows), f32),
        pltpu.VMEM((chips, kv_rows, own), f32),
        pltpu.VMEM((chips, kv_rows, own), f32),
        pltpu.VMEM((peers, chips, kv_rows, own), f32),
    ]
    scratch += [pltpu.VMEM((2 if source < 3 else chips, size, own), f32) for source, _, size in streams]
    scratch += [pltpu.VMEM((2, size if source < 3 else 8, own), f32) for source, _, size in streams]
    scratch += [pltpu.VMEM((chips + source // 3, size, own), f32) for source, _, size in streams]
    scratch += [
        dma((3, chips)), dma((3, chips)), dma((n, 2)), dma((n, 2)), dma((n, 2)), dma((n, chips)),
        dma((n + 1, chips)), dma((n + 1, chips)), dma((n, chips)), dma((n, chips)), dma((n,)), dma((2, chips)), dma((2, chips)),
        dma((frames, chips)), dma((frames, chips)), dma((peers, chips)), dma((peers, chips)), dma((2,)), dma((15,)), dma((2,)), dma((2,)), dma((2,)), dma((4,)), dma((2,)), dma,
    ]
    shape = jax.ShapeDtypeStruct
    summed = tuple(shape((2, chips, size, own), f32) for size in source_rows)
    return pl.pallas_call(
        functools.partial(backward_kernel, chips, frames, streams),
        out_shape=summed
        + (shape(tokens.shape, bf16),)
        + summed[1:3]
        + (shape((frames, 2, chips, kv_rows, own), f32),)
        + tuple(shape((chips, size, own), f32) for size in source_rows[:3])
        + (shape((frames, chips, kv_rows, own), f32),),
        in_specs=[anywhere] * 18 + [pl.BlockSpec(memory_space=pltpu.SMEM)] + [vmem] * 7,
        out_specs=(anywhere,) * 12,
        scratch_shapes=scratch,
        compiler_params=pltpu.CompilerParams(collective_id=0, has_side_effects=True, vmem_limit_bytes=62 * 2**20),
        name="backward",
    )(
        first, tokens, kv, act, hidden, mlp_in, cross, after, cotangent, heard, heard_f32, d_triple,
        w_self_qkv, w_up, w_down, w_out, w_keyval, w_query, skip, log_total, query, latent_init,
        tok_gain, query_gain, mlp_gain, self_gain,
    )


def unpack_kernel(first_ref, second_ref, third_ref, kv_ref, latent_ref, qgain_ref, *rest):
    outs, (query_out, *gain_outs), (blocks, total, tail, in_sem, out_sem) = rest[:7], rest[7:12], rest[12:]
    pieces, _, own = first_ref.shape
    loads, stores = [], []

    def place(source, offset, out):
        rows, columns = out.shape
        size = rows // pieces
        view = out.reshape(pieces, size, columns)
        for b in range(columns // own):
            at = len(loads)
            area = blocks.at[pl.ds(starts[at], pieces * size), :].reshape(pieces, size, own)
            loads.append(pltpu.make_async_copy(source.at[:, pl.ds(offset + b * size, size), :], area, in_sem.at[at]))
            stores.append(pltpu.make_async_copy(area, view.at[:, :, pl.ds(b * own, own)], out_sem.at[at]))
        return offset + size * columns // own

    starts, start = [], 0
    for out in outs[:6]:
        rows, columns = out.shape
        for b in range(columns // own):
            starts.append(start)
            start += rows
    place(first_ref, place(first_ref, 0, outs[0]), outs[1])
    place(second_ref, 0, outs[2])
    place(third_ref, place(third_ref, 0, outs[3]), outs[4])
    offset = place(kv_ref, 0, outs[5])
    latents = outs[6].shape[0]
    small = 2 * latents // pieces
    half = pieces // 2
    query = pltpu.make_async_copy(kv_ref.at[:, pl.ds(offset, small), :], total, in_sem.at[len(loads)])
    gains = pltpu.make_async_copy(kv_ref.at[0, pl.ds(offset + small, 8), :], tail, in_sem.at[len(loads) + 1])
    query.start()
    gains.start()
    for copy in loads:
        copy.start()
    normed, _ = norm_down(latent_ref[...].astype(jnp.float32).T)
    query_in = (normed * gain_columns(qgain_ref)).astype(jnp.bfloat16)
    query.wait()
    query_out[...] = nn_exact(query_in, total[pl.ds(0, half)].reshape(latents, own))
    outs[6][...] = total[pl.ds(half, half)].reshape(latents, own)
    gains.wait()
    for out, row in zip(gain_outs, (2, 3, 0, 1)):
        out[...] = tail[row]
    for load, store in zip(loads, stores):
        load.wait()
        store.start()
    for store in stores:
        store.wait()


def unpack_all(sums, latent_init, query_gain, shapes):
    f32 = jnp.float32
    own = sums[0].shape[-1]
    latents, width = latent_init.shape
    pieces = sums[0].shape[0]
    vmem = pl.BlockSpec(memory_space=pltpu.VMEM)
    anywhere = pl.BlockSpec(memory_space=pl.ANY)
    count = sum(columns // own for _, columns in shapes)
    size = sum(rows * columns // own for rows, columns in shapes)
    return pl.pallas_call(
        unpack_kernel,
        out_shape=tuple(jax.ShapeDtypeStruct(shape, f32) for shape in shapes) + (
            jax.ShapeDtypeStruct((latents, own), f32), jax.ShapeDtypeStruct((width, own), f32))
        + (jax.ShapeDtypeStruct((own,), f32),) * 4,
        in_specs=[anywhere] * 4 + [vmem] * 2,
        out_specs=(anywhere,) * len(shapes) + (vmem,) * 6,
        scratch_shapes=[
            pltpu.VMEM((size, own), f32), pltpu.VMEM((pieces, 2 * latents // pieces, own), f32), pltpu.VMEM((8, own), f32),
            pltpu.SemaphoreType.DMA((count + 2,)), pltpu.SemaphoreType.DMA((count,)),
        ],
        compiler_params=pltpu.CompilerParams(vmem_limit_bytes=60 * 2**20),
        name="unpack_all",
    )(*sums, latent_init, query_gain)


def unpack(packed, rows, columns):
    pieces, _, width = packed.shape
    split = packed.reshape(pieces, columns // width, rows // pieces, width)
    return jnp.swapaxes(split, 1, 2).reshape(rows, columns)


def cut(packed, shapes):
    start, out = 0, []
    for rows, columns in shapes:
        count = rows * columns // packed.shape[-1] // packed.shape[0]
        out.append(unpack(packed[:, start : start + count], rows, columns))
        start += count
    return out


def shards(
    tokens,
    skip,
    latent_init,
    tok_gain,
    query_gain,
    mlp_gain,
    self_gain,
    w_query,
    w_keyval,
    w_out,
    w_up,
    w_down,
    w_self_qkv,
    w_self_out,
    grad_out,
):
    frames, pieces = lax.axis_size("frames"), lax.axis_size("items")
    latents, width = latent_init.shape
    hidden = w_up.shape[1]
    own = width // frames
    kv, log_total, query, first, out_latents, act, hidden_rows, mlp_in, cross, after, cotangent, heard, heard_f32, d_triple, _ = forward(
        frames, pieces, tokens, skip, latent_init, tok_gain, query_gain, mlp_gain, self_gain,
        w_query, w_keyval, w_out, w_up, w_down, w_self_qkv, w_self_out, grad_out,
    )
    *sums, token_grad = backward(
        frames, first.reshape((2, pieces // 2) + first.shape[1:]), tokens, kv, act, hidden_rows, mlp_in, cross, after, cotangent,
        heard, heard_f32, d_triple, skip, log_total, query, latent_init, tok_gain, query_gain, mlp_gain, self_gain,
        w_query, w_keyval, w_out, w_up, w_down, w_self_qkv,
    )[:5]
    sums = [array.reshape((pieces,) + array.shape[2:]) for array in sums]
    shapes = ((width, 3 * own), (width, own), (hidden, own), (width, hidden // frames), (width, own), (width, 2 * own))
    if own % LANES == 0:
        *grads, latent_grad, grad_query, gain_tok, gain_query, gain_mlp, gain_self = unpack_all(
            sums, latent_init, query_gain, shapes
        )
    else:
        grads = cut(sums[0], shapes[:2]) + cut(sums[1], shapes[2:3]) + cut(sums[2], shapes[3:5])
        keyval_sum, small = cut(sums[3], (shapes[5], (2 * latents, own)))
        grads.append(keyval_sum)
        latent_grad = small[latents:]
        normed, _ = norm_down(latent_init.astype(jnp.float32).T)
        query_in = (normed * query_gain[:, None]).astype(jnp.bfloat16)
        grad_query = jnp.dot(query_in.astype(jnp.float32), small[:latents], precision=lax.Precision.HIGHEST)
        gain_mlp, gain_self, gain_tok, gain_query = [sums[3][0, row - 8] for row in range(4)]
    return (
        out_latents,
        token_grad,
        latent_grad,
        gain_tok,
        gain_query,
        gain_mlp,
        gain_self,
        grad_query,
        grads[5],
        grads[4],
        grads[3],
        grads[2],
        grads[0],
        grads[1],
    )


def solution(mesh):
    in_specs = (
        P("items", "frames", None),
        P("items"),
        P(),
        P(),
        P(),
        P(),
        P(),
        P(),
        P(),
        P(),
        P(),
        P(),
        P(),
        P(),
        P("items", None, None),
    )
    out_specs = (
        P("items", "frames", None),
        P("items", "frames", None),
        P(None, "frames"),
        P("frames"),
        P("frames"),
        P("frames"),
        P("frames"),
        P(None, "frames"),
        P(None, "frames"),
        P(None, "frames"),
        P(None, "frames"),
        P(None, "frames"),
        P(None, "frames"),
        P(None, "frames"),
    )
    return jax.shard_map(shards, mesh=mesh, in_specs=in_specs, out_specs=out_specs, check_vma=False)
```

```python
import functools

import jax
import jax.numpy as jnp
from jax import lax
from jax.experimental import pallas as pl
from jax.experimental.pallas import tpu as pltpu
from jax.sharding import PartitionSpec as P

MESH = pl.DeviceIdType.MESH
HEADS = 12
EPSILON = 1e-05
LANES = 128
BLOCK = 256


def nn(left, right):
    return lax.dot_general(left, right, (((1,), (0,)), ((), ())), preferred_element_type=jnp.float32)


def nt(left, right):
    return lax.dot_general(left, right, (((1,), (1,)), ((), ())), preferred_element_type=jnp.float32)


def norm_down(columns):
    centered = columns - jnp.mean(columns, axis=0, keepdims=True)
    inverse = lax.rsqrt(jnp.mean(centered * centered, axis=0, keepdims=True) + EPSILON)
    return centered * inverse, inverse


def gelu(value):
    slope = (2 / jnp.pi) ** 0.5
    tanh = jnp.tanh(value * (slope + (slope * 0.044715) * (value * value)))
    return value * (0.5 + 0.5 * tanh)


def norm_down_back(incoming, normed, inverse, gain):
    scaled = incoming * gain
    average = jnp.mean(scaled, axis=0, keepdims=True)
    along = jnp.mean(scaled * normed, axis=0, keepdims=True)
    return inverse * (scaled - average - normed * along)


def gain_columns(gain_ref):
    return jnp.broadcast_to(gain_ref[...].reshape(1, -1), (LANES, gain_ref.shape[0])).T


def loop(count, body):
    def step(index, carry):
        body(index)
        return carry

    lax.fori_loop(0, count, step, 0)


def window_at(index, size):
    return pl.ds(pl.multiple_of(index * size, size), size)


def forward_kernel(
    frames, groups,
    tokens_ref, skip_ref, latent_ref, tok_gain_ref, query_gain_ref, mlp_gain_ref, self_gain_ref,
    w_query_ref, w_keyval_ref, w_out_ref, w_up_ref, w_down_ref, w_qkv_ref, w_self_ref, grad_ref,
    kv_out, log_out, query_out, mid_out, latents_out, act_out, hidden_out, mlp_out, cross_out, after_out, cot_out, heard_out,
    heard_f32_out, d_triple_out, arrived,
    tokens, tok_in, queries, sent, got,
    w_out, w_out_t, w_self, w_self_t, w_qkv, tall, up_down, down_up,
    heard, cross, mlp_in, act, hidden_rows, after, self_in, triple, mixed, cotangent, d_mixed, d_triple, heard_f32, turned,
    tok_gain, mlp_gain, self_gain, stage,
    tok_sem, kv_sem, y_send, y_recv, w_sem, stage_sem, got_sem, save_sem,
):
    items, rows, width = tokens_ref.shape
    latents = latent_ref.shape[0]
    hidden = w_up_ref.shape[1]
    head = width // HEADS
    factor = head ** -0.5
    own = width // frames
    stat = sent.shape[1] - width
    pieces = mid_out.shape[0]
    item = lax.axis_index("items")
    frame = lax.axis_index("frames")

    barrier = pltpu.get_barrier_semaphore()
    for hop in range(1, frames):
        pl.semaphore_signal(barrier, inc=1, device_id=(item, lax.rem(frame + hop, frames)), device_id_type=MESH)

    wide = 2 * width
    load_query = pltpu.make_async_copy(w_query_ref, w_self_t, w_sem.at[0])
    load_keyval = pltpu.make_async_copy(w_keyval_ref, down_up.at[:, pl.ds(0, wide)], w_sem.at[1])
    load_self = pltpu.make_async_copy(w_self_ref, w_self, w_sem.at[2])
    load_out = pltpu.make_async_copy(w_out_ref, w_out, w_sem.at[3])
    load_qkv = pltpu.make_async_copy(w_qkv_ref, w_qkv, w_sem.at[4])
    load_up = pltpu.make_async_copy(w_up_ref, down_up, w_sem.at[5])

    def load_tokens(i):
        return pltpu.make_async_copy(tokens_ref.at[i], tokens.at[lax.rem(i, 2)], tok_sem.at[lax.rem(i, 2)])

    columns_all = items * latents
    spare = width - columns_all
    third = 3 * width
    loads_down = [
        pltpu.make_async_copy(w_down_ref.at[:, pl.ds(0, columns_all)], triple, w_sem.at[6]),
        pltpu.make_async_copy(
            w_down_ref.at[pl.ds(0, third), pl.ds(columns_all, spare)], d_triple.at[:, pl.ds(0, spare)], w_sem.at[7]
        ),
        pltpu.make_async_copy(
            w_down_ref.at[pl.ds(third, hidden - third), pl.ds(columns_all, spare)],
            d_triple.at[pl.ds(0, hidden - third), pl.ds(spare, spare)],
            w_sem.at[8],
        ),
    ]

    def kv_at(i):
        return pl.ds(pl.multiple_of(lax.rem(i, 2) * wide, wide), wide)

    def save_kv(i):
        return pltpu.make_async_copy(act.at[kv_at(i), pl.ds(0, rows)], kv_out.at[i], kv_sem.at[lax.rem(i, 2)])

    def across(i, hop, part=slice(None)):
        return pltpu.make_async_remote_copy(
            src_ref=sent.at[i, part], dst_ref=(arrived if frames > 2 else got).at[hop - 1, i, part], send_sem=y_send.at[hop - 1, i], recv_sem=y_recv.at[hop - 1, i],
            device_id=(item, lax.rem(frame + hop, frames)), device_id_type=MESH,
        )

    load_tokens(0).start()
    load_query.start()
    load_keyval.start()
    load_tokens(1).start()
    for copy in (load_self, load_out, load_qkv):
        copy.start()

    latent_t = latent_ref[...].astype(jnp.float32).T
    query_normed, _ = norm_down(latent_t)
    query_in = (query_normed * gain_columns(query_gain_ref)).T.astype(jnp.bfloat16)
    tok_gain[...] = gain_columns(tok_gain_ref)
    mlp_gain[...] = gain_columns(mlp_gain_ref)
    self_gain[...] = gain_columns(self_gain_ref)
    load_query.wait()
    query = nn(query_in, w_self_t[...]).astype(jnp.bfloat16)
    query_out[...] = query
    scaled = query * jnp.bfloat16(factor)
    for h in range(HEADS):
        queries[h] = scaled[:, h * head : (h + 1) * head]
    load_keyval.wait()
    for block in range(wide // BLOCK):
        window = pl.ds(block * BLOCK, BLOCK)
        tall[window, :] = down_up[:, window].T
    load_up.start()
    for copy in loads_down:
        copy.start()
    pl.semaphore_wait(barrier, frames - 1)

    def norm_block(slot, b):
        window = window_at(b, LANES)
        normed, _ = norm_down(tokens[slot, window, :].T.astype(jnp.float32))
        tok_in[:, window] = (normed * tok_gain[...]).astype(jnp.bfloat16)

    def heard_item(i):
        slot = lax.rem(i, 2)
        load_tokens(i).wait()

        loop(rows // LANES, lambda b: norm_block(slot, b))

        @pl.when(i + 2 < items)
        def _():
            load_tokens(i + 2).start()

        @pl.when(i >= 2)
        def _():
            save_kv(i - 2).wait()

        base = pl.multiple_of(slot * wide, wide)
        for block in range(wide // BLOCK):
            keyval_block(base, block)
        save_kv(i).start()
        stats = jnp.zeros((latents, LANES), jnp.float32)
        for h in range(HEADS):
            stats = heard_head(i, base, h, stats)
        sent[i, pl.ds(width, stat), :] = stats.T[:stat]
        for hop in range(1, frames):
            across(i, hop).start()

    def keyval_block(base, block):
        act[pl.ds(base + block * BLOCK, BLOCK), pl.ds(0, rows)] = nn(
            tall[pl.ds(block * BLOCK, BLOCK), :], tok_in[...]
        ).astype(jnp.bfloat16)

    def heard_head(i, base, h, stats):
        lane = lax.broadcasted_iota(jnp.int32, (latents, LANES), 1)
        scores = nn(queries[h], act[pl.ds(base + h * head, head), pl.ds(0, rows)])
        most = jnp.max(scores, axis=-1, keepdims=True)
        shifted = jnp.exp(scores - most)
        total = jnp.sum(shifted, axis=-1, keepdims=True)
        stats = jnp.where(lane == h, most, stats)
        stats = jnp.where(lane == h + stat // 2, total, stats)
        sent[i, pl.ds(h * head, head), :] = nt(
            act[pl.ds(base + width + h * head, head), pl.ds(0, rows)], shifted.astype(jnp.bfloat16)
        )
        return stats

    def first_item():
        load_tokens(0).wait()
        loop(rows // LANES, lambda b: norm_block(0, b))
        if items > 2:
            load_tokens(2).start()
        stats = jnp.zeros((latents, LANES), jnp.float32)
        parts = width // BLOCK
        for part in range(parts):
            keyval_block(0, part)
            keyval_block(0, part + parts)
            for h in range(part * BLOCK // head, (part + 1) * BLOCK // head):
                stats = heard_head(0, 0, h, stats)
            end = (part + 1) * BLOCK
            if part == parts - 1:
                sent[0, pl.ds(width, stat), :] = stats.T[:stat]
                end += stat
            for hop in range(1, frames):
                across(0, hop, pl.ds(part * BLOCK, end - part * BLOCK)).start()
        save_kv(0).start()

    first_item()
    loop(items - 1, lambda i: heard_item(i + 1))

    def turn(source, target, count):
        def block(b):
            window = window_at(b, BLOCK)
            target[window, :] = source[:, window].T

        loop(count // BLOCK, block)

    load_self.wait()

    def load_cotangent(i):
        cotangent[:, window_at(i, latents)] = grad_ref[i].T

    loop(items, load_cotangent)
    for block in range(width // BLOCK):
        window = pl.ds(block * BLOCK, BLOCK)
        d_mixed[window, :] = nn(w_self[window, :], cotangent[...]).astype(jnp.bfloat16)
    turn(w_self, w_self_t, width)
    load_out.wait()
    turn(w_out, w_out_t, width)
    load_up.wait()
    turn(down_up, up_down, hidden)
    for copy in loads_down:
        copy.wait()

    def turn_down(b):
        window = window_at(b, BLOCK)
        down_up[pl.ds(0, columns_all), window] = triple[window, :].T

    loop(hidden // BLOCK, turn_down)
    for b in range(hidden // BLOCK):
        window = pl.ds(b * BLOCK, BLOCK)
        if b * BLOCK < third:
            down_up[pl.ds(columns_all, spare), window] = d_triple[window, pl.ds(0, spare)].T
        else:
            down_up[pl.ds(columns_all, spare), window] = d_triple[pl.ds(b * BLOCK - third, BLOCK), pl.ds(spare, spare)].T
    load_qkv.wait()
    turn(w_qkv, tall, 3 * width)
    for i in range(max(items - 2, 0), items):
        save_kv(i).wait()

    def combine(i):
        for hop in range(1, frames):
            across(i, hop).wait_send()
            across(i, hop).wait_recv()
            if frames > 2:
                near = pltpu.make_async_copy(arrived.at[hop - 1, i], got.at[hop - 1, 0], got_sem)
                near.start()
                near.wait()
        parts = [sent.at[i]] + [got.at[hop, 0 if frames > 2 else i] for hop in range(frames - 1)]
        highs = [part[pl.ds(width, stat // 2), :] for part in parts]
        sums = [part[pl.ds(width + stat // 2, stat // 2), :] for part in parts]
        most = functools.reduce(jnp.maximum, highs)
        total = functools.reduce(jnp.add, [low * jnp.exp(high - most) for high, low in zip(highs, sums)])
        log_total = most + jnp.log(total)
        scales = [jnp.exp(high - log_total) for high in highs]
        for h in range(HEADS):
            window = pl.ds(h * head, head)
            together = functools.reduce(
                jnp.add, [part[window, :] * scale[h : h + 1] for part, scale in zip(parts, scales)]
            )
            heard_f32[window, window_at(i, latents)] = together
            heard[window, window_at(i, latents)] = together.astype(jnp.bfloat16)
        padded = jnp.concatenate([log_total, jnp.zeros((LANES - stat // 2, latents), jnp.float32)], axis=0)
        log_out[i] = padded.T

    def attend(i):
        window = window_at(i, latents)
        for first in range(0, HEADS, 4):
            at = [[pl.ds(third * width + h * head, head) for third in range(3)] for h in range(first, first + 4)]
            query = [triple[where[0], window] * jnp.bfloat16(factor) for where in at]
            key = [triple[where[1], window] for where in at]
            value = [triple[where[2], window] for where in at]
            d_mix = [d_mixed[where[0], window] for where in at]
            scores = [nn(k.T, q) for k, q in zip(key, query)]
            d_probs = [nn(v.T, d) for v, d in zip(value, d_mix)]
            shifted = [jnp.exp(s - jnp.max(s, axis=0, keepdims=True)) for s in scores]
            probs = [s * (1.0 / jnp.sum(s, axis=0, keepdims=True)) for s in shifted]
            low = [p.astype(jnp.bfloat16) for p in probs]
            mix = [nn(v, p) for v, p in zip(value, low)]
            delta = [jnp.sum(d.astype(jnp.float32) * m, axis=0, keepdims=True) for d, m in zip(d_mix, mix)]
            d_scores = [(p * (d - x)).astype(jnp.bfloat16) for p, d, x in zip(probs, d_probs, delta)]
            d_query = [nn(k, d) * factor for k, d in zip(key, d_scores)]
            d_key = [nt(q, d) for q, d in zip(query, d_scores)]
            d_value = [nt(d, p) for d, p in zip(d_mix, low)]
            for where, m, dq, dk, dv in zip(at, mix, d_query, d_key, d_value):
                mixed[where[0], window] = m.astype(jnp.bfloat16)
                d_triple[where[0], window] = dq.astype(jnp.bfloat16)
                d_triple[where[1], window] = dk.astype(jnp.bfloat16)
                d_triple[where[2], window] = dv.astype(jnp.bfloat16)

    def forward_group(group):
        size = items // groups
        first = group * size
        columns = pl.ds(first * latents, size * latents)

        def each_item(body):
            loop(size, lambda i: body(first + i))

        def each_block(count, body):
            loop(count // BLOCK, lambda b: body(window_at(b, BLOCK)))

        each_item(combine)

        def out_block(window):
            cross[window, columns] = nn(w_out_t[window, :], heard[:, columns])

        each_block(width, out_block)

        def cross_item(i):
            window = window_at(i, latents)
            keep = (1 - skip_ref[i]).astype(jnp.float32)
            total = latent_ref[...].astype(jnp.float32).T + keep * cross[:, window]
            cross[:, window] = total
            normed, _ = norm_down(total)
            mlp_in[:, window] = (normed * mlp_gain[...]).astype(jnp.bfloat16)

        each_item(cross_item)

        def up_block(window):
            value = nn(up_down[window, :], mlp_in[:, columns])
            hidden_rows[window, columns] = value
            act[window, columns] = gelu(value).astype(jnp.bfloat16)

        each_block(hidden, up_block)
        if group == groups - 1:
            for at in range(5):
                saves[at].start()

        def down_block(window):
            after[window, columns] = cross[window, columns] + nn(down_up[window, :], act[:, columns])

        each_block(width, down_block)
        if group == groups - 1:
            saves[5].start()

        def after_item(i):
            window = window_at(i, latents)
            normed, _ = norm_down(after[:, window])
            self_in[:, window] = (normed * self_gain[...]).astype(jnp.bfloat16)

        each_item(after_item)

        def triple_block(window):
            triple[window, columns] = nn(tall[window, :], self_in[:, columns]).astype(jnp.bfloat16)

        each_block(3 * width, triple_block)
        each_item(attend)

    saves = [
        pltpu.make_async_copy(source, target, save_sem.at[at])
        for at, (source, target) in enumerate(
            (
                (hidden_rows, hidden_out), (act.at[:, pl.ds(0, items * latents)], act_out), (mlp_in, mlp_out), (cross, cross_out),
                (heard_f32, heard_f32_out), (after, after_out), (heard, heard_out), (cotangent, cot_out), (d_triple, d_triple_out),
            )
        )
    ]
    saves[7].start()
    for group in range(groups):
        forward_group(group)
    saves[8].start()
    saves[6].start()

    pending = {}

    def put(first_piece, count, offset, left, right):
        size = width // count
        slot = len(pending) % stage.shape[0]
        for key in [key for key in pending if key % stage.shape[0] == slot and pending[key] is not None]:
            pending[key].wait()
            pending[key] = None
        view = stage.at[slot]
        view[...] = nt(left[...], right[...])
        copy = pltpu.make_async_copy(
            view.reshape(count, size, own), mid_out.at[pl.ds(first_piece, count), pl.ds(offset, size)], stage_sem.at[slot]
        )
        copy.start()
        pending[len(pending)] = copy

    size = width // pieces
    my_columns = pl.multiple_of(frame * own, own)
    for third in range(3):
        put(0, pieces, third * size, self_in, d_triple.at[pl.ds(3 * my_columns + third * own, own), :])
    put(0, pieces, 3 * size, mixed, cotangent.at[pl.ds(my_columns, own), :])

    share = latents // frames

    def latents_item(i):
        window = window_at(i, latents)
        for block in range(width // BLOCK):
            piece = pl.ds(block * BLOCK, BLOCK)
            turned[:, piece] = (after[piece, window] + nn(w_self_t[piece, :], mixed[:, window])).T
        latents_out[i] = turned[pl.ds(pl.multiple_of(frame * share, share), share), :].astype(jnp.bfloat16)

    loop(items, latents_item)
    for copy in saves:
        copy.wait()
    for copy in pending.values():
        if copy is not None:
            copy.wait()


def forward(
    frames, pieces, tokens, skip, latent_init, tok_gain, query_gain, mlp_gain, self_gain,
    w_query, w_keyval, w_out, w_up, w_down, w_self_qkv, w_self_out, grad_out,
):
    items, rows, width = tokens.shape
    latents = latent_init.shape[0]
    hidden = w_up.shape[1]
    own = width // frames
    columns = items * latents
    mid_rows = 4 * width // pieces
    bf16, f32 = jnp.bfloat16, jnp.float32
    vmem = pl.BlockSpec(memory_space=pltpu.VMEM)
    anywhere = pl.BlockSpec(memory_space=pl.ANY)
    dma = pltpu.SemaphoreType.DMA
    peers = max(frames - 1, 1)
    return pl.pallas_call(
        functools.partial(forward_kernel, frames, 2 if items % 2 == 0 else 1),
        out_shape=(
            jax.ShapeDtypeStruct((items, 2 * width, rows), bf16),
            jax.ShapeDtypeStruct((items, latents, LANES), f32),
            jax.ShapeDtypeStruct((latents, width), bf16),
            jax.ShapeDtypeStruct((pieces, mid_rows, own), f32),
            jax.ShapeDtypeStruct((items, latents // frames, width), bf16),
            jax.ShapeDtypeStruct((hidden, columns), bf16),
            jax.ShapeDtypeStruct((hidden, columns), f32),
            jax.ShapeDtypeStruct((width, columns), bf16),
            jax.ShapeDtypeStruct((width, columns), f32),
            jax.ShapeDtypeStruct((width, columns), f32),
            jax.ShapeDtypeStruct((width, columns), bf16),
            jax.ShapeDtypeStruct((width, columns), bf16),
            jax.ShapeDtypeStruct((width, columns), f32),
            jax.ShapeDtypeStruct((3 * width, columns), bf16),
            jax.ShapeDtypeStruct((peers, items if frames > 2 else 1, width + 32, latents), f32),
        ),
        in_specs=[anywhere, pl.BlockSpec(memory_space=pltpu.SMEM)] + [vmem] * 5 + [anywhere] * 7 + [vmem],
        out_specs=(anywhere, vmem, vmem, anywhere, vmem) + (anywhere,) * 10,
        scratch_shapes=[
            pltpu.VMEM((2, rows, width), bf16),
            pltpu.VMEM((width, rows), bf16),
            pltpu.VMEM((HEADS, latents, width // HEADS), bf16),
            pltpu.VMEM((items, width + 32, latents), f32),
            pltpu.VMEM((peers, 1 if frames > 2 else items, width + 32, latents), f32),
        ]
        + [pltpu.VMEM((width, width), bf16)] * 4
        + [
            pltpu.VMEM((width, 3 * width), bf16),
            pltpu.VMEM((3 * width, width), bf16),
            pltpu.VMEM((hidden, width), bf16),
            pltpu.VMEM((width, hidden), bf16),
            pltpu.VMEM((width, columns), bf16),
            pltpu.VMEM((width, columns), f32),
            pltpu.VMEM((width, columns), bf16),
            pltpu.VMEM((hidden, max(columns, rows)), bf16),
            pltpu.VMEM((hidden, columns), f32),
            pltpu.VMEM((width, columns), f32),
            pltpu.VMEM((width, columns), bf16),
            pltpu.VMEM((hidden, columns), bf16),
            pltpu.VMEM((width, columns), bf16),
            pltpu.VMEM((width, columns), bf16),
            pltpu.VMEM((width, columns), bf16),
            pltpu.VMEM((3 * width, columns), bf16),
            pltpu.VMEM((width, columns), f32),
            pltpu.VMEM((latents, width), f32),
            pltpu.VMEM((width, LANES), f32),
            pltpu.VMEM((width, LANES), f32),
            pltpu.VMEM((width, LANES), f32),
            pltpu.VMEM((2, width, own), f32),
            dma((2,)), dma((2,)), dma((peers, items)), dma((peers, items)), dma((9,)), dma((2,)), dma, dma((9,)),
        ],
        compiler_params=pltpu.CompilerParams(collective_id=1, has_side_effects=True, vmem_limit_bytes=62 * 2**20),
        name="forward",
    )(
        tokens, skip, latent_init, tok_gain, query_gain, mlp_gain, self_gain,
        w_query, w_keyval, w_out, w_up, w_down, w_self_qkv, w_self_out, grad_out,
    )


def add_into(target, parts, rows):
    step = next(size for size in (96, 80, 64, 60, 48, 40, 24, 16, 8) if rows % size == 0 and size % 8 == 0)

    def body(index):
        window = window_at(index, step)
        total = parts[0][window]
        for part in parts[1:]:
            total = total + part[window]
        target[window] = total

    loop(rows // step, body)


def gelu_slope(value):
    slope = (2 / jnp.pi) ** 0.5
    square = value * value
    tanh = jnp.tanh(value * (slope + (slope * 0.044715) * square))
    half = 0.5 + 0.5 * tanh
    bend = value * (2 * slope + (6 * slope * 0.044715) * square)
    return half + half * (1.0 - half) * bend


def nn_exact(left, right):
    total = jnp.zeros((left.shape[0], right.shape[1]), jnp.float32)
    rest = right
    for _ in range(3):
        part = rest.astype(jnp.bfloat16)
        total = total + nn(left, part)
        rest = rest - part.astype(jnp.float32)
    return total


def backward_kernel(
    chips, frames, streams,
    loc_a, tokens_ref, kv_ref, act_ref, hidden_ref, mlp_ref, cross_ref, after_ref, cot_ref, heard_ref, heard_f32_ref, dtri_ref,
    w_qkv_ref, w_up_ref, w_down_ref, w_out_ref, w_keyval_ref, w_query_ref,
    skip_ref, log_ref, query_ref, latent_ref, tok_gain_ref, query_gain_ref, mlp_gain_ref, self_gain_ref,
    *rest,
):
    outs, rest = rest[:12], rest[12:]
    sums, token_out, (loc_b, loc_c, loc_d), sibs = outs[:4], outs[4], outs[5:8], outs[8:12]
    locs = (loc_a, loc_b, loc_c, loc_d)
    (
        flat, tall, w_square, act, pool, mlp_in, heard, cotangent, branch, d_heard, queries, queries_t, token_stage,
        hidden_stage, after, cross, rows_f32, incoming, stage, small_stage, d_query, gain_sum, tok_gain, mlp_gain, self_gain,
        d_latent, gain_cols, delta, inverse, y_mine, y_sib, ky,
    ), rest = rest[:32], rest[32:]
    n = len(streams)
    mines, sib_slots, rxs = rest[:n], rest[n : 2 * n], rest[2 * n : 3 * n]
    (
        pair_send, pair_recv, ld_sem, ls_sem, rs_send, rs_recv, ag_send, ag_recv, share_send, share_recv, own_sem, krs_send, krs_recv,
        kpair_send, kpair_recv, y_send, y_recv, y_sem, in_sem, tok_sem, kv_sem, out_sem, hidden_sem, stage_sem, small_sem,
    ) = rest[3 * n :]

    item_index = lax.axis_index("items")
    frame = lax.axis_index("frames")
    core = lax.rem(item_index, 2)
    chip = item_index // 2
    column = lax.rem(chip, 2)
    line = chip // 2
    place = line + column * (chips - 1 - 2 * line)
    way = 1 - 2 * core
    count, rows, width = tokens_ref.shape
    latents = latent_ref.shape[0]
    hidden = hidden_ref.shape[0]
    head = width // HEADS
    factor = head ** -0.5
    own = width // frames
    pieces = 2 * chips
    per_piece = width // pieces
    kv_rows = loc_d.shape[3]
    last = n - 1

    def device_at(position):
        position = lax.rem(position + 2 * chips, chips)
        far = position // (chips // 2)
        return (2 * (position + far * (chips - 1 - 2 * position)) + far) * 2 + core

    right, left = device_at(place + way), device_at(place - way)
    sibling = item_index + way

    def chunk(offset):
        return lax.rem(place + way * offset + 4 * chips, chips)

    def sib_chunk(offset):
        return lax.rem(place - way * offset + 4 * chips, chips)

    barrier = pltpu.get_barrier_semaphore()
    for peer in (left, right, sibling):
        pl.semaphore_signal(barrier, inc=1, device_id=(peer, frame), device_id_type=MESH)
    for hop in range(1, frames):
        pl.semaphore_signal(barrier, inc=1, device_id=(item_index, lax.rem(frame + hop, frames)), device_id_type=MESH)

    def remote(src, dst, send, recv, peer):
        return pltpu.make_async_remote_copy(
            src_ref=src, dst_ref=dst, send_sem=send, recv_sem=recv, device_id=peer, device_id_type=MESH
        )

    def pair(source, k):
        return remote(
            locs[source].at[1 - core, k], sibs[source].at[k], pair_send.at[source, k], pair_recv.at[source, k], (sibling, frame)
        )

    def frame_at(hop):
        return lax.rem(frame + hop, frames)

    def pair_frame(hop, k):
        f = frame_at(hop)
        return remote(
            loc_d.at[f, 1 - core, k], sibs[3].at[f, k], kpair_send.at[hop - 1, k], kpair_recv.at[hop - 1, k], (sibling, frame)
        )

    def start_pairs(source):
        loop(chips, lambda index: pair(source, sib_chunk(-index)).start())

    def part_of(j):
        source, start, size = streams[j]
        return source, pl.ds(start, size)

    def load_mine(j, k, slot):
        source, part = part_of(j)
        return pltpu.make_async_copy(locs[source].at[core, k, part], mines[j].at[slot], ld_sem.at[j, slot])

    def load_sib(j, k, slot):
        source, part = part_of(j)
        return pltpu.make_async_copy(sibs[source].at[k, part], sib_slots[j].at[slot], ls_sem.at[j, slot])

    def ring(j, k, slot):
        return remote(mines[j].at[slot], rxs[j].at[k], rs_send.at[j, slot], rs_recv.at[j, k], (right, frame))

    def own_at(j, k):
        source, part = part_of(j)
        return sums[source].at[core, k, part]

    def gather(j, k, src):
        return remote(src, own_at(j, k), ag_send.at[j, k], ag_recv.at[j, k], (right, frame))

    def share(j, k, src):
        return remote(src, own_at(j, k), share_send.at[j, k], share_recv.at[j, k], (sibling, frame))

    def share_from(j, k):
        source, part = part_of(j)
        return remote(mines[j].at[0], sums[source].at[1 - core, k, part], share_send.at[j, k], share_recv.at[j, k], (sibling, frame))

    def keep(j, k, slot):
        return pltpu.make_async_copy(mines[j].at[slot], own_at(j, k), own_sem.at[j])

    def across(hop, k):
        other = lax.rem(frame + hop, frames)
        return remote(y_mine.at[k], ky.at[hop - 1, k], y_send.at[hop - 1, k], y_recv.at[hop - 1, k], (item_index, other))

    def prefetch(j, op):
        k, slot = chunk(-op), lax.rem(op, 2)
        source, part = part_of(j)
        pair(source, k).wait_recv()
        load_mine(j, k, slot).start()
        load_sib(j, k, slot).start()

    def when(condition, body):
        if isinstance(condition, (bool, int)):
            if condition:
                body()
        else:
            pl.when(condition)(body)

    def tick(j, op):
        source, part = part_of(j)
        size = streams[j][2]
        slot = lax.rem(op, 2)

        def reduce_op():
            k = chunk(-op)
            load_mine(j, k, slot).wait()
            load_sib(j, k, slot).wait()
            parts = [mines[j].at[slot], sib_slots[j].at[slot]]
            if not (isinstance(op, int) and op == 0):
                ring(j, k, slot).wait_recv()
                parts.append(rxs[j].at[k])
            add_into(mines[j].at[slot], parts, size)

            def pass_on():
                ring(j, k, slot).start()
                if isinstance(op, int) and op == 0:
                    prefetch(j, op + 1)
                else:
                    ring(j, k, 1 - slot).wait_send()
                    prefetch(j, op + 1)

            def finish():
                gather(j, k, mines[j].at[slot]).start()
                share(j, k, mines[j].at[slot]).start()
                keep(j, k, slot).start()

            when(op < chips - 1, pass_on)
            when(op == chips - 1, finish)

        def gather_op():
            k = chunk(-op)
            gather(j, k, mines[j].at[0]).wait_recv()

            def forward_on():
                gather(j, k, own_at(j, k)).start()

            when(op < 2 * chips - 2, forward_on)
            share(j, k, own_at(j, k)).start()

        when(op < chips, reduce_op)
        when((op >= chips) & (op < 2 * chips - 1) if not isinstance(op, int) else chips <= op < 2 * chips - 1, gather_op)

    ahead = chips // 2
    behind = chips - 1 - ahead
    kmine, krx = mines[last], rxs[last]

    def kv_ring(flow, k, arriving_own):
        peer = (right, left)[flow]
        slot = chips if flow == 1 and arriving_own else k
        return remote(kmine.at[k], krx.at[slot], krs_send.at[flow, k], krs_recv.at[flow, k], (peer, frame))

    def kv_gather(flow, k, src):
        return remote(src, sums[3].at[core, k], ag_send.at[last + flow, k], ag_recv.at[last + flow, k], ((right, left)[flow], frame))

    def kv_total(k, arrived):
        parts = [kmine.at[k], y_sib.at[k]]
        for hop in range(1, frames):
            across(hop, k).wait_recv()
            parts.append(ky.at[hop - 1, k])
        add_into(kmine.at[k], parts + arrived, kv_rows)

    def kv_tick(op):
        if op < ahead:
            for flow, length in ((0, ahead), (1, behind)):
                distance = length - op
                if distance < 1:
                    continue
                k = chunk(distance if flow == 0 else -distance)
                arrived = []
                if op > 0:
                    kv_ring(flow, k, False).wait_recv()
                    arrived.append(krx.at[k])
                kv_total(k, arrived)
                kv_ring(flow, k, distance == 1).start()
        elif op == ahead:
            k = chunk(0)
            kv_ring(0, k, False).wait_recv()
            kv_ring(1, k, True).wait_recv()
            kv_total(k, [krx.at[k], krx.at[chips]])
            for flow in range(2):
                kv_gather(flow, k, kmine.at[k]).start()
            share(last, k, kmine.at[k]).start()
            keep(last, k, k).start()
        else:
            step = op - ahead
            for flow, length in ((0, behind), (1, ahead)):
                if step > length:
                    continue
                k = chunk(-step if flow == 0 else step)
                kv_gather(flow, k, kmine.at[0]).wait_recv()
                if step < length:
                    kv_gather(flow, k, sums[3].at[core, k]).start()
                share(last, k, sums[3].at[core, k]).start()

    kv_order = [0] + [offset for step in range(1, ahead + 1) for offset in ((step, -step) if step <= behind else (step,))]
    kv_order = kv_order[::-1]

    third = 3 * width
    names = [
        (dtri_ref, pool.at[pl.ds(hidden, third), :]),
        (w_qkv_ref, flat.at[:, pl.ds(0, third)]),
        (after_ref, after),
        (cot_ref, cotangent),
        (act_ref, act),
        (w_down_ref, tall),
        (mlp_ref, mlp_in),
        (cross_ref, cross),
        (heard_ref, heard),
        (w_out_ref, w_square),
        (w_up_ref, flat),
        (heard_f32_ref, cross),
        (w_query_ref, w_square),
        (w_keyval_ref.at[:, pl.ds(0, width)], tall.at[pl.ds(2 * rows, width), :]),
        (w_keyval_ref.at[:, pl.ds(width, width)], tall.at[pl.ds(2 * rows + width, width), :]),
    ]
    copies = [pltpu.make_async_copy(src, dst, in_sem.at[at]) for at, (src, dst) in enumerate(names)]
    (
        get_dtri, get_qkv, get_after, get_cot, get_act, get_down, get_mlp, get_cross, get_heard, get_out, get_up, get_heard_f32,
        get_query, get_keys, get_values,
    ) = copies

    def load_hidden(b):
        slot = lax.rem(b, 4)
        return pltpu.make_async_copy(hidden_ref.at[window_at(b, BLOCK), :], hidden_stage.at[slot], hidden_sem.at[slot])

    def tok_load(i):
        slot = lax.rem(i, 2)
        return pltpu.make_async_copy(tokens_ref.at[i], tall.at[window_at(slot, rows), :], tok_sem.at[slot])

    def kv_load(i):
        slot = lax.rem(i, 2)
        return pltpu.make_async_copy(kv_ref.at[i], act.at[window_at(slot, 2 * width), pl.ds(0, rows)], kv_sem.at[slot])

    def token_save(i, b):
        slot = lax.rem(b, 2)
        return pltpu.make_async_copy(token_stage.at[slot], token_out.at[i, window_at(b, LANES), :], out_sem.at[slot])

    for copy in (get_dtri, get_qkv, get_after, get_cot, get_act, get_down, get_mlp, get_cross, get_heard, get_out):
        copy.start()
    for b in range(3):
        load_hidden(b).start()
    pl.semaphore_wait(barrier, 3 + frames - 1)
    start_pairs(0)
    tok_gain[...] = gain_columns(tok_gain_ref)
    mlp_gain[...] = gain_columns(mlp_gain_ref)
    self_gain[...] = gain_columns(self_gain_ref)
    scaled = query_ref[...] * jnp.bfloat16(factor)
    for h in range(HEADS):
        queries[h] = scaled[:, h * head : (h + 1) * head]
    queries_t[...] = scaled.T
    d_query[...] = jnp.zeros_like(d_query)
    gain_sum[...] = jnp.zeros_like(gain_sum)
    gain_cols[...] = jnp.zeros_like(gain_cols)
    d_latent[...] = jnp.zeros_like(d_latent)
    prefetch(0, 0)

    done = [0] * n

    def advance(*which):
        for j in which:
            if done[j] < 2 * chips - 1:
                tick(j, done[j])
                done[j] += 1

    def each_item(body):
        loop(count, lambda i: body(i, window_at(i, latents)))

    def each_block(first, total, body):
        loop(total // BLOCK, lambda b: body(b + first, window_at(b + first, BLOCK)))

    pending = {}

    def put(target, left, right):
        slot = len(pending) % stage.shape[0]
        for key in [key for key in pending if key % stage.shape[0] == slot and pending[key] is not None]:
            pending[key].wait()
            pending[key] = None
        view = stage.at[slot]
        view[...] = nt(left[...], right[...])
        put_start(target, slot)

    def put_start(target, slot):
        copy = pltpu.make_async_copy(stage.at[slot].reshape(*target.shape), target, stage_sem.at[slot])
        copy.start()
        pending[len(pending)] = copy

    def put_done():
        for key in pending:
            if pending[key] is not None:
                pending[key].wait()
                pending[key] = None

    my_columns = pl.multiple_of(frame * own, own)
    lane = lax.broadcasted_iota(jnp.int32, (width, LANES), 1)

    get_dtri.wait()
    get_qkv.wait()
    advance(0)

    def self_block(b, window):
        incoming[window, :] = nn(flat[window, pl.ds(0, third)], pool[pl.ds(hidden, third), :])

    each_block(0, width, self_block)
    get_up.start()
    get_after.wait()
    get_cot.wait()

    def self_back(i, window):
        normed, inverse_row = norm_down(after[:, window])
        arriving = incoming[:, window]
        gain_cols[...] += jnp.where(lane == 1, jnp.sum(arriving * normed, axis=-1, keepdims=True), 0.0)
        d_after = cotangent[:, window].astype(jnp.float32) + norm_down_back(arriving, normed, inverse_row, self_gain[...])
        branch[:, window] = d_after.astype(jnp.bfloat16)
        rows_f32[:, window] = d_after

    each_item(self_back)
    advance(0)
    get_act.wait()
    groups = hidden // width
    for group in range(groups):
        size = hidden // pieces
        span = pieces // groups
        target = loc_b.at[group * span // chips, pl.ds(group * span % chips, span)] if span <= chips else None
        put(target, act.at[pl.ds(group * width, width), :], branch.at[pl.ds(my_columns, own), :])
    put_done()
    start_pairs(1)
    kv_load(0).start()
    get_down.wait()

    def hidden_block(b, window):
        load_hidden(b).wait()

        @pl.when(b + 3 < hidden // BLOCK)
        def _():
            load_hidden(b + 3).start()

        d_act = nn(tall[window, :], branch[...])
        pool[window, :] = (d_act * gelu_slope(hidden_stage[lax.rem(b, 4)])).astype(jnp.bfloat16)

    half = hidden // BLOCK // 2
    each_block(0, half * BLOCK, hidden_block)
    advance(0)
    prefetch(1, 0)
    each_block(half, hidden - half * BLOCK, hidden_block)
    advance(1)
    tok_load(0).start()
    get_keys.start()
    get_values.start()
    get_mlp.wait()
    advance(0)
    for part in range(groups):
        source = pool.at[pl.ds(frame * (hidden // frames) + part * own, own), :]
        put(loc_c.at[:, :, pl.ds(part * per_piece, per_piece)], mlp_in, source)
        if part == groups // 2 - 1:
            advance(1)
    get_up.wait()
    advance(0)

    def mlp_block(b, window):
        incoming[window, :] = nn(flat[window, :], pool[pl.ds(0, hidden), :])

    each_block(0, width, mlp_block)
    get_cross.wait()
    advance(1)

    def mlp_back(i, window):
        normed, inverse_row = norm_down(cross[:, window])
        arriving = incoming[:, window]
        gain_cols[...] += jnp.where(lane == 0, jnp.sum(arriving * normed, axis=-1, keepdims=True), 0.0)
        d_cross = rows_f32[:, window] + norm_down_back(arriving, normed, inverse_row, mlp_gain[...])
        d_latent[...] += d_cross.T
        keep_item = (1 - skip_ref[i]).astype(jnp.float32)
        branch[:, window] = (keep_item * d_cross).astype(jnp.bfloat16)

    each_item(mlp_back)
    get_heard_f32.start()
    get_heard.wait()
    advance(0)
    put(loc_c.at[:, :, pl.ds(groups * per_piece, per_piece)], heard, branch.at[pl.ds(my_columns, own), :])
    put_done()
    start_pairs(2)
    get_out.wait()

    def heard_block(b, window):
        d_heard[window, :] = nn(w_square[window, :], branch[...]).astype(jnp.bfloat16)

    each_block(0, width, heard_block)
    get_query.start()
    get_heard_f32.wait()
    advance(1)

    def delta_item(i, window):
        product = d_heard[:, window].astype(jnp.float32) * cross[:, window]
        sums_of = jnp.sum(product.reshape(HEADS, head, latents), axis=1)
        padded = jnp.concatenate([sums_of, jnp.zeros((LANES - HEADS, latents), jnp.float32)], axis=0)
        delta[i] = padded.T

    each_item(delta_item)
    prefetch(2, 0)
    get_keys.wait()
    get_values.wait()
    advance(0, 2)

    def attend(i, heads):
        base = pl.multiple_of(lax.rem(i, 2) * 2 * width, 2 * width)
        target = pl.multiple_of(i * 2 * width, 2 * width)
        latent_window = window_at(i, latents)
        for h in heads:
            keys_at = pl.ds(h * head, head)
            keys = act[pl.ds(base + h * head, head), pl.ds(0, rows)]
            values = act[pl.ds(base + width + h * head, head), pl.ds(0, rows)]
            d_heard_t = d_heard[keys_at, latent_window]
            probs = jnp.exp(nn(queries[h], keys) - log_ref[i, :, h : h + 1])
            d_probs = nn(d_heard_t.T, values)
            d_scores = (probs * (d_probs - delta[i, :, h : h + 1])).astype(jnp.bfloat16)
            pool[pl.ds(target + h * head, head), pl.ds(0, rows)] = nn(queries_t[keys_at, :], d_scores).astype(jnp.bfloat16)
            pool[pl.ds(target + width + h * head, head), pl.ds(0, rows)] = nn(d_heard_t, probs.astype(jnp.bfloat16)).astype(
                jnp.bfloat16
            )
            d_query[keys_at, :] += nt(keys, d_scores)

    def norm_tokens(i):
        tok_load(i).wait()
        base = pl.multiple_of(lax.rem(i, 2) * rows, rows)

        def norm_block(b):
            window = window_at(b, LANES)
            columns = tall[pl.ds(base + b * LANES, LANES), :].T.astype(jnp.float32)
            block, inverse_row = norm_down(columns)
            after[:, window] = block
            inverse[:, window] = jnp.broadcast_to(inverse_row, (8, LANES))
            flat[:, pl.ds(pl.multiple_of(i * rows + b * LANES, LANES), LANES)] = (block * tok_gain[...]).astype(jnp.bfloat16)

        loop(rows // LANES, norm_block)

    def token_back(i):
        base = pl.multiple_of(i * 2 * width, 2 * width)

        def product(b):
            window = window_at(b, BLOCK)
            keys_w = tall[pl.ds(pl.multiple_of(2 * rows + b * BLOCK, BLOCK), BLOCK), :]
            values_w = tall[pl.ds(pl.multiple_of(2 * rows + width + b * BLOCK, BLOCK), BLOCK), :]
            incoming[window, :] = nn(keys_w, pool[pl.ds(base, width), pl.ds(0, rows)]) + nn(
                values_w, pool[pl.ds(base + width, width), pl.ds(0, rows)]
            )

        loop(width // BLOCK, product)

        def back_block(b):
            window = window_at(b, LANES)
            block = after[:, window]
            arriving = incoming[:, window]
            gain_sum[...] += arriving * block
            result = norm_down_back(arriving, block, inverse[pl.ds(0, 1), window], tok_gain[...])

            @pl.when((i > 0) | (b > 1))
            def _():
                token_save(i, b).wait()

            token_stage[lax.rem(b, 2)] = result.T.astype(jnp.bfloat16)
            token_save(i, b).start()

        loop(rows // LANES, back_block)

    base_ops = list(done)

    def one_item(i):
        kv_load(i).wait()

        @pl.when(i + 1 < count)
        def _():
            kv_load(i + 1).start()
            tok_load(i + 1).start()

        norm_tokens(i)
        attend(i, range(HEADS // 2))
        tick(1, base_ops[1] + i)
        attend(i, range(HEADS // 2, HEADS))
        tick(2, base_ops[2] + i)
        token_back(i)

        tick(0, base_ops[0] + i)

    loop(count, one_item)
    for j in range(last):
        done[j] = base_ops[j] + count

    small = 2 * latents // pieces
    get_query.wait()
    d_query[...] = d_query[...] * factor
    q_total = d_query[...]
    q_normed, q_inverse = norm_down(latent_ref[...].astype(jnp.float32).T)
    q_incoming = nn_exact(w_square[...], q_total)
    all_gains = gain_cols[...]
    all_gains = jnp.where(lane == 2, jnp.sum(gain_sum[...], axis=-1, keepdims=True), all_gains)
    all_gains = jnp.where(lane == 3, jnp.sum(q_incoming * q_normed, axis=-1, keepdims=True), all_gains)
    gain_rows = all_gains.T[:8]
    latent_rows = norm_down_back(q_incoming, q_normed, q_inverse, gain_columns(query_gain_ref)).T
    query_rows = q_total.T
    for f in range(frames):
        mask = (frame == f).astype(jnp.float32)
        mine_columns = slice(f * own, (f + 1) * own)
        latent_part = latent_rows[:, mine_columns] + mask * d_latent[:, mine_columns]
        both = jnp.concatenate([query_rows[:, mine_columns], latent_part], axis=0)
        small_stage[f, :, :, pl.ds(0, small), :] = both.reshape(2, chips, small, own)
        row = lax.broadcasted_iota(jnp.int32, (8, own), 0)
        gain_block = gain_rows[:, mine_columns] * jnp.where(row < 2, mask, 1.0)
        small_stage[f, :, :, pl.ds(small, 8), :] = jnp.zeros((2, chips, 8, own), jnp.float32)
        small_stage[f, 0, 0, pl.ds(small, 8), :] = gain_block
    put_small = pltpu.make_async_copy(small_stage, loc_d.at[:, :, :, pl.ds(2 * per_piece, small + 8)], small_sem)
    put_small.start()
    advance(1)
    for hop in range(1, frames + 1):
        f = frame_at(hop)
        for b in range(2):
            slot = len(pending) % stage.shape[0]
            for key in [key for key in pending if key % stage.shape[0] == slot and pending[key] is not None]:
                pending[key].wait()
                pending[key] = None
            first_row = pl.multiple_of((2 * f + b) * own, own)
            source = jnp.concatenate(
                [pool[pl.ds(i * 2 * width + first_row, own), pl.ds(0, rows)] for i in range(count)], axis=1
            )
            stage[slot] = nt(flat[:, pl.ds(0, count * rows)], source)
            put_start(loc_d.at[f, :, :, pl.ds(b * per_piece, per_piece)], slot)
        if hop == 1:
            put_small.wait()
        put_done()
        loop(chips, lambda index: pair_frame(hop, sib_chunk(-index)).start())
        if hop <= 2:
            advance(2 if hop == 1 else 0)
    advance(1)
    for hop in range(1, frames):
        other = frame_at(hop)
        if hop > 1:
            for k in range(chips):
                across(hop - 1, k).wait_send()
        for k in range(chips):
            pair_frame(hop, k).wait_recv()
        one = pltpu.make_async_copy(loc_d.at[other, core], y_mine, y_sem.at[0])
        two = pltpu.make_async_copy(sibs[3].at[other], y_sib, y_sem.at[1])
        one.start()
        two.start()
        one.wait()
        two.wait()

        for offset in kv_order:
            k = chunk(offset)
            add_into(y_mine.at[k], [y_mine.at[k], y_sib.at[k]], kv_rows)
            across(hop, k).start()
    advance(2)
    for k in range(chips):
        pair_frame(frames, k).wait_recv()
    one = pltpu.make_async_copy(loc_d.at[frame, core], kmine, y_sem.at[0])
    two = pltpu.make_async_copy(sibs[3].at[frame], y_sib, y_sem.at[1])
    one.start()
    two.start()
    advance(0)
    one.wait()
    two.wait()
    total = 2 * chips - 1
    others = sum(total - done[j] for j in range(last))
    turns, taken = chips + 1, 0
    for turn in range(turns):
        kv_tick(turn)
        while taken * turns < (turn + 1) * others:
            j = max(range(last), key=lambda j: (total - done[j]) * (streams[j][2] + 160))
            advance(j)
            taken += 1

    def drain(k):
        for source in range(3):
            pair(source, k).wait_send()
        for hop in range(1, frames + 1):
            pair_frame(hop, k).wait_send()
        for j in range(n):
            share(j, k, mines[j].at[0]).wait_send()
            share_from(j, k).wait_recv()
        if frames > 1:
            across(frames - 1, k).wait_send()

    loop(chips, drain)

    def drain_ring(step):
        for j in range(last):
            gather(j, chunk(1 - step), mines[j].at[0]).wait_send()

    loop(chips - 1, drain_ring)
    for j in range(last):
        ring(j, 0, (chips - 2) % 2).wait_send()
        keep(j, chunk(1), (chips - 1) % 2).wait()
    keep(last, chunk(0), 0).wait()
    for distance in range(1, ahead + 1):
        kv_ring(0, chunk(distance), False).wait_send()
        kv_gather(1, chunk(distance - 1), kmine.at[0]).wait_send()
    for distance in range(1, behind + 1):
        kv_ring(1, chunk(-distance), False).wait_send()
        kv_gather(0, chunk(1 - distance), kmine.at[0]).wait_send()
    for b in range(2):
        token_save(0, b).wait()


def backward(
    frames, first, tokens, kv, act, hidden, mlp_in, cross, after, cotangent, heard, heard_f32, d_triple, skip, log_total, query,
    latent_init, tok_gain, query_gain, mlp_gain, self_gain, w_query, w_keyval, w_out, w_up, w_down, w_self_qkv,
):
    chips, first_rows, own = first.shape[1:]
    items, rows, width = tokens.shape
    latents = latent_init.shape[0]
    hidden_width, columns = hidden.shape
    pieces = 2 * chips
    per_piece = width // pieces
    kv_rows = 2 * per_piece + 2 * latents // pieces + 8
    source_rows = (first_rows, hidden_width // pieces, per_piece * (hidden_width // width + 1), kv_rows)
    streams = tuple((source, 0, size) for source, size in enumerate(source_rows))
    n = len(streams)
    dma = pltpu.SemaphoreType.DMA
    peers = max(frames - 1, 1)
    f32, bf16 = jnp.float32, jnp.bfloat16
    vmem = pl.BlockSpec(memory_space=pltpu.VMEM)
    anywhere = pl.BlockSpec(memory_space=pl.ANY)
    wide = max(columns, rows)
    scratch = [
        pltpu.VMEM((width, max(hidden_width, items * rows)), bf16),
        pltpu.VMEM((max(hidden_width, 2 * rows + 2 * width), width), bf16),
        pltpu.VMEM((width, width), bf16),
        pltpu.VMEM((max(hidden_width, 4 * width), wide), bf16),
        pltpu.VMEM((max(hidden_width + 3 * width, items * 2 * width), wide), bf16),
        pltpu.VMEM((width, columns), bf16),
        pltpu.VMEM((width, columns), bf16),
        pltpu.VMEM((width, columns), bf16),
        pltpu.VMEM((width, columns), bf16),
        pltpu.VMEM((width, columns), bf16),
        pltpu.VMEM((HEADS, latents, width // HEADS), bf16),
        pltpu.VMEM((width, latents), bf16),
        pltpu.VMEM((2, LANES, width), bf16),
        pltpu.VMEM((4, BLOCK, columns), f32),
        pltpu.VMEM((width, wide), f32),
        pltpu.VMEM((width, columns), f32),
        pltpu.VMEM((width, columns), f32),
        pltpu.VMEM((width, wide), f32),
        pltpu.VMEM((2, width, own), f32),
        pltpu.VMEM((frames, 2, chips, 2 * latents // pieces + 8, own), f32),
        pltpu.VMEM((width, latents), f32),
        pltpu.VMEM((width, LANES), f32),
        pltpu.VMEM((width, LANES), f32),
        pltpu.VMEM((width, LANES), f32),
        pltpu.VMEM((width, LANES), f32),
        pltpu.VMEM((latents, width), f32),
        pltpu.VMEM((width, LANES), f32),
        pltpu.VMEM((items, latents, LANES), f32),
        pltpu.VMEM((8, rows), f32),
        pltpu.VMEM((chips, kv_rows, own), f32),
        pltpu.VMEM((chips, kv_rows, own), f32),
        pltpu.VMEM((peers, chips, kv_rows, own), f32),
    ]
    scratch += [pltpu.VMEM((2 if source < 3 else chips, size, own), f32) for source, _, size in streams]
    scratch += [pltpu.VMEM((2, size if source < 3 else 8, own), f32) for source, _, size in streams]
    scratch += [pltpu.VMEM((chips + source // 3, size, own), f32) for source, _, size in streams]
    scratch += [
        dma((3, chips)), dma((3, chips)), dma((n, 2)), dma((n, 2)), dma((n, 2)), dma((n, chips)),
        dma((n + 1, chips)), dma((n + 1, chips)), dma((n, chips)), dma((n, chips)), dma((n,)), dma((2, chips)), dma((2, chips)),
        dma((frames, chips)), dma((frames, chips)), dma((peers, chips)), dma((peers, chips)), dma((2,)), dma((15,)), dma((2,)), dma((2,)), dma((2,)), dma((4,)), dma((2,)), dma,
    ]
    shape = jax.ShapeDtypeStruct
    summed = tuple(shape((2, chips, size, own), f32) for size in source_rows)
    return pl.pallas_call(
        functools.partial(backward_kernel, chips, frames, streams),
        out_shape=summed
        + (shape(tokens.shape, bf16),)
        + summed[1:3]
        + (shape((frames, 2, chips, kv_rows, own), f32),)
        + tuple(shape((chips, size, own), f32) for size in source_rows[:3])
        + (shape((frames, chips, kv_rows, own), f32),),
        in_specs=[anywhere] * 18 + [pl.BlockSpec(memory_space=pltpu.SMEM)] + [vmem] * 7,
        out_specs=(anywhere,) * 12,
        scratch_shapes=scratch,
        compiler_params=pltpu.CompilerParams(collective_id=0, has_side_effects=True, vmem_limit_bytes=62 * 2**20),
        name="backward",
    )(
        first, tokens, kv, act, hidden, mlp_in, cross, after, cotangent, heard, heard_f32, d_triple,
        w_self_qkv, w_up, w_down, w_out, w_keyval, w_query, skip, log_total, query, latent_init,
        tok_gain, query_gain, mlp_gain, self_gain,
    )


def unpack_kernel(first_ref, second_ref, third_ref, kv_ref, latent_ref, qgain_ref, *rest):
    outs, (query_out, *gain_outs), (blocks, total, tail, in_sem, out_sem) = rest[:7], rest[7:12], rest[12:]
    pieces, _, own = first_ref.shape
    loads, stores = [], []

    def place(source, offset, out):
        rows, columns = out.shape
        size = rows // pieces
        view = out.reshape(pieces, size, columns)
        for b in range(columns // own):
            at = len(loads)
            area = blocks.at[pl.ds(starts[at], pieces * size), :].reshape(pieces, size, own)
            loads.append(pltpu.make_async_copy(source.at[:, pl.ds(offset + b * size, size), :], area, in_sem.at[at]))
            stores.append(pltpu.make_async_copy(area, view.at[:, :, pl.ds(b * own, own)], out_sem.at[at]))
        return offset + size * columns // own

    starts, start = [], 0
    for out in outs[:6]:
        rows, columns = out.shape
        for b in range(columns // own):
            starts.append(start)
            start += rows
    place(first_ref, place(first_ref, 0, outs[0]), outs[1])
    place(second_ref, 0, outs[2])
    place(third_ref, place(third_ref, 0, outs[3]), outs[4])
    offset = place(kv_ref, 0, outs[5])
    latents = outs[6].shape[0]
    small = 2 * latents // pieces
    half = pieces // 2
    query = pltpu.make_async_copy(kv_ref.at[:, pl.ds(offset, small), :], total, in_sem.at[len(loads)])
    gains = pltpu.make_async_copy(kv_ref.at[0, pl.ds(offset + small, 8), :], tail, in_sem.at[len(loads) + 1])
    query.start()
    gains.start()
    for copy in loads:
        copy.start()
    for load, store in zip(loads, stores):
        load.wait()
        store.start()
    normed, _ = norm_down(latent_ref[...].astype(jnp.float32).T)
    query_in = (normed * gain_columns(qgain_ref)).astype(jnp.bfloat16)
    query.wait()
    query_out[...] = nn_exact(query_in, total[pl.ds(0, half)].reshape(latents, own))
    outs[6][...] = total[pl.ds(half, half)].reshape(latents, own)
    gains.wait()
    for out, row in zip(gain_outs, (2, 3, 0, 1)):
        out[...] = tail[row]
    for store in stores:
        store.wait()


def unpack_all(sums, latent_init, query_gain, shapes):
    f32 = jnp.float32
    own = sums[0].shape[-1]
    latents, width = latent_init.shape
    pieces = sums[0].shape[0]
    vmem = pl.BlockSpec(memory_space=pltpu.VMEM)
    anywhere = pl.BlockSpec(memory_space=pl.ANY)
    count = sum(columns // own for _, columns in shapes)
    size = sum(rows * columns // own for rows, columns in shapes)
    return pl.pallas_call(
        unpack_kernel,
        out_shape=tuple(jax.ShapeDtypeStruct(shape, f32) for shape in shapes) + (
            jax.ShapeDtypeStruct((latents, own), f32), jax.ShapeDtypeStruct((width, own), f32))
        + (jax.ShapeDtypeStruct((own,), f32),) * 4,
        in_specs=[anywhere] * 4 + [vmem] * 2,
        out_specs=(anywhere,) * len(shapes) + (vmem,) * 6,
        scratch_shapes=[
            pltpu.VMEM((size, own), f32), pltpu.VMEM((pieces, 2 * latents // pieces, own), f32), pltpu.VMEM((8, own), f32),
            pltpu.SemaphoreType.DMA((count + 2,)), pltpu.SemaphoreType.DMA((count,)),
        ],
        compiler_params=pltpu.CompilerParams(vmem_limit_bytes=60 * 2**20),
        name="unpack_all",
    )(*sums, latent_init, query_gain)


def unpack(packed, rows, columns):
    pieces, _, width = packed.shape
    split = packed.reshape(pieces, columns // width, rows // pieces, width)
    return jnp.swapaxes(split, 1, 2).reshape(rows, columns)


def cut(packed, shapes):
    start, out = 0, []
    for rows, columns in shapes:
        count = rows * columns // packed.shape[-1] // packed.shape[0]
        out.append(unpack(packed[:, start : start + count], rows, columns))
        start += count
    return out


def shards(
    tokens,
    skip,
    latent_init,
    tok_gain,
    query_gain,
    mlp_gain,
    self_gain,
    w_query,
    w_keyval,
    w_out,
    w_up,
    w_down,
    w_self_qkv,
    w_self_out,
    grad_out,
):
    frames, pieces = lax.axis_size("frames"), lax.axis_size("items")
    latents, width = latent_init.shape
    hidden = w_up.shape[1]
    own = width // frames
    kv, log_total, query, first, out_latents, act, hidden_rows, mlp_in, cross, after, cotangent, heard, heard_f32, d_triple, _ = forward(
        frames, pieces, tokens, skip, latent_init, tok_gain, query_gain, mlp_gain, self_gain,
        w_query, w_keyval, w_out, w_up, w_down, w_self_qkv, w_self_out, grad_out,
    )
    *sums, token_grad = backward(
        frames, first.reshape((2, pieces // 2) + first.shape[1:]), tokens, kv, act, hidden_rows, mlp_in, cross, after, cotangent,
        heard, heard_f32, d_triple, skip, log_total, query, latent_init, tok_gain, query_gain, mlp_gain, self_gain,
        w_query, w_keyval, w_out, w_up, w_down, w_self_qkv,
    )[:5]
    sums = [array.reshape((pieces,) + array.shape[2:]) for array in sums]
    shapes = ((width, 3 * own), (width, own), (hidden, own), (width, hidden // frames), (width, own), (width, 2 * own))
    if own % LANES == 0:
        *grads, latent_grad, grad_query, gain_tok, gain_query, gain_mlp, gain_self = unpack_all(
            sums, latent_init, query_gain, shapes
        )
    else:
        grads = cut(sums[0], shapes[:2]) + cut(sums[1], shapes[2:3]) + cut(sums[2], shapes[3:5])
        keyval_sum, small = cut(sums[3], (shapes[5], (2 * latents, own)))
        grads.append(keyval_sum)
        latent_grad = small[latents:]
        normed, _ = norm_down(latent_init.astype(jnp.float32).T)
        query_in = (normed * query_gain[:, None]).astype(jnp.bfloat16)
        grad_query = jnp.dot(query_in.astype(jnp.float32), small[:latents], precision=lax.Precision.HIGHEST)
        gain_mlp, gain_self, gain_tok, gain_query = [sums[3][0, row - 8] for row in range(4)]
    return (
        out_latents,
        token_grad,
        latent_grad,
        gain_tok,
        gain_query,
        gain_mlp,
        gain_self,
        grad_query,
        grads[5],
        grads[4],
        grads[3],
        grads[2],
        grads[0],
        grads[1],
    )


def solution(mesh):
    in_specs = (
        P("items", "frames", None),
        P("items"),
        P(),
        P(),
        P(),
        P(),
        P(),
        P(),
        P(),
        P(),
        P(),
        P(),
        P(),
        P(),
        P("items", None, None),
    )
    out_specs = (
        P("items", "frames", None),
        P("items", "frames", None),
        P(None, "frames"),
        P("frames"),
        P("frames"),
        P("frames"),
        P("frames"),
        P(None, "frames"),
        P(None, "frames"),
        P(None, "frames"),
        P(None, "frames"),
        P(None, "frames"),
        P(None, "frames"),
        P(None, "frames"),
    )
    return jax.shard_map(shards, mesh=mesh, in_specs=in_specs, out_specs=out_specs, check_vma=False)
```
